256 devices in a mesh: gx: 4 (over x), gy: 8 (over z), gz: 8 (over y, core).
Axes of the slice: x: 4, y: 4, z: 8, core: 2. Of those that a mesh axis runs over, the one named last changes fastest.
Arguments:
- right_side: float32 [128, 256, 1024], P('gx', 'gy', 'gz'), may hold values from -8 to 8
- conductivity: float32 [128, 256, 1024], P('gx', 'gy', 'gz'), may hold values from 0.1 to 10
Outputs:
- correction: float32 [128, 256, 1024], P('gx', 'gy', 'gz')
The draws below stay inside these ranges and needn't reach their ends.
All inputs are finite; a program needn't handle non-finite values.
Results may differ from the reference program's by a relative error of at most 0.0003.
Values sent between devices are 32-bit elements; how exact they have to be, the bound alone decides.
No kernel may reach another device: no remote copies, remote signals or barrier semaphores. Data moves between devices by JAX's collectives and lax.ppermute only.
A program may use at most 128 MiB of HBM per device.

```python
import math
import jax
import jax.numpy as jnp

COARSEST = 7
NX = 128
NY = 256
NZ = 1024


def draw_right_side(key, part):
    key = jax.random.fold_in(key, 11)
    grid_shape = (NX, NY, NZ)
    return jnp.clip(jax.random.normal(key, grid_shape, jnp.float32), -6.0, 6.0)


def level_of(key, dims, split, least, top_value):
    def one(dim, parts):
        steps = jax.random.uniform(jax.random.fold_in(jax.random.fold_in(key, 6), dim), (parts,), jnp.float32, least / len(split), top_value / len(split))
        return jnp.repeat(jnp.exp(steps), dims[dim] // parts).reshape((-1,) + (1,) * (len(dims) - dim - 1))

    level = one(*split[0])
    for cut in split[1:]:
        level = level * one(*cut)
    return level


def setup_inputs(seed: int = 0) -> dict:
    streams_of = jax.random.split(jax.random.key(seed), 3)
    right_side = draw_right_side(jax.random.fold_in(streams_of[2], 71), 0)
    conductivity = jnp.clip(jnp.exp(math.log(10.0) - 4.6051702 * jax.random.uniform(streams_of[1], (NX, NY, NZ), jnp.float32) ** level_of(streams_of[1], (NX, NY, NZ), ((0, 4), (1, 8), (2, 8)), -0.2, 0.2)), 0.1, 10.0)
    return dict(right_side=right_side, conductivity=conductivity)


center_eig = 1.25
half_width = 0.75
rho_first = half_width / center_eig
rho_second = 1.0 / (2.0 * center_eig / half_width - rho_first)
keep_coef = rho_second * rho_first
push_coef = 2.0 * rho_second / half_width


def harmonic(left_side, right_hand):
    product = left_side * right_hand
    inside = product > 0
    return jnp.where(inside, 2.0 * product / jnp.where(inside, left_side + right_hand, 1.0), left_side + right_hand)


def shifted(tensor, dimension, offset):
    slicer = [slice(1, -1), slice(1, -1), slice(1, -1)]
    slicer[dimension] = slice(1 + offset, tensor.shape[dimension] - 1 + offset)
    return tensor[tuple(slicer)]


def apply_stencil(values, conduct, level_scale):
    center = shifted(values, 0, 0)
    middle = shifted(conduct, 0, 0)
    summed = jnp.zeros(center.shape, jnp.float32)
    for dimension in range(3):
        lower_face = harmonic(middle, shifted(conduct, dimension, -1))
        upper_face = harmonic(middle, shifted(conduct, dimension, 1))
        summed = summed + lower_face * (center - shifted(values, dimension, -1)) + upper_face * (center - shifted(values, dimension, 1))
    return level_scale * summed


def inverse_diag(conduct, level_scale):
    middle = shifted(conduct, 0, 0)
    weights = jnp.zeros(middle.shape, jnp.float32)
    for dimension in range(3):
        weights = weights + harmonic(middle, shifted(conduct, dimension, -1)) + harmonic(middle, shifted(conduct, dimension, 1))
    inside = middle > 0
    return jnp.where(inside, 1.0 / jnp.where(inside, level_scale * weights, 1.0), 0.0)


def restrict(values):
    reshaped = values.reshape(values.shape[0] // 2, 2, values.shape[1] // 2, 2, values.shape[2] // 2, 2)
    return reshaped.mean(axis=(1, 3, 5))


def prolong(coarse):
    grid_shape = (coarse.shape[0], 2, coarse.shape[1], 2, coarse.shape[2], 2)
    expanded = jnp.broadcast_to(coarse[:, None, :, None, :, None], grid_shape)
    return expanded.reshape(2 * coarse.shape[0], 2 * coarse.shape[1], 2 * coarse.shape[2])


def cycle(source, conduct, level_index):
    level_scale = 0.25 ** (level_index - 2)
    cond_pad = jnp.pad(conduct, 1)
    inverse = inverse_diag(cond_pad, level_scale)
    first_step = inverse * source / center_eig
    rest_one = source - apply_stencil(jnp.pad(first_step, 1), cond_pad, level_scale)
    second_step = keep_coef * first_step + push_coef * inverse * rest_one
    approx = first_step + second_step
    if level_index == COARSEST:
        return approx
    leftover = rest_one - apply_stencil(jnp.pad(second_step, 1), cond_pad, level_scale)
    coarse = cycle(restrict(leftover), restrict(conduct), level_index + 1)
    approx = approx + prolong(coarse)
    start_resid = source - apply_stencil(jnp.pad(approx, 1), cond_pad, level_scale)
    first_step = inverse * start_resid / center_eig
    rest_one = start_resid - apply_stencil(jnp.pad(first_step, 1), cond_pad, level_scale)
    second_step = keep_coef * first_step + push_coef * inverse * rest_one
    return approx + first_step + second_step


def reference(right_side, conductivity):
    return cycle(right_side, conductivity, 2)
```

```python
import functools

import jax
import jax.numpy as jnp
from jax import lax
from jax.experimental import pallas as pl
from jax.experimental.pallas import tpu as pltpu
from jax.sharding import PartitionSpec as P

F32 = jnp.float32
AXES = ("gx", "gy", "gz")
DEV = (4, 8, 8)

center_eig = 1.25
half_width = 0.75
rho_first = half_width / center_eig
rho_second = 1.0 / (2.0 * center_eig / half_width - rho_first)
keep_coef = rho_second * rho_first
push_coef = 2.0 * rho_second / half_width
inv_center = 1.0 / center_eig

N2, R2, T2 = 40, 40, 56
N3, R3, T3 = 42, 48, 64
N4, R4, T4 = 20, 24, 40


def rcp(value):
    guess = pl.reciprocal(value, approx=True)
    return guess * (2.0 - value * guess)


def lanes_of(rows):
    return lax.broadcasted_iota(jnp.int32, (rows, 128), 1)


def rows_of(rows):
    return lax.broadcasted_iota(jnp.int32, (rows, 128), 0)


def rolled(value, shift):
    shift = shift % 128
    return value if shift == 0 else pltpu.roll(value, shift, 1)


def select_dot(value, matrix):
    return jnp.dot(value, matrix, precision=lax.Precision.HIGHEST, preferred_element_type=F32)


def square(condition, value):
    source = lax.broadcasted_iota(jnp.int32, (128, 128), 0)
    target = lax.broadcasted_iota(jnp.int32, (128, 128), 1)
    return jnp.where(condition(source, target), value, 0.0).astype(F32)


def loop(low, high, body):
    @pl.loop(low, high)
    def _(index):
        body(index)


def rows_kernel(pos, b, k, xlo, xhi, low, high):
    gx = pos[0]

    def put(plane, bv, kv):
        low[plane, 0:4] = bv[0:4]
        low[plane, 4:8] = kv[0:4]
        high[plane, 0:4] = bv[28:32]
        high[plane, 4:8] = kv[28:32]

    for j in range(4):
        kl = jnp.where(gx == 0, k[0], xlo[7]) if j == 3 else xlo[4 + j]
        kh = jnp.where(gx == DEV[0] - 1, k[31], xhi[4]) if j == 0 else xhi[4 + j]
        put(j, xlo[j], kl)
        put(36 + j, xhi[j], kh)
    loop(0, 32, lambda i: put(i + 4, b[i], k[i]))


def assemble_two(pos, b, k, xlo, xhi, ylo, yhi, put_b, put_k, get_k):
    gx, gy = pos[0], pos[1]
    for j in range(4):
        kl = jnp.where(gx == 0, k[0], xlo[7]) if j == 3 else xlo[4 + j]
        kh = jnp.where(gx == DEV[0] - 1, k[31], xhi[4]) if j == 0 else xhi[4 + j]
        put_b(j, 12, 32, xlo[j])
        put_k(j, 12, 32, kl)
        put_b(36 + j, 12, 32, xhi[j])
        put_k(36 + j, 12, 32, kh)

    def inner(i):
        put_b(i + 4, 12, 32, b[i])
        put_k(i + 4, 12, 32, k[i])

    loop(0, 32, inner)
    row = rows_of(4)

    def edges(i):
        put_b(i, 8, 4, ylo[i, 0:4])
        put_b(i, 44, 4, yhi[i, 0:4])
        kl = jnp.where((row == 3) & (gy == 0), get_k(i, 12, 1), ylo[i, 4:8])
        kh = jnp.where((row == 0) & (gy == DEV[1] - 1), get_k(i, 43, 1), yhi[i, 4:8])
        put_k(i, 8, 4, kl)
        put_k(i, 44, 4, kh)

    loop(0, N2, edges)


def accessors(b_ref, k_ref):
    def put_b(i, start, count, value):
        b_ref[i, start : start + count] = value

    def put_k(i, start, count, value):
        k_ref[i, start : start + count] = value

    def get_k(i, start, count):
        return k_ref[i, start : start + count]

    return put_b, put_k, get_k


def lanes_kernel(pos, b, k, xlo, xhi, ylo, yhi, low, high, eb, ek):
    assemble_two(pos, b, k, xlo, xhi, ylo, yhi, *accessors(eb, ek))
    group = lanes_of(R2) >> 2

    def column(col, slots):
        lo = jnp.zeros((R2, 128), F32)
        hi = jnp.zeros((R2, 128), F32)
        for s in range(slots):
            bv = eb[col * 16 + s, 8:48]
            kv = ek[col * 16 + s, 8:48]
            first, second = group == 2 * s, group == 2 * s + 1
            lo = jnp.where(first, rolled(bv, 8 * s), lo)
            lo = jnp.where(second, rolled(kv, 8 * s + 4), lo)
            hi = jnp.where(first, rolled(bv, 8 * s + 4), hi)
            hi = jnp.where(second, rolled(kv, 8 * s + 8), hi)
        low[col] = lo
        high[col] = hi

    loop(0, 2, lambda col: column(col, 16))
    column(2, 8)


def up_two(pair):
    last = lanes_of(pair[0].shape[0]) == 127
    left, right = pltpu.roll(pair[0], 127, 1), pltpu.roll(pair[1], 127, 1)
    return jnp.where(last, right, left), jnp.where(last, left, right)


def down_two(pair):
    first = lanes_of(pair[0].shape[0]) == 0
    left, right = pltpu.roll(pair[0], 1, 1), pltpu.roll(pair[1], 1, 1)
    return jnp.where(first, right, left), jnp.where(first, left, right)


def flux_two(v_ref, wx, wy, wz, p, start, rows, columns):
    here = slice(start, start + rows)
    above = slice(start + 1, start + rows + 1)
    below = slice(start - 1, start + rows - 1)
    v = [v_ref[c, p, here] for c in range(2)]
    fz = [wz[c, p, here] * (v[c] - u) for c, u in enumerate(up_two(v))]
    fzm = down_two(fz)
    result = []
    for c in range(columns):
        fx = wx[c, p, here] * (v[c] - v_ref[c, p + 1, here])
        gx = wx[c, p - 1, here] * (v_ref[c, p - 1, here] - v[c])
        fy = wy[c, p, here] * (v[c] - v_ref[c, p, above])
        gy = wy[c, p, below] * (v_ref[c, p, below] - v[c])
        result.append((fx - gx) + (fy - gy) + (fz[c] - fzm[c]))
    return result


def down_kernel(
    pos, b, k, xlo, xhi, ylo, yhi, zlo, zhi,
    bk3, eb, wx, wy, wz, inv, xs,
    ek, q, f, r1, s, masks, tmp,
):
    gx, gy, gz = pos[0], pos[1], pos[2]
    assemble_two(pos, b, k, xlo, xhi, ylo, yhi, *accessors(eb.at[0], ek))
    lane = lanes_of(R2)
    row = rows_of(R2) - 4
    here = slice(8, 48)

    def unpack(plane, lo, hi, slot):
        bv = jnp.where(lane < 4, rolled(hi, -8 * slot), 0.0)
        eb[1, plane, here] = jnp.where(lane >= 124, rolled(lo, 124 - 8 * slot), bv)
        kv = jnp.where(lane < 4, rolled(hi, -8 * slot - 4), 1.0)
        kv = jnp.where(lane >= 124, rolled(lo, 120 - 8 * slot), kv)
        q[1, plane, here] = 0.5 * rcp(kv)
        q[0, plane, here] = 0.5 * rcp(ek[plane, here])

    def column(col, slots):
        lo, hi = zlo[col], zhi[col]
        for slot in range(slots):
            unpack(col * 16 + slot, lo, hi, slot)

    loop(0, 2, lambda col: column(col, 16))
    column(2, 8)

    inside_y = ((row >= 0) | (gy > 0)) & ((row < 32) | (gy < DEV[1] - 1))
    inside_z = ((lane < 64) & (gz < DEV[2] - 1)) | ((lane >= 64) & (gz > 0))
    masks[0] = jnp.where(inside_y, 1.0, 0.0)
    masks[1] = jnp.where(inside_y & inside_z, 1.0, 0.0)
    low_edge = (lane == 127) & (gz == 0)
    high_edge = (lane == 127) & (gz == DEV[2] - 1)

    for c in range(2):
        wx[c, 0, here] = rcp(q[c, 0, here] + q[c, 1, here])

    def weigh(p):
        inside_x = ((p >= 4) | (gx > 0)) & ((p < 36) | (gx < DEV[0] - 1))
        scale_x = jnp.where(inside_x, 1.0, 0.0)
        v = [q[c, p, here] for c in range(2)]
        u = up_two(v)
        faces = [
            rcp(v[0] + jnp.where(high_edge, v[0], u[0])),
            rcp(u[1] + jnp.where(low_edge, u[1], v[1])),
        ]
        lower = down_two(faces)
        for c in range(2):
            face_x = rcp(v[c] + q[c, p + 1, here])
            face_y = rcp(v[c] + q[c, p, 9:49])
            wx[c, p, here] = face_x
            wy[c, p, here] = face_y
            wz[c, p, here] = faces[c]
            total = wx[c, p - 1, here] + face_x + face_y + wy[c, p, 7:47] + faces[c] + lower[c]
            value = jnp.where(masks[c] * scale_x > 0.5, rcp(total), 0.0)
            inv[c, p, here] = value
            f[c, p, here] = value * eb[c, p, here] * inv_center

    loop(1, N2 - 1, weigh)

    def smooth(p):
        flux = flux_two(f, wx, wy, wz, p, 8, R2, 2)
        for c in range(2):
            rest = eb[c, p, here] - flux[c]
            step = keep_coef * f[c, p, here] + push_coef * inv[c, p, here] * rest
            r1[c, p, here] = rest
            s[c, p, here] = step
            xs[c, p, here] = f[c, p, here] + step

    loop(2, N2 - 2, smooth)

    to_b = square(lambda i, j: (i >> 1) == j, 0.125)
    to_k = square(lambda i, j: (i >> 1) + 64 == j, 0.125)

    def coarsen(i):
        p = 2 * i + 4
        total = r1[0, p, 12:44] + r1[0, p + 1, 12:44]
        total = total - flux_two(s, wx, wy, wz, p, 12, 32, 1)[0]
        tmp[0, 0:32] = total - flux_two(s, wx, wy, wz, p + 1, 12, 32, 1)[0]
        tmp[1, 0:32] = ek[p, 12:44] + ek[p + 1, 12:44]
        pairs = [tmp[j, pl.ds(0, 16, stride=2)] + tmp[j, pl.ds(1, 16, stride=2)] for j in range(2)]
        bk3[i] = select_dot(pairs[0], to_b) + select_dot(pairs[1], to_k)

    loop(0, 16, coarsen)


def planes_kernel(pos, bk, xlo, xhi, out):
    gx = pos[0]
    right = lanes_of(16) >= 64
    for j in range(13):
        lo, hi = xlo[3 + j], xhi[j]
        if j == 12:
            lo = jnp.where(right & (gx == 0), bk[0], lo)
        if j == 0:
            hi = jnp.where(right & (gx == DEV[0] - 1), bk[15], hi)
        out[j] = lo
        out[29 + j] = hi
    for j in range(16):
        out[13 + j] = bk[j]


def three_rows(pos, own, ylo, yhi, p):
    gy = pos[1]
    right = lanes_of(16) >= 64
    row = rows_of(16)
    middle = own[p]
    lo = jnp.where(right & (row == 15) & (gy == 0), own[p, 0:1], ylo[p])
    hi = jnp.where(right & (row == 0) & (gy == DEV[1] - 1), own[p, 15:16], yhi[p])
    return lo, middle, hi


def slots_kernel(pos, own, ylo, yhi, low, high):
    lane = lanes_of(16)

    def column(col):
        total_lo = [None] * 3
        total_hi = [None] * 3
        for slot in range(4):
            p = jnp.minimum(col * 4 + slot, N3 - 1)
            for g, e in enumerate(three_rows(pos, own, ylo, yhi, p)):
                near = pltpu.roll(e, 80, 1)
                far = pltpu.roll(e, 32, 1)
                lo = rolled(jnp.where(lane < 16, e, near), 32 * slot)
                hi = rolled(jnp.where(lane < 16, near, far), 32 * slot)
                mine = (lane >> 5) == slot
                total_lo[g] = lo if slot == 0 else jnp.where(mine, lo, total_lo[g])
                total_hi[g] = hi if slot == 0 else jnp.where(mine, hi, total_hi[g])
        for g in range(3):
            low[col, 16 * g : 16 * g + 16] = total_lo[g]
            high[col, 16 * g : 16 * g + 16] = total_hi[g]

    loop(0, 11, column)


def flux_one(v_ref, wx, wy, wz, p, rows, full=None):
    here, above, below = slice(8, 8 + rows), slice(9, 9 + rows), slice(7, 7 + rows)
    v = v_ref[p, here]
    fx = wx[p, here] * (v - v_ref[p + 1, here])
    gx = wx[p - 1, here] * (v_ref[p - 1, here] - v)
    fy = wy[p, here] * (v - v_ref[p, above])
    gy = wy[p, below] * (v_ref[p, below] - v)
    up = pltpu.roll(v, 127, 1)
    if full is not None:
        lane = lanes_of(rows)
        up = jnp.where(lane == 127, 0.0, up)
    fz = wz[p, here] * (v - up)
    fzm = pltpu.roll(fz, 1, 1)
    if full is not None:
        fzm = jnp.where(lane == 0, -full[p, here] * v, fzm)
    return (fx - gx) + (fy - gy) + (fz - fzm)


def weigh_one(q, b, wx, wy, wz, inv, f, rows, low, high, last, low_edge, high_edge, inside, full=None):
    here = slice(8, 8 + rows)
    lane = lanes_of(rows)
    wx[low - 1, here] = rcp(q[low - 1, here] + q[low, here])

    def body(p):
        v = q[p, here]
        up = pltpu.roll(v, 127, 1)
        if full is None:
            v_low = jnp.where((lane == 127) & low_edge, up, v)
        else:
            v_low = v
        up = jnp.where((lane == last) & high_edge, v, up)
        face_x = rcp(v + q[p + 1, here])
        face_y = rcp(v + q[p, 9 : 9 + rows])
        face_z = rcp(v_low + up)
        lower_z = pltpu.roll(face_z, 1, 1)
        if full is not None:
            edge = rcp(v + v)
            full[p, here] = edge
            lower_z = jnp.where(lane == 0, edge, lower_z)
        wx[p, here] = face_x
        wy[p, here] = face_y
        wz[p, here] = face_z
        total = wx[p - 1, here] + face_x + face_y + wy[p, 7 : 7 + rows] + face_z + lower_z
        value = jnp.where(inside(p), rcp(total), 0.0)
        inv[p, here] = value
        f[p, here] = value * b[p, here] * inv_center

    loop(low, high, body)


def smooth_one(b, wx, wy, wz, inv, f, r1, s, xs, rows, low, high, full=None):
    here = slice(8, 8 + rows)

    def body(p):
        rest = b[p, here] - flux_one(f, wx, wy, wz, p, rows, full)
        step = keep_coef * f[p, here] + push_coef * inv[p, here] * rest
        r1[p, here] = rest
        s[p, here] = step
        xs[p, here] = f[p, here] + step

    loop(low, high, body)


def finish_one(b, wx, wy, wz, inv, xs, f, r0, out, shift, rows, ranges, full=None):
    here = slice(8, 8 + rows)

    def start(p):
        rest = b[p, here] - flux_one(xs, wx, wy, wz, p, rows, full)
        r0[p, here] = rest
        f[p, here] = inv[p, here] * rest * inv_center

    loop(*ranges[0], start)

    def end(p):
        rest = r0[p, here] - flux_one(f, wx, wy, wz, p, rows, full)
        step = keep_coef * f[p, here] + push_coef * inv[p, here] * rest
        out[p + shift, here] = xs[p, here] + f[p, here] + step

    loop(*ranges[1], end)


def signed(lane, limit):
    return jnp.where(lane < limit, lane, lane - 128)


def middle_kernel(
    pos, own, ylo, yhi, zlo, zhi,
    payload, b3, wx3, wy3, wz3, inv3, x3, b4, wx4, wy4, wz4, inv4, x4,
    k3, q3, f3, r3, s3, k4, q4, f4, r4, s4, tmp,
):
    gx, gy, gz = pos[0], pos[1], pos[2]
    lane = lanes_of(16)

    def unpack(p, lo, hi, slot):
        for g, e in enumerate(three_rows(pos, own, ylo, yhi, p)):
            rows = slice(8 + 16 * g, 24 + 16 * g)
            part = slice(16 * g, 16 * g + 16)
            up, dn = hi[part], lo[part]
            bv = jnp.where(lane < 80, rolled(up, 64 - 32 * slot), 0.0)
            bv = jnp.where(lane >= 112, rolled(dn, 112 - 32 * slot), bv)
            b3[p, rows] = jnp.where(lane < 64, e, bv)
            kv = jnp.where(lane < 80, rolled(up, 48 - 32 * slot), 1.0)
            kv = jnp.where(lane >= 112, rolled(dn, 96 - 32 * slot), kv)
            kv = jnp.where(lane < 64, pltpu.roll(e, 64, 1), kv)
            k3[p, rows] = kv
            q3[p, rows] = 2.0 * rcp(kv)

    def column(col, slots):
        lo, hi = zlo[col], zhi[col]
        for slot in range(slots):
            unpack(col * 4 + slot, lo, hi, slot)

    loop(0, 10, lambda col: column(col, 4))
    column(10, 2)

    def region(rows, y_first, x_first, nx, ny, nz):
        y = rows_of(rows) + y_first
        z = signed(lanes_of(rows), 96)
        inside_y = ((y >= 0) | (gy > 0)) & ((y < ny) | (gy < DEV[1] - 1))
        inside_z = ((z >= 0) | (gz > 0)) & ((z < nz) | (gz < DEV[2] - 1))
        inside_yz = jnp.where(inside_y & inside_z, 1.0, 0.0)

        def inside(p):
            x = p + x_first
            inside_x = ((x >= 0) | (gx > 0)) & ((x < nx) | (gx < DEV[0] - 1))
            return inside_yz * jnp.where(inside_x, 1.0, 0.0) > 0.5

        return inside

    low_edge, high_edge = gz == 0, gz == DEV[2] - 1
    inside = region(R3, -16, -13, 16, 16, 64)
    weigh_one(q3, b3, wx3, wy3, wz3, inv3, f3, R3, 1, N3 - 1, 63, low_edge, high_edge, inside)
    smooth_one(b3, wx3, wy3, wz3, inv3, f3, r3, s3, x3, R3, 2, N3 - 2)

    def pick(i, j):
        target = signed(j, 64)
        return ((signed(i, 96) >> 1) == target) & (target >= -6) & (target < 38)

    narrow = square(pick, 0.125)
    valid = (lanes_of(R4) < 38) | (lanes_of(R4) >= 122)
    row = rows_of(R4)

    def coarse_k(i):
        p = 2 * i + 1
        tmp[1, 8:56] = k3[p, 8:56] + k3[p + 1, 8:56]
        value = tmp[1, pl.ds(12, 24, stride=2)] + tmp[1, pl.ds(13, 24, stride=2)]
        value = jnp.where(valid, select_dot(value, narrow), 1.0)
        value = jnp.where((row == 5) & (gy == 0), pltpu.roll(value, R4 - 1, 0), value)
        value = jnp.where((row == 14) & (gy == DEV[1] - 1), pltpu.roll(value, 1, 0), value)
        k4[i, 8:32] = value

    def coarse_b(i):
        p = 2 * i + 1
        total = r3[p, 8:56] + r3[p + 1, 8:56] - flux_one(s3, wx3, wy3, wz3, p, R3)
        tmp[0, 8:56] = total - flux_one(s3, wx3, wy3, wz3, p + 1, R3)
        value = tmp[0, pl.ds(12, 24, stride=2)] + tmp[0, pl.ds(13, 24, stride=2)]
        b4[i, 8:32] = select_dot(value, narrow)

    loop(0, N4, coarse_k)
    loop(1, N4 - 1, coarse_b)
    k4[5, 8:32] = jnp.where(gx == 0, k4[6, 8:32], k4[5, 8:32])
    k4[14, 8:32] = jnp.where(gx == DEV[0] - 1, k4[13, 8:32], k4[14, 8:32])

    def invert(i):
        q4[i, 8:32] = 8.0 * rcp(k4[i, 8:32])

    loop(0, N4, invert)
    inside = region(R4, -6, -6, 8, 8, 32)
    weigh_one(q4, b4, wx4, wy4, wz4, inv4, f4, R4, 1, N4 - 1, 31, low_edge, high_edge, inside)
    smooth_one(b4, wx4, wy4, wz4, inv4, f4, r4, s4, x4, R4, 2, N4 - 2)

    spread = square(lambda i, j: (i < 32) & ((i >> 1) == (j & 15)), 0.125)
    slot = lanes_of(4) >> 4
    quad = rows_of(4)
    parts = [[None, None], [None, None]]
    for i in range(4):
        p = 2 * i + 6
        total = r4[p, 8:32] + r4[p + 1, 8:32] - flux_one(s4, wx4, wy4, wz4, p, R4)
        tmp[0, 8:32] = total - flux_one(s4, wx4, wy4, wz4, p + 1, R4)
        tmp[1, 8:32] = k4[p, 8:32] + k4[p + 1, 8:32]
        mine = slot == (i % 2) * 4 + quad
        for a in range(2):
            value = tmp[a, pl.ds(14, 4, stride=2)] + tmp[a, pl.ds(15, 4, stride=2)]
            value = jnp.where(mine, select_dot(value, spread), 0.0)
            value = jnp.sum(value, axis=0, keepdims=True)
            old = parts[a][i // 2]
            parts[a][i // 2] = value if old is None else old + value
    for a in range(2):
        for g in range(2):
            payload[2 * a + g : 2 * a + g + 1] = parts[a][g]


def exchange_blocks(value):
    row = rows_of(8)
    group = lanes_of(8) >> 4
    for bit in (1, 2):
        upper = pltpu.roll(pltpu.roll(value, 8 - bit, 0), 16 * bit, 1)
        lower = pltpu.roll(pltpu.roll(value, bit, 0), 128 - 16 * bit, 1)
        moved = jnp.where((row & bit) == 0, upper, lower)
        value = jnp.where((row & bit) == (group & bit), value, moved)
    moved = pltpu.roll(pltpu.roll(value, 4, 0), 64, 1)
    return jnp.where((row & 4) == (group & 4), value, moved)


WHOLE = ((16, 32, 128), (8, 16, 64), (4, 8, 32))


def up_kernel(
    pos, recv, b3, wx3, wy3, wz3, inv3, x3, b4, wx4, wy4, wz4, inv4, x4,
    eb, wx, wy, wz, inv, xs,
    out, *scratch,
):
    gx, gy, gz = pos[0], pos[1], pos[2]
    levels = [scratch[12 * i : 12 * i + 12] for i in range(3)]
    e5, e6, full, f4, r4, e4, y4, f3, r3, e3, y3, f2, r2, y2, tmp = scratch[36:]

    for level, (nx, ny, nz) in enumerate(WHOLE):
        b, k, q, wx_, wy_, wz_, inv_, f, r, s, x, r0 = levels[level]
        for ref in (f, s, x):
            ref[0] = jnp.zeros(ref.shape[1:], F32)
            ref[nx + 1] = jnp.zeros(ref.shape[1:], F32)

            def clear(p, ref=ref, ny=ny):
                ref[p, 0:8] = jnp.zeros((8, 128), F32)
                ref[p, 8 + ny : 16 + ny] = jnp.zeros((8, 128), F32)

            loop(1, nx + 1, clear)
    for p in (0, 1, 2, 19, 20, 21):
        e5[p] = jnp.zeros(e5.shape[1:], F32)

    def clear(p):
        e5[p, 0:8] = jnp.zeros((8, 128), F32)
        e5[p, 40:48] = jnp.zeros((8, 128), F32)

    loop(3, 19, clear)

    b5, k5 = levels[0][0], levels[0][1]

    def unpack(d):
        dx, dy = d // 8, d % 8
        rows = pl.ds(8 + 4 * dy, 4)
        for kind in range(4):
            value = exchange_blocks(recv[pl.ds(d * 32 + kind, 8, stride=4)])
            target = (b5, k5)[kind // 2]
            p = 1 + 4 * dx + 2 * (kind % 2)
            target[p, rows] = value[0:4]
            target[p + 1, rows] = value[4:8]

    loop(0, 32, unpack)

    def ends(level):
        nx, ny, nz = WHOLE[level]
        k, q = levels[level][1], levels[level][2]
        factor = 0.5 * 4.0 ** (level + 3)

        def invert(p):
            value = factor * rcp(k[p, 8 : 8 + ny])
            q[p, 8 : 8 + ny] = value
            q[p, 7:8] = value[0:1]
            q[p, 8 + ny : 9 + ny] = value[ny - 1 : ny]

        loop(1, nx + 1, invert)
        q[0] = q[1]
        q[nx + 1] = q[nx]

    def down(level):
        nx, ny, nz = WHOLE[level]
        b, k, q, wx_, wy_, wz_, inv_, f, r, s, x, r0 = levels[level]
        edge = full if level == 0 else None
        ends(level)

        def below(p):
            wy_[p, 7:8] = rcp(q[p, 7:8] + q[p, 8:9])

        loop(1, nx + 1, below)
        lane = lanes_of(ny)
        weigh_one(
            q, b, wx_, wy_, wz_, inv_, f, ny, 1, nx + 1, nz - 1, True, True,
            lambda p: lane < nz, edge,
        )
        smooth_one(b, wx_, wy_, wz_, inv_, f, r, s, x, ny, 1, nx + 1, edge)
        if level == 2:
            return
        nb, nk = levels[level + 1][0], levels[level + 1][1]
        half = nz // 2
        narrow = square(lambda i, j: ((i >> 1) == j) & (j < half), 0.125)
        valid = lanes_of(ny // 2) < half

        def coarsen(i):
            p = 2 * i - 1
            here = slice(8, 8 + ny)
            total = r[p, here] + r[p + 1, here] - flux_one(s, wx_, wy_, wz_, p, ny, edge)
            tmp[0, here] = total - flux_one(s, wx_, wy_, wz_, p + 1, ny, edge)
            tmp[1, here] = k[p, here] + k[p + 1, here]
            count = ny // 2
            for a, target in enumerate((nb, nk)):
                value = tmp[a, pl.ds(8, count, stride=2)] + tmp[a, pl.ds(9, count, stride=2)]
                value = select_dot(value, narrow)
                if a == 1:
                    value = jnp.where(valid, value, 1.0)
                target[i, 8 : 8 + count] = value

        loop(1, nx // 2 + 1, coarsen)

    for level in range(3):
        down(level)

    def up(level, coarse, target, shift):
        nx, ny, nz = WHOLE[level]
        b, k, q, wx_, wy_, wz_, inv_, f, r, s, x, r0 = levels[level]
        edge = full if level == 0 else None
        widen = square(lambda i, j: (i == (j >> 1)) & (j < nz), 1.0)
        count = ny // 2

        def add(i):
            value = select_dot(coarse[i, 8 : 8 + count], widen)
            tmp[0, pl.ds(8, count, stride=2)] = value
            tmp[0, pl.ds(9, count, stride=2)] = value
            wide = tmp[0, 8 : 8 + ny]
            x[2 * i - 1, 8 : 8 + ny] += wide
            x[2 * i, 8 : 8 + ny] += wide

        loop(1, nx // 2 + 1, add)
        span = (1, nx + 1)
        finish_one(b, wx_, wy_, wz_, inv_, x, f, r0, target, shift, ny, (span, span), edge)

    up(1, levels[2][10], e6, 0)
    up(0, e6, e5, 2)

    def pick_four(i, j):
        return i == gz * 16 + (signed(j, 64) >> 1)

    widen = square(pick_four, 1.0)

    def add_four(i):
        value = select_dot(e5[gx * 4 + i, pl.ds(5 + 4 * gy, 12)], widen)
        tmp[0, pl.ds(8, 12, stride=2)] = value
        tmp[0, pl.ds(9, 12, stride=2)] = value
        wide = tmp[0, 8:32]
        y4[2 * i, 8:32] = x4[2 * i, 8:32] + wide
        y4[2 * i + 1, 8:32] = x4[2 * i + 1, 8:32] + wide

    loop(1, 9, add_four)
    finish_one(b4, wx4, wy4, wz4, inv4, y4, f4, r4, e4, 0, R4, ((3, 17), (4, 16)))

    widen3 = square(lambda i, j: signed(i, 64) == (signed(j, 96) >> 1), 1.0)

    def add_three(i):
        value = select_dot(e4[i, 8:32], widen3)
        tmp[0, pl.ds(12, 24, stride=2)] = value
        tmp[0, pl.ds(13, 24, stride=2)] = value
        wide = tmp[0, 8:56]
        y3[2 * i + 1, 8:56] = x3[2 * i + 1, 8:56] + wide
        y3[2 * i + 2, 8:56] = x3[2 * i + 2, 8:56] + wide

    tmp[0, 8:16] = jnp.zeros((8, 128), F32)
    loop(4, 16, add_three)
    finish_one(b3, wx3, wy3, wz3, inv3, y3, f3, r3, e3, 0, R3, ((11, 31), (12, 30)))

    wide0 = square(lambda i, j: i == (j >> 1), 1.0)
    wide1 = square(lambda i, j: signed(i, 96) == ((jnp.where(j < 64, j + 128, j - 128)) >> 1), 1.0)

    def add_two(i):
        e = e3[i + 11, 22:46]
        for c, matrix in enumerate((wide0, wide1)):
            value = select_dot(e, matrix)
            tmp[c, pl.ds(8, 24, stride=2)] = value
            tmp[c, pl.ds(9, 24, stride=2)] = value
            wide = tmp[c, 8:48]
            y2[c, 2 * i, 8:48] = xs[c, 2 * i, 8:48] + wide
            y2[c, 2 * i + 1, 8:48] = xs[c, 2 * i + 1, 8:48] + wide

    loop(1, 19, add_two)
    here = slice(8, 48)

    def start(p):
        flux = flux_two(y2, wx, wy, wz, p, 8, R2, 2)
        for c in range(2):
            rest = eb[c, p, here] - flux[c]
            r2[c, p, here] = rest
            f2[c, p, here] = inv[c, p, here] * rest * inv_center

    loop(3, 37, start)
    core = slice(12, 44)

    def end(i):
        p = i + 4
        rest = r2[0, p, core] - flux_two(f2, wx, wy, wz, p, 12, 32, 1)[0]
        first = f2[0, p, core]
        step = keep_coef * first + push_coef * inv[0, p, core] * rest
        out[i] = y2[0, p, core] + first + step

    loop(0, 32, end)


def call(kernel, args, outs, scratch=()):
    return pl.pallas_call(
        kernel,
        out_shape=[jax.ShapeDtypeStruct(shape, F32) for shape in outs],
        in_specs=[pl.BlockSpec(memory_space=pltpu.SMEM)]
        + [pl.BlockSpec(memory_space=pltpu.VMEM)] * (len(args) - 1),
        out_specs=[pl.BlockSpec(memory_space=pltpu.VMEM)] * len(outs),
        scratch_shapes=[pltpu.VMEM(shape, F32) for shape in scratch],
        compiler_params=pltpu.CompilerParams(vmem_limit_bytes=56 * 1024 * 1024),
    )(*args)


def swap(low, high, axis):
    count = lax.axis_size(axis)
    ring = range(count)
    before = lax.ppermute(high, axis, [(i, (i + 1) % count) for i in ring])
    after = lax.ppermute(low, axis, [(i, (i - 1) % count) for i in ring])
    return before, after


def shards(b, k):
    pos = jnp.stack([lax.axis_index(axis) for axis in AXES]).astype(jnp.int32)
    low = jnp.concatenate([b[:4], k[:4]])
    high = jnp.concatenate([b[28:], k[28:]])
    xlo, xhi = swap(low, high, "gx")
    low, high = call(rows_kernel, (pos, b, k, xlo, xhi), [(N2, 8, 128)] * 2)
    ylo, yhi = swap(low, high, "gy")
    ext2 = (N2, T2, 128)
    low, high = call(
        lanes_kernel, (pos, b, k, xlo, xhi, ylo, yhi), [(3, R2, 128)] * 2, [ext2] * 2
    )
    zlo, zhi = swap(low, high, "gz")
    two = (2,) + ext2
    bk3, *state2 = call(
        down_kernel,
        (pos, b, k, xlo, xhi, ylo, yhi, zlo, zhi),
        [(16, 16, 128)] + [two] * 6,
        [ext2] + [two] * 4 + [(2, R2, 128), (2, 32, 128)],
    )
    xlo, xhi = swap(bk3, bk3, "gx")
    (own,) = call(planes_kernel, (pos, bk3, xlo, xhi), [(N3, 16, 128)])
    ylo, yhi = swap(own, own, "gy")
    low, high = call(slots_kernel, (pos, own, ylo, yhi), [(11, 48, 128)] * 2)
    zlo, zhi = swap(low, high, "gz")
    three, four = (N3, T3, 128), (N4, T4, 128)
    payload, *state = call(
        middle_kernel,
        (pos, own, ylo, yhi, zlo, zhi),
        [(4, 128)] + [three] * 6 + [four] * 6,
        [three] * 5 + [four] * 5 + [(2, 64, 128)],
    )
    copies = jnp.broadcast_to(payload[None], (256, 4, 128))
    recv = lax.all_to_all(copies, AXES, 0, 0, tiled=True).reshape(1024, 128)
    scratch = []
    for nx, ny, _ in WHOLE:
        scratch += [(nx + 2, ny + 16, 128)] * 12
    scratch += [(22, 48, 128), (10, 32, 128), (18, 48, 128)]
    scratch += [four] * 4 + [three] * 4 + [two] * 3 + [(2, 64, 128)]
    (out,) = call(up_kernel, (pos, recv, *state, *state2), [(32, 32, 128)], scratch)
    return out


def solution(mesh):
    spec = P(*AXES)
    return jax.shard_map(shards, mesh=mesh, in_specs=(spec, spec), out_specs=spec, check_vma=False)
```

```python
import math

import jax
import jax.numpy as jnp
from jax import lax
from jax.experimental import pallas as pl
from jax.experimental.pallas import tpu as pltpu
from jax.sharding import PartitionSpec as P

F32 = jnp.float32
AXES = ("gx", "gy", "gz")
DEV = (4, 8, 8)

center_eig = 1.25
half_width = 0.75
rho_first = half_width / center_eig
rho_second = 1.0 / (2.0 * center_eig / half_width - rho_first)
keep_coef = rho_second * rho_first
push_coef = 2.0 * rho_second / half_width
inv_center = 1.0 / center_eig

N2, R2, T2 = 40, 40, 56
N3, R3, T3 = 42, 48, 64
N4, R4, T4 = 20, 24, 40


def rcp(value):
    guess = pl.reciprocal(value, approx=True)
    return guess * (2.0 - value * guess)


def row_pairs(ref, planes, start, count):
    even = [ref[i, pl.ds(start, count, stride=2)] for i in planes]
    odd = [ref[i, pl.ds(start + 1, count, stride=2)] for i in planes]
    return jnp.concatenate(even, axis=0) + jnp.concatenate(odd, axis=0)


def spread_rows(ref, planes, start, count, value):
    for n, i in enumerate(planes):
        part = value[n * count : (n + 1) * count]
        ref[i, pl.ds(start, count, stride=2)] = part
        ref[i, pl.ds(start + 1, count, stride=2)] = part


def lanes_of(rows):
    return lax.broadcasted_iota(jnp.int32, (rows, 128), 1)


def rows_of(rows):
    return lax.broadcasted_iota(jnp.int32, (rows, 128), 0)


def rolled(value, shift):
    shift = shift % 128
    return value if shift == 0 else pltpu.roll(value, shift, 1)


def select_dot(value, matrix):
    high = value.astype(jnp.bfloat16)
    rest = value - high.astype(F32)
    middle = rest.astype(jnp.bfloat16)
    low = (rest - middle.astype(F32)).astype(jnp.bfloat16)
    parts = jnp.concatenate([high, middle, low], axis=1)
    return jnp.dot(parts, jnp.concatenate([matrix] * 3, axis=0), preferred_element_type=F32)


def square(condition, value):
    source = lax.broadcasted_iota(jnp.int32, (128, 128), 0)
    target = lax.broadcasted_iota(jnp.int32, (128, 128), 1)
    return jnp.where(condition(source, target), value, 0.0).astype(jnp.bfloat16)


def loop(low, high, body, unroll=1):
    blocks = (high - low) // unroll
    if blocks > 1:

        @pl.loop(0, blocks)
        def _(block):
            for j in range(unroll):
                body(low + block * unroll + j)

        low += blocks * unroll
    for index in range(low, high):
        body(index)


def copy_all(pairs, sems):
    copies = [
        pltpu.make_async_copy(source, target, sems.at[n]) for n, (source, target) in enumerate(pairs)
    ]
    for copy in copies:
        copy.start()
    for copy in copies:
        copy.wait()


def edge_kernel(b, k, low, high, sems):
    copy_all(
        (
            (b.at[pl.ds(0, 3)], low.at[pl.ds(0, 3)]),
            (k.at[pl.ds(0, 4)], low.at[pl.ds(3, 4)]),
            (b.at[pl.ds(29, 3)], high.at[pl.ds(0, 3)]),
            (k.at[pl.ds(28, 4)], high.at[pl.ds(3, 4)]),
        ),
        sems,
    )


def load_kernel(b, k, bv, kv, sems):
    parts = [pl.ds(8 * n, 8) for n in range(4)]
    copy_all([(x.at[part], y.at[part]) for part in parts for x, y in ((b, bv), (k, kv))], sems)


def outer_planes(pos, k, xlo, xhi, put):
    gx = pos[0]
    for j in range(4):
        kl = jnp.where(gx == 0, k[0], xlo[6]) if j == 3 else xlo[3 + j]
        kh = jnp.where(gx == DEV[0] - 1, k[31], xhi[3]) if j == 0 else xhi[3 + j]
        put(j, xlo[max(j - 1, 0)], kl)
        put(36 + j, xhi[min(j, 2)], kh)


def rows_kernel(pos, b, k, xlo, xhi, low, high):
    def put(plane, bv, kv):
        low[plane, 0:4] = bv[0:4]
        low[plane, 4:8] = kv[0:4]
        high[plane, 0:4] = bv[28:32]
        high[plane, 4:8] = kv[28:32]

    outer_planes(pos, k, xlo, xhi, put)
    loop(0, 32, lambda i: put(i + 4, b[i], k[i]), 4)


def assemble_two(pos, b, k, xlo, xhi, ylo, yhi, eb, ek):
    gy = pos[1]

    def put(plane, bv, kv):
        eb[plane, 12:44] = bv
        ek[plane, 12:44] = kv

    outer_planes(pos, k, xlo, xhi, put)
    loop(0, 32, lambda i: put(i + 4, b[i], k[i]), 4)
    row = rows_of(4)

    def edges(i):
        eb[i, 8:12] = ylo[i, 0:4]
        eb[i, 44:48] = yhi[i, 0:4]
        ek[i, 8:12] = jnp.where((row == 3) & (gy == 0), ek[i, 12:13], ylo[i, 4:8])
        ek[i, 44:48] = jnp.where((row == 0) & (gy == DEV[1] - 1), ek[i, 43:44], yhi[i, 4:8])

    loop(0, N2, edges, 4)


def lanes_kernel(pos, b, k, xlo, xhi, ylo, yhi, low, high, eb, ek):
    assemble_two(pos, b, k, xlo, xhi, ylo, yhi, eb, ek)
    group = lanes_of(R2) >> 2

    def column(col, slots):
        lo = jnp.zeros((R2, 128), F32)
        hi = jnp.zeros((R2, 128), F32)
        for s in range(slots):
            bv = eb[col * 16 + s, 8:48]
            kv = ek[col * 16 + s, 8:48]
            first, second = group == 2 * s, group == 2 * s + 1
            lo = jnp.where(first, rolled(bv, 8 * s), lo)
            lo = jnp.where(second, rolled(kv, 8 * s + 4), lo)
            hi = jnp.where(first, rolled(bv, 8 * s + 4), hi)
            hi = jnp.where(second, rolled(kv, 8 * s + 8), hi)
        low[col] = lo
        high[col] = hi

    loop(0, 2, lambda col: column(col, 16))
    column(2, 8)


def next_plane(parts):
    edge = lanes_of(parts[0].shape[0]) >= 120
    moved = [pltpu.roll(part, 120, 1) for part in parts]
    return [jnp.where(edge, moved[(c + 1) % 3], moved[c]) for c in range(3)]


def last_plane(parts):
    edge = lanes_of(parts[0].shape[0]) < 8
    moved = [pltpu.roll(part, 8, 1) for part in parts]
    return [jnp.where(edge, moved[c - 1], moved[c]) for c in range(3)]


def merge_faces(low, high):
    return jnp.where((lanes_of(low.shape[0]) & 7) == 3, high, pltpu.roll(low, 1, 1))


def flux_strips(v_ref, wx, wy, wz, faces):
    here, above, below = slice(8, 48), slice(9, 49), slice(7, 47)
    result, through = [], []
    for t in range(2):
        v = [v_ref[t, c, here] for c in range(3)]
        ahead = next_plane(v)
        fx = [wx[t, c, here] * (v[c] - ahead[c]) for c in range(3)]
        gx = last_plane(fx)
        total = []
        for c in range(3):
            fy = wy[t, c, here] * (v[c] - v_ref[t, c, above])
            gy = wy[t, c, below] * (v_ref[t, c, below] - v[c])
            fz = wz[t, c, here] * (v[c] - pltpu.roll(v[c], 127, 1))
            through.append(fz)
            total.append((fx[c] - gx[c]) + (fy - gy) + (fz - pltpu.roll(fz, 1, 1)))
        result.append(total)
    for c in range(3):
        faces[c, here] = merge_faces(through[c], through[3 + c])
    return result


def face_lanes(faces, p, here):
    return pltpu.roll(faces[p // 16, here], 124 - 8 * (p % 16), 1)


def flux_two(v_ref, wx, wy, wz, faces, p, start, rows):
    here = slice(start, start + rows)
    above = slice(start + 1, start + rows + 1)
    below = slice(start - 1, start + rows - 1)
    lane = lanes_of(rows)
    v = v_ref[p, here]
    through = face_lanes(faces, p, here)
    fx = wx[p, here] * (v - v_ref[p + 1, here])
    gx = wx[p - 1, here] * (v_ref[p - 1, here] - v)
    fy = wy[p, here] * (v - v_ref[p, above])
    gy = wy[p, below] * (v_ref[p, below] - v)
    fz = jnp.where(lane == 127, through, wz[p, here] * (v - pltpu.roll(v, 127, 1)))
    gz = jnp.where(lane == 0, through, pltpu.roll(fz, 1, 1))
    return (fx - gx) + (fy - gy) + (fz - gz)


def weights_kernel(pos, ek, wx, wy, wz, sums, q):
    here = slice(8, 48)

    def invert(p):
        q[p, here] = 0.5 * rcp(ek[p, here])

    loop(0, N2, invert, 8)
    wx[0, here] = rcp(q[0, here] + q[1, here])

    def body(p):
        v = q[p, here]
        face_x = rcp(v + q[p + 1, here])
        face_y = rcp(v + q[p, 9:49])
        wx[p, here] = face_x
        wy[p, here] = face_y
        wz[p, here] = rcp(v + pltpu.roll(v, 127, 1))
        sums[p, here] = rcp(v + q[p - 1, here]) + face_x + face_y + rcp(v + q[p, 7:47])

    loop(1, N2 - 1, body, 4)


def down_kernel(
    pos, eb, ek, wx, wy, wz, sums, low, high, zlo, zhi,
    bk3, low3, high3, inv, xs, tb, twx, twy, twz, tinv, tx,
    f, r1, s, tq, tf, ts, face_w, face_f, face_s, tmp,
):
    gx, gy, gz = pos[0], pos[1], pos[2]
    lane = lanes_of(R2)
    row = rows_of(R2) - 4
    here, above, below = slice(8, 48), slice(9, 49), slice(7, 47)
    inside_y = ((row >= 0) | (gy > 0)) & ((row < 32) | (gy < DEV[1] - 1))
    cell = lane & 7

    def inside_x(p):
        return ((p >= 4) | (gx > 0)) & ((p < 36) | (gx < DEV[0] - 1))

    for t, (first, second) in enumerate(((zlo, low), (high, zhi))):
        for c in range(3):
            one, two = first[c], second[c]
            tb[t, c, here] = jnp.where(cell < 4, one, pltpu.roll(two, 4, 1))
            k = jnp.where(cell < 4, pltpu.roll(one, 124, 1), two)
            if c == 2:
                k = jnp.where(lane < 64, k, 1.0)
            tq[t, c, here] = 0.5 * rcp(k)
    through = []
    for t in range(2):
        v = [tq[t, c, here] for c in range(3)]
        face_x = [rcp(a + b) for a, b in zip(v, next_plane(v))]
        below_x = last_plane(face_x)
        inside_z = ((cell >= 4) | (gz > 0)) if t == 0 else ((cell < 4) | (gz < DEV[2] - 1))
        for c in range(3):
            face_y = rcp(v[c] + tq[t, c, above])
            below_y = rcp(v[c] + tq[t, c, below])
            ahead = pltpu.roll(v[c], 127, 1)
            if t == 0:
                face_z = rcp(jnp.where((cell == 3) & (gz == 0), ahead, v[c]) + ahead)
            else:
                face_z = rcp(v[c] + jnp.where((cell == 3) & (gz == DEV[2] - 1), v[c], ahead))
            through.append(face_z)
            twx[t, c, here] = face_x[c]
            twy[t, c, here] = face_y
            twz[t, c, here] = face_z
            total = below_x[c] + face_x[c] + face_y + below_y + face_z + pltpu.roll(face_z, 1, 1)
            inside = inside_y & inside_z & inside_x(16 * c + (lane >> 3))
            value = jnp.where(inside, rcp(total), 0.0)
            tinv[t, c, here] = value
            tf[t, c, here] = value * tb[t, c, here] * inv_center
    for c in range(3):
        face_w[c, here] = merge_faces(through[c], through[3 + c])
    flux = flux_strips(tf, twx, twy, twz, face_f)
    for t in range(2):
        for c in range(3):
            rest = tb[t, c, here] - flux[t][c]
            step = keep_coef * tf[t, c, here] + push_coef * tinv[t, c, here] * rest
            ts[t, c, here] = step
            tx[t, c, here] = tf[t, c, here] + step
    through = [
        twz[t, c, here] * (ts[t, c, here] - pltpu.roll(ts[t, c, here], 127, 1))
        for t in range(2)
        for c in range(3)
    ]
    for c in range(3):
        face_s[c, here] = merge_faces(through[c], through[3 + c])

    mask = jnp.where(inside_y, 1.0, 0.0)

    def weigh(p):
        through = face_lanes(face_w, p, here)
        face_z = jnp.where(lane == 127, through, wz[p, here])
        below_z = jnp.where(lane == 0, through, pltpu.roll(face_z, 1, 1))
        scale = jnp.where(inside_x(p), 1.0, 0.0)
        value = jnp.where(mask * scale > 0.5, rcp(sums[p, here] + face_z + below_z), 0.0)
        inv[p, here] = value
        f[p, here] = value * eb[p, here] * inv_center

    loop(1, N2 - 1, weigh, 4)

    def smooth(p):
        rest = eb[p, here] - flux_two(f, wx, wy, wz, face_f, p, 8, R2)
        step = keep_coef * f[p, here] + push_coef * inv[p, here] * rest
        r1[p, here] = rest
        s[p, here] = step
        xs[p, here] = f[p, here] + step

    loop(2, N2 - 2, smooth, 6)

    to_b = square(lambda i, j: (i >> 1) == j, 0.125)
    to_k = square(lambda i, j: (i >> 1) + 64 == j, 0.125)

    def coarsen(i):
        p = 2 * i + 4
        total = r1[p, 12:44] + r1[p + 1, 12:44]
        total = total - flux_two(s, wx, wy, wz, face_s, p, 12, 32)
        tmp[0, i, 0:32] = total - flux_two(s, wx, wy, wz, face_s, p + 1, 12, 32)
        tmp[1, i, 0:32] = ek[p, 12:44] + ek[p + 1, 12:44]

    loop(0, 16, coarsen, 4)
    pairs = [row_pairs(tmp.at[j], range(16), 0, 16) for j in range(2)]
    both = select_dot(pairs[0], to_b) + select_dot(pairs[1], to_k)
    for i in range(16):
        part = both[16 * i : 16 * i + 16]
        bk3[i] = part
        if i < 13:
            low3[i] = part
        if i >= 3:
            high3[i - 3] = part


def planes_kernel(pos, bk, xlo, xhi, out, low, high):
    gx = pos[0]
    right = lanes_of(16) >= 64

    def put(p, value):
        out[p] = value
        low[p] = value[0:8]
        high[p] = value[8:16]
        if 9 <= p < 33:
            low[p + 33] = value[8:16]
            high[p + 33] = value[0:8]

    for j in range(13):
        lo, hi = xlo[j], xhi[j]
        if j == 12:
            lo = jnp.where(right & (gx == 0), bk[0], lo)
        if j == 0:
            hi = jnp.where(right & (gx == DEV[0] - 1), bk[15], hi)
        put(j, lo)
        put(29 + j, hi)
    for j in range(16):
        put(13 + j, bk[j])


def three_rows(pos, own, ylo, yhi, p):
    gy = pos[1]
    right = lanes_of(16) >= 64
    row = rows_of(16)
    far = jnp.where((p >= 9) & (p < 33), p + 33, p)
    lo = jnp.concatenate([ylo[far], ylo[p]], axis=0)
    hi = jnp.concatenate([yhi[p], yhi[far]], axis=0)
    lo = jnp.where(right & (row == 15) & (gy == 0), own[p, 0:1], lo)
    hi = jnp.where(right & (row == 0) & (gy == DEV[1] - 1), own[p, 15:16], hi)
    return lo, own[p], hi


def slots_kernel(pos, own, ylo, yhi, low, high):
    quarter = (lanes_of(16) & 63) >> 4

    def column(col):
        total_lo = [None] * 3
        total_hi = [None] * 3
        for slot in range(4):
            p = jnp.minimum(col * 4 + slot, N3 - 1)
            mine = quarter == slot
            for g, e in enumerate(three_rows(pos, own, ylo, yhi, p)):
                lo, hi = rolled(e, 16 * slot), rolled(e, 16 * slot - 48)
                total_lo[g] = lo if slot == 0 else jnp.where(mine, lo, total_lo[g])
                total_hi[g] = hi if slot == 0 else jnp.where(mine, hi, total_hi[g])
        for g in range(3):
            low[col, 16 * g : 16 * g + 16] = total_lo[g]
            high[col, 16 * g : 16 * g + 16] = total_hi[g]

    loop(0, 11, column, 4)


def flux_one(v_ref, wx, wy, wz, p, rows):
    here, above, below = slice(8, 8 + rows), slice(9, 9 + rows), slice(7, 7 + rows)
    v = v_ref[p, here]
    fx = wx[p, here] * (v - v_ref[p + 1, here])
    gx = wx[p - 1, here] * (v_ref[p - 1, here] - v)
    fy = wy[p, here] * (v - v_ref[p, above])
    gy = wy[p, below] * (v_ref[p, below] - v)
    fz = wz[p, here] * (v - pltpu.roll(v, 127, 1))
    return (fx - gx) + (fy - gy) + (fz - pltpu.roll(fz, 1, 1))


UNROLL = {48: 4, 24: 6, 32: 8, 16: 8, 8: 4}


def weigh_one(q, b, wx, wy, wz, inv, f, rows, low, high, first, last, inside):
    here = slice(8, 8 + rows)
    wx[low - 1, here] = rcp(q[low - 1, here] + q[low, here])

    def body(p):
        v = q[p, here]
        up = pltpu.roll(v, 127, 1)
        face_x = rcp(v + q[p + 1, here])
        face_y = rcp(v + q[p, 9 : 9 + rows])
        below_x = rcp(v + q[p - 1, here])
        below_y = rcp(v + q[p, 7 : 7 + rows])
        face_z = rcp(jnp.where(first, up, v) + jnp.where(last, v, up))
        lower_z = pltpu.roll(face_z, 1, 1)
        wx[p, here] = face_x
        wy[p, here] = face_y
        wz[p, here] = face_z
        total = below_x + face_x + face_y + below_y + face_z + lower_z
        value = jnp.where(inside(p), rcp(total), 0.0)
        inv[p, here] = value
        f[p, here] = value * b[p, here] * inv_center

    loop(low, high, body, UNROLL[rows])


def smooth_one(b, wx, wy, wz, inv, f, r1, s, xs, rows, low, high):
    here = slice(8, 8 + rows)

    def body(p):
        rest = b[p, here] - flux_one(f, wx, wy, wz, p, rows)
        step = keep_coef * f[p, here] + push_coef * inv[p, here] * rest
        r1[p, here] = rest
        s[p, here] = step
        xs[p, here] = f[p, here] + step

    loop(low, high, body, UNROLL[rows])


def finish_one(b, wx, wy, wz, inv, xs, f, r0, out, shift, rows, ranges):
    here = slice(8, 8 + rows)

    def start(p):
        rest = b[p, here] - flux_one(xs, wx, wy, wz, p, rows)
        r0[p, here] = rest
        f[p, here] = inv[p, here] * rest * inv_center

    loop(*ranges[0], start, UNROLL[rows])

    def end(p):
        rest = r0[p, here] - flux_one(f, wx, wy, wz, p, rows)
        step = keep_coef * f[p, here] + push_coef * inv[p, here] * rest
        out[p + shift, here] = xs[p, here] + f[p, here] + step

    loop(*ranges[1], end, UNROLL[rows])


def signed(lane, limit):
    return jnp.where(lane < limit, lane, lane - 128)


def middle_kernel(
    pos, own, ylo, yhi, zlo, zhi,
    payload, b3, wx3, wy3, wz3, inv3, x3, b4, wx4, wy4, wz4, inv4, x4,
    k3, q3, f3, r3, s3, k4, q4, f4, r4, s4, tmp,
):
    gx, gy, gz = pos[0], pos[1], pos[2]
    lane = lanes_of(16)

    def unpack(p, lo, hi, slot):
        for g, e in enumerate(three_rows(pos, own, ylo, yhi, p)):
            rows = slice(8 + 16 * g, 24 + 16 * g)
            part = slice(16 * g, 16 * g + 16)
            up, dn = rolled(hi[part], 64 - 16 * slot), rolled(lo[part], 112 - 16 * slot)
            bv = jnp.where((lane >= 64) & (lane < 80), up, e)
            b3[p, rows] = jnp.where(lane >= 112, dn, bv)
            kv = jnp.where(lane < 16, up, jnp.where((lane >= 48) & (lane < 64), dn, e))
            kv = pltpu.roll(kv, 64, 1)
            kv = jnp.where((lane >= 80) & (lane < 112), 1.0, kv)
            k3[p, rows] = kv
            q3[p, rows] = 2.0 * rcp(kv)

    def column(col, slots):
        lo, hi = zlo[col], zhi[col]
        for slot in range(slots):
            unpack(col * 4 + slot, lo, hi, slot)

    loop(0, 10, lambda col: column(col, 4), 2)
    column(10, 2)

    def region(rows, y_first, x_first, nx, ny, nz):
        y = rows_of(rows) + y_first
        z = signed(lanes_of(rows), 96)
        inside_y = ((y >= 0) | (gy > 0)) & ((y < ny) | (gy < DEV[1] - 1))
        inside_z = ((z >= 0) | (gz > 0)) & ((z < nz) | (gz < DEV[2] - 1))
        inside_yz = jnp.where(inside_y & inside_z, 1.0, 0.0)

        def inside(p):
            x = p + x_first
            inside_x = ((x >= 0) | (gx > 0)) & ((x < nx) | (gx < DEV[0] - 1))
            return inside_yz * jnp.where(inside_x, 1.0, 0.0) > 0.5

        return inside

    def edges(rows, cells):
        lane = lanes_of(rows)
        return (lane == 127) & (gz == 0), (lane == cells - 1) & (gz == DEV[2] - 1)

    inside = region(R3, -16, -13, 16, 16, 64)
    weigh_one(q3, b3, wx3, wy3, wz3, inv3, f3, R3, 1, N3 - 1, *edges(R3, 64), inside)
    smooth_one(b3, wx3, wy3, wz3, inv3, f3, r3, s3, x3, R3, 2, N3 - 2)

    def pick(i, j):
        target = signed(j, 64)
        return ((signed(i, 96) >> 1) == target) & (target >= -6) & (target < 38)

    narrow = square(pick, 0.125)
    valid = (lanes_of(R4) < 38) | (lanes_of(R4) >= 122)
    row = rows_of(R4)

    def coarse_k(i):
        p = 2 * i + 1
        tmp[0, i, 8:56] = k3[p, 8:56] + k3[p + 1, 8:56]

    def coarse_b(i):
        p = 2 * i + 1
        total = r3[p, 8:56] + r3[p + 1, 8:56] - flux_one(s3, wx3, wy3, wz3, p, R3)
        tmp[1, i, 8:56] = total - flux_one(s3, wx3, wy3, wz3, p + 1, R3)

    loop(0, N4, coarse_k, 5)
    loop(1, N4 - 1, coarse_b, 3)
    value = select_dot(row_pairs(tmp.at[0], range(N4), 12, R4), narrow)
    for i in range(N4):
        part = jnp.where(valid, value[R4 * i : R4 * i + R4], 1.0)
        part = jnp.where((row == 5) & (gy == 0), pltpu.roll(part, R4 - 1, 0), part)
        part = jnp.where((row == 14) & (gy == DEV[1] - 1), pltpu.roll(part, 1, 0), part)
        k4[i, 8:32] = part
    value = select_dot(row_pairs(tmp.at[1], range(1, N4 - 1), 12, R4), narrow)
    for i in range(1, N4 - 1):
        b4[i, 8:32] = value[R4 * (i - 1) : R4 * i]
    k4[5, 8:32] = jnp.where(gx == 0, k4[6, 8:32], k4[5, 8:32])
    k4[14, 8:32] = jnp.where(gx == DEV[0] - 1, k4[13, 8:32], k4[14, 8:32])

    def invert(i):
        q4[i, 8:32] = 8.0 * rcp(k4[i, 8:32])

    loop(0, N4, invert, 5)
    inside = region(R4, -6, -6, 8, 8, 32)
    weigh_one(q4, b4, wx4, wy4, wz4, inv4, f4, R4, 1, N4 - 1, *edges(R4, 32), inside)
    smooth_one(b4, wx4, wy4, wz4, inv4, f4, r4, s4, x4, R4, 2, N4 - 2)

    spread = square(lambda i, j: (i < 32) & ((i >> 1) == (j & 15)), 0.125)
    slot = lanes_of(4) >> 4
    quad = rows_of(4)
    parts = [[None, None], [None, None]]
    for i in range(4):
        p = 2 * i + 6
        total = r4[p, 8:32] + r4[p + 1, 8:32] - flux_one(s4, wx4, wy4, wz4, p, R4)
        tmp[0, i, 8:32] = total - flux_one(s4, wx4, wy4, wz4, p + 1, R4)
        tmp[1, i, 8:32] = k4[p, 8:32] + k4[p + 1, 8:32]
    for i in range(4):
        mine = slot == (i % 2) * 4 + quad
        for a in range(2):
            value = row_pairs(tmp.at[a], [i], 14, 4)
            value = jnp.where(mine, select_dot(value, spread), 0.0)
            value = jnp.sum(value, axis=0, keepdims=True)
            old = parts[a][i // 2]
            parts[a][i // 2] = value if old is None else old + value
    value = jnp.concatenate(parts[0] + parts[1], axis=0)
    for d in range(32):
        payload[d] = value


def exchange_blocks(value):
    row = rows_of(8)
    group = lanes_of(8) >> 4
    for bit in (1, 2):
        upper = pltpu.roll(pltpu.roll(value, 8 - bit, 0), 16 * bit, 1)
        lower = pltpu.roll(pltpu.roll(value, bit, 0), 128 - 16 * bit, 1)
        moved = jnp.where((row & bit) == 0, upper, lower)
        value = jnp.where((row & bit) == (group & bit), value, moved)
    moved = pltpu.roll(pltpu.roll(value, 4, 0), 64, 1)
    return jnp.where((row & 4) == (group & 4), value, moved)


WHOLE = ((16, 32, 128), (8, 16, 64), (4, 8, 32))


def up_kernel(
    pos, own, up1, up2, down2, down1, b3, wx3, wy3, wz3, inv3, x3, b4, wx4, wy4, wz4, inv4, x4,
    eb, wx, wy, wz, inv, xs, tb, twx, twy, twz, tinv, tx,
    out, *scratch,
):
    gx, gy, gz = pos[0], pos[1], pos[2]
    levels = [scratch[12 * i : 12 * i + 12] for i in range(3)]
    e5, e6, raw, f4, r4, e4, y4, f3, r3, e3, y3, f2, r2, y2, tf, ty, face_x, face_f, tmp = scratch[36:]

    for level, (nx, ny, nz) in enumerate(WHOLE):
        b, k, q, wx_, wy_, wz_, inv_, f, r, s, x, r0 = levels[level]
        for ref in (f, s, x):
            ref[0] = jnp.zeros(ref.shape[1:], F32)
            ref[nx + 1] = jnp.zeros(ref.shape[1:], F32)

            def clear(p, ref=ref, ny=ny):
                ref[p, 0:8] = jnp.zeros((8, 128), F32)
                ref[p, 8 + ny : 16 + ny] = jnp.zeros((8, 128), F32)

            loop(1, nx + 1, clear)
    for p in (0, 1, 2, 19, 20, 21):
        e5[p] = jnp.zeros(e5.shape[1:], F32)

    def clear(p):
        e5[p, 0:8] = jnp.zeros((8, 128), F32)
        e5[p, 40:48] = jnp.zeros((8, 128), F32)

    loop(3, 19, clear)

    b5, k5 = levels[0][0], levels[0][1]

    unused = jnp.ones((128, 128), F32)
    parts = (own[...], up1[...], up2[...], unused, unused, unused, down2[...], down1[...])
    for n, part in enumerate(parts):
        raw[pl.ds(n, 128, stride=8)] = part

    def unpack(d):
        dx, dy = d // 8, d % 8
        rows = pl.ds(8 + 4 * dy, 4)
        for kind in range(4):
            value = exchange_blocks(raw[pl.ds(pl.multiple_of(d * 32 + kind * 8, 8), 8)])
            target = (b5, k5)[kind // 2]
            p = 1 + 4 * dx + 2 * (kind % 2)
            target[p, rows] = value[0:4]
            target[p + 1, rows] = value[4:8]

    loop(0, 32, unpack, 4)

    def ends(level):
        nx, ny, nz = WHOLE[level]
        k, q = levels[level][1], levels[level][2]
        factor = 0.5 * 4.0 ** (level + 3)

        def invert(p):
            value = factor * rcp(k[p, 8 : 8 + ny])
            q[p, 8 : 8 + ny] = value
            q[p, 7:8] = value[0:1]
            q[p, 8 + ny : 9 + ny] = value[ny - 1 : ny]

        loop(1, nx + 1, invert, 4)
        q[0] = q[1]
        q[nx + 1] = q[nx]

    def down(level):
        nx, ny, nz = WHOLE[level]
        b, k, q, wx_, wy_, wz_, inv_, f, r, s, x, r0 = levels[level]
        ends(level)

        def below(p):
            wy_[p, 7:8] = rcp(q[p, 7:8] + q[p, 8:9])

        loop(1, nx + 1, below, 4)
        z = signed(lanes_of(ny), 72) + gz * (nz // DEV[2])
        weigh_one(
            q, b, wx_, wy_, wz_, inv_, f, ny, 1, nx + 1, z == -1, z == nz - 1,
            lambda p: (z >= 0) & (z < nz),
        )
        smooth_one(b, wx_, wy_, wz_, inv_, f, r, s, x, ny, 1, nx + 1)
        if level == 2:
            return
        nb, nk = levels[level + 1][0], levels[level + 1][1]
        low, high = ((-9, 17), (-4, 8))[level]

        def kept(lane):
            return (signed(lane, 64) >= low) & (signed(lane, 64) < high)

        narrow = square(lambda i, j: ((signed(i, 72) >> 1) == signed(j, 64)) & kept(j), 0.125)
        valid = kept(lanes_of(ny // 2))

        def coarsen(i):
            p = 2 * i - 1
            here = slice(8, 8 + ny)
            total = r[p, here] + r[p + 1, here] - flux_one(s, wx_, wy_, wz_, p, ny)
            tmp[0, i, here] = total - flux_one(s, wx_, wy_, wz_, p + 1, ny)
            tmp[1, i, here] = k[p, here] + k[p + 1, here]

        count = ny // 2
        planes = range(1, nx // 2 + 1)
        loop(1, nx // 2 + 1, coarsen, 64 // ny)
        for a, target in enumerate((nb, nk)):
            value = select_dot(row_pairs(tmp.at[a], planes, 8, count), narrow)
            for n, i in enumerate(planes):
                part = value[count * n : count * n + count]
                target[i, 8 : 8 + count] = jnp.where(valid, part, 1.0) if a == 1 else part

    for level in range(3):
        down(level)

    def up(level, coarse, target, shift):
        nx, ny, nz = WHOLE[level]
        b, k, q, wx_, wy_, wz_, inv_, f, r, s, x, r0 = levels[level]
        widen = square(lambda i, j: signed(i, 64) == (signed(j, 64) >> 1), 1.0)
        count = ny // 2

        planes = range(1, nx // 2 + 1)
        value = jnp.concatenate([coarse[i, 8 : 8 + count] for i in planes], axis=0)
        spread_rows(tmp.at[0], planes, 8, count, select_dot(value, widen))

        def add(i):
            wide = tmp[0, i, 8 : 8 + ny]
            x[2 * i - 1, 8 : 8 + ny] += wide
            x[2 * i, 8 : 8 + ny] += wide

        loop(1, nx // 2 + 1, add, 64 // ny)
        span = (1, nx + 1)
        finish_one(b, wx_, wy_, wz_, inv_, x, f, r0, target, shift, ny, (span, span))

    up(1, levels[2][10], e6, 0)
    up(0, e6, e5, 2)

    widen = square(lambda i, j: signed(i, 64) == (signed(j, 64) >> 1), 1.0)

    planes = range(1, 9)
    value = [e5[gx * 4 + i, pl.ds(pl.multiple_of(4 * gy, 4), 24)] for i in planes]
    value = select_dot(jnp.concatenate(value, axis=0), widen)
    for n, i in enumerate(planes):
        spread_rows(tmp.at[0], [i], 8, 12, value[24 * n + 5 : 24 * n + 17])

    def add_four(i):
        wide = tmp[0, i, 8:32]
        y4[2 * i, 8:32] = x4[2 * i, 8:32] + wide
        y4[2 * i + 1, 8:32] = x4[2 * i + 1, 8:32] + wide

    loop(1, 9, add_four, 4)
    finish_one(b4, wx4, wy4, wz4, inv4, y4, f4, r4, e4, 0, R4, ((3, 17), (4, 16)))

    widen3 = square(lambda i, j: signed(i, 64) == (signed(j, 96) >> 1), 1.0)

    planes = range(4, 16)
    value = jnp.concatenate([e4[i, 8:32] for i in planes], axis=0)
    spread_rows(tmp.at[0], planes, 12, 24, select_dot(value, widen3))

    def add_three(i):
        wide = tmp[0, i, 8:56]
        y3[2 * i + 1, 8:56] = x3[2 * i + 1, 8:56] + wide
        y3[2 * i + 2, 8:56] = x3[2 * i + 2, 8:56] + wide

    loop(4, 16, add_three, 3)
    finish_one(b3, wx3, wy3, wz3, inv3, y3, f3, r3, e3, 0, R3, ((11, 31), (12, 30)))

    wide = square(lambda i, j: i == (j >> 1), 1.0)
    planes = range(1, 19)
    value = jnp.concatenate([e3[i + 11, 22:46] for i in planes], axis=0)
    spread_rows(tmp.at[0], planes, 8, 24, select_dot(value, wide))
    here = slice(8, 48)
    group = lanes_of(24) >> 4
    for t in range(2):
        wide = square(lambda i, j: signed(i, 96) == ((j & 7) + 128 * t - 4) >> 1, 1.0)
        parts = select_dot(value, wide)
        for c in range(3):
            total = jnp.zeros((24, 128), F32)
            for n, i in enumerate(planes):
                if i // 8 == c:
                    total = jnp.where(group == i % 8, parts[24 * n : 24 * n + 24], total)
            spread_rows(tmp.at[1], [3 * t + c], 8, 24, total)
            ty[t, c, here] = tx[t, c, here] + tmp[1, 3 * t + c, here]
    flux = flux_strips(ty, twx, twy, twz, face_x)
    for t in range(2):
        for c in range(3):
            tf[t, c, here] = tinv[t, c, here] * (tb[t, c, here] - flux[t][c]) * inv_center
    through = [
        twz[t, c, here] * (tf[t, c, here] - pltpu.roll(tf[t, c, here], 127, 1))
        for t in range(2)
        for c in range(3)
    ]
    for c in range(3):
        face_f[c, here] = merge_faces(through[c], through[3 + c])

    def add_two(i):
        part = tmp[0, i, here]
        y2[2 * i, here] = xs[2 * i, here] + part
        y2[2 * i + 1, here] = xs[2 * i + 1, here] + part

    loop(1, 19, add_two, 3)

    def start(p):
        rest = eb[p, here] - flux_two(y2, wx, wy, wz, face_x, p, 8, R2)
        r2[p, here] = rest
        f2[p, here] = inv[p, here] * rest * inv_center

    loop(3, 37, start, 5)
    core = slice(12, 44)

    def end(i):
        p = i + 4
        rest = r2[p, core] - flux_two(f2, wx, wy, wz, face_f, p, 12, 32)
        first = f2[p, core]
        step = keep_coef * first + push_coef * inv[p, core] * rest
        out[i] = y2[p, core] + first + step

    loop(0, 32, end, 8)


def vmem(array):
    return pltpu.with_memory_space_constraint(array, pltpu.VMEM)


def call(kernel, args, outs, scratch=(), final=False):
    size = sum(4 * math.prod(shape) for shape in scratch) + sum(4 * math.prod(shape) for shape in outs)
    out_type = jax.ShapeDtypeStruct if final else pltpu.VMEM
    held = args[1:]
    return pl.pallas_call(
        kernel,
        out_shape=[out_type(shape, F32) for shape in outs],
        in_specs=[pl.BlockSpec(memory_space=pltpu.SMEM)]
        + [pl.BlockSpec(memory_space=pltpu.VMEM)] * len(held),
        out_specs=[pl.BlockSpec(memory_space=pltpu.VMEM)] * len(outs),
        scratch_shapes=[pltpu.VMEM(shape, F32) for shape in scratch],
        compiler_params=pltpu.CompilerParams(vmem_limit_bytes=size + (4 << 20)),
    )(args[0], *held)


def load(kernel, b, k, shape, count):
    return pl.pallas_call(
        kernel,
        out_shape=[pltpu.VMEM(shape, F32)] * 2,
        in_specs=[pl.BlockSpec(memory_space=pl.ANY)] * 2,
        out_specs=[pl.BlockSpec(memory_space=pltpu.VMEM)] * 2,
        scratch_shapes=[pltpu.SemaphoreType.DMA((count,))],
    )(b, k)


def swap(low, high, axis):
    count = lax.axis_size(axis)
    ring = range(count)
    before = lax.ppermute(high, axis, [(i, (i + 1) % count) for i in ring])
    after = lax.ppermute(low, axis, [(i, (i - 1) % count) for i in ring])
    return vmem(before), vmem(after)


def shards(b, k):
    pos = jnp.stack([lax.axis_index(axis) for axis in AXES]).astype(jnp.int32)
    low, high = load(edge_kernel, b, k, (7, 32, 128), 4)
    xlo, xhi = swap(low, high, "gx")
    b, k = load(load_kernel, b, k, (32, 32, 128), 8)
    low, high = call(rows_kernel, (pos, b, k, xlo, xhi), [(N2, 8, 128)] * 2)
    ylo, yhi = swap(low, high, "gy")
    ext2, strip, face = (N2, T2, 128), (2, 3, T2, 128), (3, T2, 128)
    low, high, eb, ek = call(
        lanes_kernel, (pos, b, k, xlo, xhi, ylo, yhi), [(3, R2, 128)] * 2 + [ext2] * 2
    )
    zlo, zhi = swap(low, high, "gz")
    wx, wy, wz, sums = call(weights_kernel, (pos, ek), [ext2] * 4, [ext2])
    bk3, low, high, *rest = call(
        down_kernel,
        (pos, eb, ek, wx, wy, wz, sums, low, high, zlo, zhi),
        [(16, 16, 128)] + [(13, 16, 128)] * 2 + [ext2] * 2 + [strip] * 6,
        [ext2] * 3 + [strip] * 3 + [face] * 3 + [(2, 16, 32, 128)],
    )
    state2 = [eb, wx, wy, wz, *rest]
    xlo, xhi = swap(low, high, "gx")
    own, low, high = call(
        planes_kernel, (pos, bk3, xlo, xhi), [(N3, 16, 128)] + [(N3 + 24, 8, 128)] * 2
    )
    ylo, yhi = swap(low, high, "gy")
    low, high = call(slots_kernel, (pos, own, ylo, yhi), [(11, 48, 128)] * 2)
    zlo, zhi = swap(low, high, "gz")
    three, four = (N3, T3, 128), (N4, T4, 128)
    payload, *state = call(
        middle_kernel,
        (pos, own, ylo, yhi, zlo, zhi),
        [(32, 4, 128)] + [three] * 6 + [four] * 6,
        [three] * 5 + [four] * 5 + [(2, N4, T3, 128)],
    )
    recv = lax.all_to_all(payload, AXES[:2], 0, 0, tiled=True).reshape(128, 128)
    ring = range(DEV[2])
    recv = [recv] + [
        lax.ppermute(recv, "gz", [(i, (i - d) % DEV[2]) for i in ring]) for d in (1, 2, -2, -1)
    ]
    recv = [vmem(part) for part in recv]
    scratch = []
    for nx, ny, _ in WHOLE:
        scratch += [(nx + 2, ny + 16, 128)] * 12
    scratch += [(22, 56, 128), (10, 32, 128), (1024, 128)]
    scratch += [four] * 4 + [three] * 4 + [ext2] * 3 + [strip] * 2 + [face] * 2
    scratch += [(2, 20, T3, 128)]
    (out,) = call(up_kernel, (pos, *recv, *state, *state2), [(32, 32, 128)], scratch, True)
    return out


def solution(mesh):
    spec = P(*AXES)
    return jax.shard_map(shards, mesh=mesh, in_specs=(spec, spec), out_specs=spec, check_vma=False)
```

```python
import math

import jax
import jax.numpy as jnp
from jax import lax
from jax.experimental import pallas as pl
from jax.experimental.pallas import tpu as pltpu
from jax.sharding import PartitionSpec as P

F32 = jnp.float32
AXES = ("gx", "gy", "gz")
DEV = (4, 8, 8)

center_eig = 1.25
half_width = 0.75
rho_first = half_width / center_eig
rho_second = 1.0 / (2.0 * center_eig / half_width - rho_first)
keep_coef = rho_second * rho_first
push_coef = 2.0 * rho_second / half_width
inv_center = 1.0 / center_eig

N2, R2, T2 = 40, 40, 56
N3, R3, T3 = 42, 48, 64
N4, R4, T4 = 20, 24, 40


def rcp(value):
    guess = pl.reciprocal(value, approx=True)
    return guess * (2.0 - value * guess)


def row_pairs(ref, planes, start, count):
    even = [ref[i, pl.ds(start, count, stride=2)] for i in planes]
    odd = [ref[i, pl.ds(start + 1, count, stride=2)] for i in planes]
    return jnp.concatenate(even, axis=0) + jnp.concatenate(odd, axis=0)


def spread_rows(ref, planes, start, count, value):
    for n, i in enumerate(planes):
        part = value[n * count : (n + 1) * count]
        ref[i, pl.ds(start, count, stride=2)] = part
        ref[i, pl.ds(start + 1, count, stride=2)] = part


def lanes_of(rows):
    return lax.broadcasted_iota(jnp.int32, (rows, 128), 1)


def rows_of(rows):
    return lax.broadcasted_iota(jnp.int32, (rows, 128), 0)


def rolled(value, shift):
    shift = shift % 128
    return value if shift == 0 else pltpu.roll(value, shift, 1)


def select_dot(value, matrix):
    high = value.astype(jnp.bfloat16)
    rest = value - high.astype(F32)
    middle = rest.astype(jnp.bfloat16)
    low = (rest - middle.astype(F32)).astype(jnp.bfloat16)
    parts = jnp.concatenate([high, middle, low], axis=1)
    return jnp.dot(parts, jnp.concatenate([matrix] * 3, axis=0), preferred_element_type=F32)


def square(condition, value):
    source = lax.broadcasted_iota(jnp.int32, (128, 128), 0)
    target = lax.broadcasted_iota(jnp.int32, (128, 128), 1)
    return jnp.where(condition(source, target), value, 0.0).astype(jnp.bfloat16)


def loop(low, high, body, unroll=1):
    blocks = (high - low) // unroll
    if blocks > 1:

        @pl.loop(0, blocks)
        def _(block):
            for j in range(unroll):
                body(low + block * unroll + j)

        low += blocks * unroll
    for index in range(low, high):
        body(index)


def copy_all(pairs, sems):
    copies = [
        pltpu.make_async_copy(source, target, sems.at[n]) for n, (source, target) in enumerate(pairs)
    ]
    for copy in copies:
        copy.start()
    for copy in copies:
        copy.wait()


def edge_kernel(b, k, low, high, sems):
    copy_all(
        (
            (b.at[pl.ds(0, 3)], low.at[pl.ds(0, 3)]),
            (k.at[pl.ds(0, 4)], low.at[pl.ds(3, 4)]),
            (b.at[pl.ds(29, 3)], high.at[pl.ds(0, 3)]),
            (k.at[pl.ds(28, 4)], high.at[pl.ds(3, 4)]),
        ),
        sems,
    )


def load_kernel(b, k, bv, kv, sems):
    parts = [pl.ds(8 * n, 8) for n in range(4)]
    copy_all([(x.at[part], y.at[part]) for part in parts for x, y in ((b, bv), (k, kv))], sems)


def outer_planes(pos, k, xlo, xhi, put):
    gx = pos[0]
    for j in range(4):
        kl = jnp.where(gx == 0, k[0], xlo[6]) if j == 3 else xlo[3 + j]
        kh = jnp.where(gx == DEV[0] - 1, k[31], xhi[3]) if j == 0 else xhi[3 + j]
        put(j, xlo[max(j - 1, 0)], kl)
        put(36 + j, xhi[min(j, 2)], kh)


def rows_kernel(pos, b, k, xlo, xhi, low, high):
    def put(plane, bv, kv):
        low[plane, 0:4] = bv[0:4]
        low[plane, 4:8] = kv[0:4]
        high[plane, 0:4] = bv[28:32]
        high[plane, 4:8] = kv[28:32]

    outer_planes(pos, k, xlo, xhi, put)
    loop(0, 32, lambda i: put(i + 4, b[i], k[i]), 4)


def assemble_two(pos, b, k, xlo, xhi, ylo, yhi, eb, ek):
    gy = pos[1]

    def put(plane, bv, kv):
        eb[plane, 12:44] = bv
        ek[plane, 12:44] = kv

    outer_planes(pos, k, xlo, xhi, put)
    loop(0, 32, lambda i: put(i + 4, b[i], k[i]), 4)
    row = rows_of(4)

    def edges(i):
        eb[i, 8:12] = ylo[i, 0:4]
        eb[i, 44:48] = yhi[i, 0:4]
        ek[i, 8:12] = jnp.where((row == 3) & (gy == 0), ek[i, 12:13], ylo[i, 4:8])
        ek[i, 44:48] = jnp.where((row == 0) & (gy == DEV[1] - 1), ek[i, 43:44], yhi[i, 4:8])

    loop(0, N2, edges, 4)


def lanes_kernel(pos, b, k, xlo, xhi, ylo, yhi, low, high, eb, ek):
    assemble_two(pos, b, k, xlo, xhi, ylo, yhi, eb, ek)
    group = lanes_of(R2) >> 2

    def column(col, slots):
        lo = jnp.zeros((R2, 128), F32)
        hi = jnp.zeros((R2, 128), F32)
        for s in range(slots):
            bv = eb[col * 16 + s, 8:48]
            kv = ek[col * 16 + s, 8:48]
            first, second = group == 2 * s, group == 2 * s + 1
            lo = jnp.where(first, rolled(bv, 8 * s), lo)
            lo = jnp.where(second, rolled(kv, 8 * s + 4), lo)
            hi = jnp.where(first, rolled(bv, 8 * s + 4), hi)
            hi = jnp.where(second, rolled(kv, 8 * s + 8), hi)
        low[col] = lo
        high[col] = hi

    loop(0, 2, lambda col: column(col, 16))
    column(2, 8)


def next_plane(parts):
    edge = lanes_of(parts[0].shape[0]) >= 120
    moved = [pltpu.roll(part, 120, 1) for part in parts]
    return [jnp.where(edge, moved[(c + 1) % 3], moved[c]) for c in range(3)]


def last_plane(parts):
    edge = lanes_of(parts[0].shape[0]) < 8
    moved = [pltpu.roll(part, 8, 1) for part in parts]
    return [jnp.where(edge, moved[c - 1], moved[c]) for c in range(3)]


def merge_faces(low, high):
    return jnp.where((lanes_of(low.shape[0]) & 7) == 3, high, pltpu.roll(low, 1, 1))


def flux_strips(v_ref, wx, wy, wz, faces):
    here, above, below = slice(8, 48), slice(9, 49), slice(7, 47)
    result, through = [], []
    for t in range(2):
        v = [v_ref[t, c, here] for c in range(3)]
        ahead = next_plane(v)
        fx = [wx[t, c, here] * (v[c] - ahead[c]) for c in range(3)]
        gx = last_plane(fx)
        total = []
        for c in range(3):
            fy = wy[t, c, here] * (v[c] - v_ref[t, c, above])
            gy = wy[t, c, below] * (v_ref[t, c, below] - v[c])
            fz = wz[t, c, here] * (v[c] - pltpu.roll(v[c], 127, 1))
            through.append(fz)
            total.append((fx[c] - gx[c]) + (fy - gy) + (fz - pltpu.roll(fz, 1, 1)))
        result.append(total)
    for c in range(3):
        faces[c, here] = merge_faces(through[c], through[3 + c])
    return result


def face_lanes(faces, p, here):
    return pltpu.roll(faces[p // 16, here], 124 - 8 * (p % 16), 1)


def flux_two(v_ref, wx, wy, wz, faces, p, start, rows):
    here = slice(start, start + rows)
    above = slice(start + 1, start + rows + 1)
    below = slice(start - 1, start + rows - 1)
    lane = lanes_of(rows)
    v = v_ref[p, here]
    through = face_lanes(faces, p, here)
    fx = wx[p, here] * (v - v_ref[p + 1, here])
    gx = wx[p - 1, here] * (v_ref[p - 1, here] - v)
    fy = wy[p, here] * (v - v_ref[p, above])
    gy = wy[p, below] * (v_ref[p, below] - v)
    fz = jnp.where(lane == 127, through, wz[p, here] * (v - pltpu.roll(v, 127, 1)))
    gz = jnp.where(lane == 0, through, pltpu.roll(fz, 1, 1))
    return (fx - gx) + (fy - gy) + (fz - gz)


def weights_kernel(pos, ek, wx, wy, wz, sums, q):
    here = slice(8, 48)

    def invert(p):
        q[p, here] = 0.5 * rcp(ek[p, here])

    loop(0, N2, invert, 8)
    wx[0, here] = rcp(q[0, here] + q[1, here])

    def body(p):
        v = q[p, here]
        face_x = rcp(v + q[p + 1, here])
        face_y = rcp(v + q[p, 9:49])
        wx[p, here] = face_x
        wy[p, here] = face_y
        wz[p, here] = rcp(v + pltpu.roll(v, 127, 1))
        sums[p, here] = rcp(v + q[p - 1, here]) + face_x + face_y + rcp(v + q[p, 7:47])

    loop(1, N2 - 1, body, 8)


def add_kernel(pos, first, second, out):
    planes, rows = out.shape[0], out.shape[1] - 16
    here = slice(8, 8 + rows)

    def add(p):
        out[p, here] = first[p, here] + second[p, here]

    loop(0, planes, add, 8)


def down_kernel(
    pos, eb, ek, wx, wy, wz, sums, low, high, zlo, zhi,
    bk3, low3, high3, inv, f, s, tb, twx, twy, twz, tinv, tx,
    r1, tq, tf, ts, face_w, face_f, face_s, tmp,
):
    gx, gy, gz = pos[0], pos[1], pos[2]
    lane = lanes_of(R2)
    row = rows_of(R2) - 4
    here, above, below = slice(8, 48), slice(9, 49), slice(7, 47)
    inside_y = ((row >= 0) | (gy > 0)) & ((row < 32) | (gy < DEV[1] - 1))
    cell = lane & 7

    def inside_x(p):
        return ((p >= 4) | (gx > 0)) & ((p < 36) | (gx < DEV[0] - 1))

    for t, (first, second) in enumerate(((zlo, low), (high, zhi))):
        for c in range(3):
            one, two = first[c], second[c]
            tb[t, c, here] = jnp.where(cell < 4, one, pltpu.roll(two, 4, 1))
            k = jnp.where(cell < 4, pltpu.roll(one, 124, 1), two)
            if c == 2:
                k = jnp.where(lane < 64, k, 1.0)
            tq[t, c, here] = 0.5 * rcp(k)
    through = []
    for t in range(2):
        v = [tq[t, c, here] for c in range(3)]
        face_x = [rcp(a + b) for a, b in zip(v, next_plane(v))]
        below_x = last_plane(face_x)
        inside_z = ((cell >= 4) | (gz > 0)) if t == 0 else ((cell < 4) | (gz < DEV[2] - 1))
        for c in range(3):
            face_y = rcp(v[c] + tq[t, c, above])
            below_y = rcp(v[c] + tq[t, c, below])
            ahead = pltpu.roll(v[c], 127, 1)
            if t == 0:
                face_z = rcp(jnp.where((cell == 3) & (gz == 0), ahead, v[c]) + ahead)
            else:
                face_z = rcp(v[c] + jnp.where((cell == 3) & (gz == DEV[2] - 1), v[c], ahead))
            through.append(face_z)
            twx[t, c, here] = face_x[c]
            twy[t, c, here] = face_y
            twz[t, c, here] = face_z
            total = below_x[c] + face_x[c] + face_y + below_y + face_z + pltpu.roll(face_z, 1, 1)
            inside = inside_y & inside_z & inside_x(16 * c + (lane >> 3))
            value = jnp.where(inside, rcp(total), 0.0)
            tinv[t, c, here] = value
            tf[t, c, here] = value * tb[t, c, here] * inv_center
    for c in range(3):
        face_w[c, here] = merge_faces(through[c], through[3 + c])
    flux = flux_strips(tf, twx, twy, twz, face_f)
    for t in range(2):
        for c in range(3):
            rest = tb[t, c, here] - flux[t][c]
            step = keep_coef * tf[t, c, here] + push_coef * tinv[t, c, here] * rest
            ts[t, c, here] = step
            tx[t, c, here] = tf[t, c, here] + step
    through = [
        twz[t, c, here] * (ts[t, c, here] - pltpu.roll(ts[t, c, here], 127, 1))
        for t in range(2)
        for c in range(3)
    ]
    for c in range(3):
        face_s[c, here] = merge_faces(through[c], through[3 + c])

    mask = jnp.where(inside_y, 1.0, 0.0)

    def weigh(p):
        through = face_lanes(face_w, p, here)
        face_z = jnp.where(lane == 127, through, wz[p, here])
        below_z = jnp.where(lane == 0, through, pltpu.roll(face_z, 1, 1))
        scale = jnp.where(inside_x(p), 1.0, 0.0)
        value = jnp.where(mask * scale > 0.5, rcp(sums[p, here] + face_z + below_z), 0.0)
        inv[p, here] = value
        f[p, here] = value * eb[p, here] * inv_center

    loop(1, N2 - 1, weigh, 13)

    def smooth(p):
        rest = eb[p, here] - flux_two(f, wx, wy, wz, face_f, p, 8, R2)
        step = keep_coef * f[p, here] + push_coef * inv[p, here] * rest
        r1[p, here] = rest
        s[p, here] = step

    loop(2, N2 - 2, smooth, 6)

    to_b = square(lambda i, j: (i >> 1) == j, 0.125)
    to_k = square(lambda i, j: (i >> 1) + 64 == j, 0.125)

    def coarsen(i):
        p = 2 * i + 4
        total = r1[p, 12:44] + r1[p + 1, 12:44]
        total = total - flux_two(s, wx, wy, wz, face_s, p, 12, 32)
        tmp[0, i, 0:32] = total - flux_two(s, wx, wy, wz, face_s, p + 1, 12, 32)
        tmp[1, i, 0:32] = ek[p, 12:44] + ek[p + 1, 12:44]

    loop(0, 16, coarsen, 4)
    pairs = [row_pairs(tmp.at[j], range(16), 0, 16) for j in range(2)]
    both = select_dot(pairs[0], to_b) + select_dot(pairs[1], to_k)
    for i in range(16):
        part = both[16 * i : 16 * i + 16]
        bk3[i] = part
        if i < 13:
            low3[i] = part
        if i >= 3:
            high3[i - 3] = part


def planes_kernel(pos, bk, xlo, xhi, out, low, high):
    gx = pos[0]
    right = lanes_of(16) >= 64

    def put(p, value):
        out[p] = value
        low[p] = value[0:8]
        high[p] = value[8:16]
        if 9 <= p < 33:
            low[p + 33] = value[8:16]
            high[p + 33] = value[0:8]

    for j in range(13):
        lo, hi = xlo[j], xhi[j]
        if j == 12:
            lo = jnp.where(right & (gx == 0), bk[0], lo)
        if j == 0:
            hi = jnp.where(right & (gx == DEV[0] - 1), bk[15], hi)
        put(j, lo)
        put(29 + j, hi)
    for j in range(16):
        put(13 + j, bk[j])


def three_rows(pos, own, ylo, yhi, p):
    gy = pos[1]
    right = lanes_of(16) >= 64
    row = rows_of(16)
    far = jnp.where((p >= 9) & (p < 33), p + 33, p)
    lo = jnp.concatenate([ylo[far], ylo[p]], axis=0)
    hi = jnp.concatenate([yhi[p], yhi[far]], axis=0)
    lo = jnp.where(right & (row == 15) & (gy == 0), own[p, 0:1], lo)
    hi = jnp.where(right & (row == 0) & (gy == DEV[1] - 1), own[p, 15:16], hi)
    return lo, own[p], hi


def slots_kernel(pos, own, ylo, yhi, low, high):
    quarter = (lanes_of(16) & 63) >> 4

    def column(col):
        total_lo = [None] * 3
        total_hi = [None] * 3
        for slot in range(4):
            p = jnp.minimum(col * 4 + slot, N3 - 1)
            mine = quarter == slot
            for g, e in enumerate(three_rows(pos, own, ylo, yhi, p)):
                lo, hi = rolled(e, 16 * slot), rolled(e, 16 * slot - 48)
                total_lo[g] = lo if slot == 0 else jnp.where(mine, lo, total_lo[g])
                total_hi[g] = hi if slot == 0 else jnp.where(mine, hi, total_hi[g])
        for g in range(3):
            low[col, 16 * g : 16 * g + 16] = total_lo[g]
            high[col, 16 * g : 16 * g + 16] = total_hi[g]

    loop(0, 11, column, 4)


def flux_one(v_ref, wx, wy, wz, p, rows):
    here, above, below = slice(8, 8 + rows), slice(9, 9 + rows), slice(7, 7 + rows)
    v = v_ref[p, here]
    fx = wx[p, here] * (v - v_ref[p + 1, here])
    gx = wx[p - 1, here] * (v_ref[p - 1, here] - v)
    fy = wy[p, here] * (v - v_ref[p, above])
    gy = wy[p, below] * (v_ref[p, below] - v)
    fz = wz[p, here] * (v - pltpu.roll(v, 127, 1))
    return (fx - gx) + (fy - gy) + (fz - pltpu.roll(fz, 1, 1))


UNROLL = {48: 10, 24: 9, 32: 8, 16: 8, 8: 4}


def weigh_one(q, b, wx, wy, wz, inv, f, rows, low, high, first, last, inside):
    here = slice(8, 8 + rows)
    wx[low - 1, here] = rcp(q[low - 1, here] + q[low, here])

    def body(p):
        v = q[p, here]
        up = pltpu.roll(v, 127, 1)
        face_x = rcp(v + q[p + 1, here])
        face_y = rcp(v + q[p, 9 : 9 + rows])
        below_x = rcp(v + q[p - 1, here])
        below_y = rcp(v + q[p, 7 : 7 + rows])
        face_z = rcp(jnp.where(first, up, v) + jnp.where(last, v, up))
        lower_z = pltpu.roll(face_z, 1, 1)
        wx[p, here] = face_x
        wy[p, here] = face_y
        wz[p, here] = face_z
        total = below_x + face_x + face_y + below_y + face_z + lower_z
        value = jnp.where(inside(p), rcp(total), 0.0)
        inv[p, here] = value
        f[p, here] = value * b[p, here] * inv_center

    loop(low, high, body, UNROLL[rows])


def smooth_one(b, wx, wy, wz, inv, f, r1, s, xs, rows, low, high):
    here = slice(8, 8 + rows)

    def body(p):
        rest = b[p, here] - flux_one(f, wx, wy, wz, p, rows)
        step = keep_coef * f[p, here] + push_coef * inv[p, here] * rest
        r1[p, here] = rest
        s[p, here] = step
        if xs is not None:
            xs[p, here] = f[p, here] + step

    loop(low, high, body, UNROLL[rows])


def finish_one(b, wx, wy, wz, inv, xs, f, r0, out, shift, rows, ranges):
    here = slice(8, 8 + rows)

    def start(p):
        rest = b[p, here] - flux_one(xs, wx, wy, wz, p, rows)
        r0[p, here] = rest
        f[p, here] = inv[p, here] * rest * inv_center

    loop(*ranges[0], start, UNROLL[rows])

    def end(p):
        rest = r0[p, here] - flux_one(f, wx, wy, wz, p, rows)
        step = keep_coef * f[p, here] + push_coef * inv[p, here] * rest
        out[p + shift, here] = xs[p, here] + f[p, here] + step

    loop(*ranges[1], end, UNROLL[rows])


def signed(lane, limit):
    return jnp.where(lane < limit, lane, lane - 128)


def middle_kernel(
    pos, own, ylo, yhi, zlo, zhi,
    payload, b3, wx3, wy3, wz3, inv3, f3, s3, b4, wx4, wy4, wz4, inv4, f4, s4,
    k3, q3, r3, k4, q4, r4, tmp,
):
    gx, gy, gz = pos[0], pos[1], pos[2]
    lane = lanes_of(16)

    def unpack(p, lo, hi, slot):
        for g, e in enumerate(three_rows(pos, own, ylo, yhi, p)):
            rows = slice(8 + 16 * g, 24 + 16 * g)
            part = slice(16 * g, 16 * g + 16)
            up, dn = rolled(hi[part], 64 - 16 * slot), rolled(lo[part], 112 - 16 * slot)
            bv = jnp.where((lane >= 64) & (lane < 80), up, e)
            b3[p, rows] = jnp.where(lane >= 112, dn, bv)
            kv = jnp.where(lane < 16, up, jnp.where((lane >= 48) & (lane < 64), dn, e))
            kv = pltpu.roll(kv, 64, 1)
            kv = jnp.where((lane >= 80) & (lane < 112), 1.0, kv)
            k3[p, rows] = kv
            q3[p, rows] = 2.0 * rcp(kv)

    def column(col, slots):
        lo, hi = zlo[col], zhi[col]
        for slot in range(slots):
            unpack(col * 4 + slot, lo, hi, slot)

    loop(0, 10, lambda col: column(col, 4), 2)
    column(10, 2)

    def region(rows, y_first, x_first, nx, ny, nz):
        y = rows_of(rows) + y_first
        z = signed(lanes_of(rows), 96)
        inside_y = ((y >= 0) | (gy > 0)) & ((y < ny) | (gy < DEV[1] - 1))
        inside_z = ((z >= 0) | (gz > 0)) & ((z < nz) | (gz < DEV[2] - 1))
        inside_yz = jnp.where(inside_y & inside_z, 1.0, 0.0)

        def inside(p):
            x = p + x_first
            inside_x = ((x >= 0) | (gx > 0)) & ((x < nx) | (gx < DEV[0] - 1))
            return inside_yz * jnp.where(inside_x, 1.0, 0.0) > 0.5

        return inside

    def edges(rows, cells):
        lane = lanes_of(rows)
        return (lane == 127) & (gz == 0), (lane == cells - 1) & (gz == DEV[2] - 1)

    inside = region(R3, -16, -13, 16, 16, 64)
    weigh_one(q3, b3, wx3, wy3, wz3, inv3, f3, R3, 1, N3 - 1, *edges(R3, 64), inside)
    smooth_one(b3, wx3, wy3, wz3, inv3, f3, r3, s3, None, R3, 2, N3 - 2)

    def pick(i, j):
        target = signed(j, 64)
        return ((signed(i, 96) >> 1) == target) & (target >= -7) & (target < 39)

    narrow = square(pick, 0.125)
    valid = (lanes_of(R4) < 39) | (lanes_of(R4) >= 121)
    row = rows_of(R4)

    def coarse_k(i):
        p = 2 * i + 1
        tmp[0, i, 8:56] = k3[p, 8:56] + k3[p + 1, 8:56]

    def coarse_b(i):
        p = 2 * i + 1
        total = r3[p, 8:56] + r3[p + 1, 8:56] - flux_one(s3, wx3, wy3, wz3, p, R3)
        tmp[1, i, 8:56] = total - flux_one(s3, wx3, wy3, wz3, p + 1, R3)

    loop(0, N4, coarse_k, 5)
    loop(1, N4 - 1, coarse_b, 3)
    value = select_dot(row_pairs(tmp.at[0], range(N4), 12, R4), narrow)
    for i in range(N4):
        part = jnp.where(valid, value[R4 * i : R4 * i + R4], 1.0)
        part = jnp.where((row == 5) & (gy == 0), pltpu.roll(part, R4 - 1, 0), part)
        part = jnp.where((row == 14) & (gy == DEV[1] - 1), pltpu.roll(part, 1, 0), part)
        k4[i, 8:32] = part
    value = select_dot(row_pairs(tmp.at[1], range(1, N4 - 1), 12, R4), narrow)
    for i in range(1, N4 - 1):
        b4[i, 8:32] = value[R4 * (i - 1) : R4 * i]
    k4[5, 8:32] = jnp.where(gx == 0, k4[6, 8:32], k4[5, 8:32])
    k4[14, 8:32] = jnp.where(gx == DEV[0] - 1, k4[13, 8:32], k4[14, 8:32])

    def invert(i):
        q4[i, 8:32] = 8.0 * rcp(k4[i, 8:32])

    loop(0, N4, invert, 5)
    inside = region(R4, -6, -6, 8, 8, 32)
    weigh_one(q4, b4, wx4, wy4, wz4, inv4, f4, R4, 1, N4 - 1, *edges(R4, 32), inside)
    smooth_one(b4, wx4, wy4, wz4, inv4, f4, r4, s4, None, R4, 2, N4 - 2)

    cell = lanes_of(4) & 15
    spread = square(lambda i, j: (signed(i, 64) >> 1) == (j & 15), 0.125)
    spread_halo = square(
        lambda i, j: ((signed(i, 64) >> 1) == ((j & 15) ^ 16) - ((j & 8) << 2))
        & (((j & 15) < 4) | ((j & 15) >= 12)),
        0.125,
    )
    between = (cell >= 4) & (cell < 12)
    slot = lanes_of(4) >> 4
    quad = rows_of(4)
    parts = [[[None, None], [None, None]] for _ in range(2)]
    for i in range(4):
        p = 2 * i + 6
        total = r4[p, 8:32] + r4[p + 1, 8:32] - flux_one(s4, wx4, wy4, wz4, p, R4)
        tmp[0, i, 8:32] = total - flux_one(s4, wx4, wy4, wz4, p + 1, R4)
        tmp[1, i, 8:32] = k4[p, 8:32] + k4[p + 1, 8:32]
    for i in range(4):
        mine = slot == (i % 2) * 4 + quad
        for a in range(2):
            pair = row_pairs(tmp.at[a], [i], 14, 4)
            for h, matrix in enumerate((spread, spread_halo)):
                value = select_dot(pair, matrix)
                if h == 1:
                    value = jnp.where(between, 1.0, value)
                value = jnp.sum(jnp.where(mine, value, 0.0), axis=0, keepdims=True)
                old = parts[h][a][i // 2]
                parts[h][a][i // 2] = value if old is None else old + value
    value = jnp.concatenate([row for h in parts for a in h for row in a], axis=0)
    for d in range(32):
        payload[d] = value


def exchange_blocks(value):
    row = rows_of(8)
    group = lanes_of(8) >> 4
    for bit in (1, 2):
        upper = pltpu.roll(pltpu.roll(value, 8 - bit, 0), 16 * bit, 1)
        lower = pltpu.roll(pltpu.roll(value, bit, 0), 128 - 16 * bit, 1)
        moved = jnp.where((row & bit) == 0, upper, lower)
        value = jnp.where((row & bit) == (group & bit), value, moved)
    moved = pltpu.roll(pltpu.roll(value, 4, 0), 64, 1)
    return jnp.where((row & 4) == (group & 4), value, moved)


WHOLE = ((16, 32, 128), (8, 16, 64), (4, 8, 32))


def up_kernel(
    pos, own, up, down, b3, wx3, wy3, wz3, inv3, x3, b4, wx4, wy4, wz4, inv4, x4,
    eb, wx, wy, wz, inv, xs, tb, twx, twy, twz, tinv, tx,
    out, *scratch,
):
    gx, gy, gz = pos[0], pos[1], pos[2]
    levels = [scratch[12 * i : 12 * i + 12] for i in range(3)]
    e5, e6, raw, f4, r4, e4, y4, f3, r3, e3, y3, f2, r2, y2, tf, ty, face_x, face_f, ob, tmp, sems = scratch[36:]

    for level, (nx, ny, nz) in enumerate(WHOLE):
        b, k, q, wx_, wy_, wz_, inv_, f, r, s, x, r0 = levels[level]
        for ref in (f, s, x):
            ref[0] = jnp.zeros(ref.shape[1:], F32)
            ref[nx + 1] = jnp.zeros(ref.shape[1:], F32)

            def clear(p, ref=ref, ny=ny):
                ref[p, 0:8] = jnp.zeros((8, 128), F32)
                ref[p, 8 + ny : 16 + ny] = jnp.zeros((8, 128), F32)

            loop(1, nx + 1, clear)
    for p in (0, 1, 2, 19, 20, 21):
        e5[p] = jnp.zeros(e5.shape[1:], F32)

    def clear(p):
        e5[p, 0:8] = jnp.zeros((8, 128), F32)
        e5[p, 40:48] = jnp.zeros((8, 128), F32)

    loop(3, 19, clear)

    b5, k5 = levels[0][0], levels[0][1]

    for n in (3, 4, 5):
        raw[pl.ds(n, 128, stride=8)] = jnp.ones((128, 128), F32)
    for n, part, first in ((0, own, 0), (1, up, 0), (2, up, 4), (6, down, 4), (7, down, 0)):
        for kind in range(4):
            raw[pl.ds(8 * kind + n, 32, stride=32)] = part[pl.ds(first + kind, 32, stride=8)]

    def unpack(d):
        dx, dy = d // 8, d % 8
        rows = pl.ds(8 + 4 * dy, 4)
        for kind in range(4):
            value = exchange_blocks(raw[pl.ds(pl.multiple_of(d * 32 + kind * 8, 8), 8)])
            target = (b5, k5)[kind // 2]
            p = 1 + 4 * dx + 2 * (kind % 2)
            target[p, rows] = value[0:4]
            target[p + 1, rows] = value[4:8]

    loop(0, 32, unpack, 8)

    def ends(level):
        nx, ny, nz = WHOLE[level]
        k, q = levels[level][1], levels[level][2]
        factor = 0.5 * 4.0 ** (level + 3)

        def invert(p):
            value = factor * rcp(k[p, 8 : 8 + ny])
            q[p, 8 : 8 + ny] = value
            q[p, 7:8] = value[0:1]
            q[p, 8 + ny : 9 + ny] = value[ny - 1 : ny]

        loop(1, nx + 1, invert, 4)
        q[0] = q[1]
        q[nx + 1] = q[nx]

    def down(level):
        nx, ny, nz = WHOLE[level]
        b, k, q, wx_, wy_, wz_, inv_, f, r, s, x, r0 = levels[level]
        ends(level)

        def below(p):
            wy_[p, 7:8] = rcp(q[p, 7:8] + q[p, 8:9])

        loop(1, nx + 1, below, 4)
        z = signed(lanes_of(ny), 72) + gz * (nz // DEV[2])
        weigh_one(
            q, b, wx_, wy_, wz_, inv_, f, ny, 1, nx + 1, z == -1, z == nz - 1,
            lambda p: (z >= 0) & (z < nz),
        )
        smooth_one(b, wx_, wy_, wz_, inv_, f, r, s, x, ny, 1, nx + 1)
        if level == 2:
            return
        nb, nk = levels[level + 1][0], levels[level + 1][1]
        low, high = ((-9, 17), (-4, 8))[level]

        def kept(lane):
            return (signed(lane, 64) >= low) & (signed(lane, 64) < high)

        narrow = square(lambda i, j: ((signed(i, 72) >> 1) == signed(j, 64)) & kept(j), 0.125)
        valid = kept(lanes_of(ny // 2))

        def coarsen(i):
            p = 2 * i - 1
            here = slice(8, 8 + ny)
            total = r[p, here] + r[p + 1, here] - flux_one(s, wx_, wy_, wz_, p, ny)
            tmp[0, i, here] = total - flux_one(s, wx_, wy_, wz_, p + 1, ny)
            tmp[1, i, here] = k[p, here] + k[p + 1, here]

        count = ny // 2
        planes = range(1, nx // 2 + 1)
        loop(1, nx // 2 + 1, coarsen, 64 // ny)
        for a, target in enumerate((nb, nk)):
            value = select_dot(row_pairs(tmp.at[a], planes, 8, count), narrow)
            for n, i in enumerate(planes):
                part = value[count * n : count * n + count]
                target[i, 8 : 8 + count] = jnp.where(valid, part, 1.0) if a == 1 else part

    for level in range(3):
        down(level)

    def rise(level, coarse, target, shift):
        nx, ny, nz = WHOLE[level]
        b, k, q, wx_, wy_, wz_, inv_, f, r, s, x, r0 = levels[level]
        widen = square(lambda i, j: signed(i, 64) == (signed(j, 64) >> 1), 1.0)
        count = ny // 2

        planes = range(1, nx // 2 + 1)
        value = jnp.concatenate([coarse[i, 8 : 8 + count] for i in planes], axis=0)
        spread_rows(tmp.at[0], planes, 8, count, select_dot(value, widen))

        def add(i):
            wide = tmp[0, i, 8 : 8 + ny]
            x[2 * i - 1, 8 : 8 + ny] += wide
            x[2 * i, 8 : 8 + ny] += wide

        loop(1, nx // 2 + 1, add, 64 // ny)
        span = (1, nx + 1)
        finish_one(b, wx_, wy_, wz_, inv_, x, f, r0, target, shift, ny, (span, span))

    rise(1, levels[2][10], e6, 0)
    rise(0, e6, e5, 2)

    widen = square(lambda i, j: signed(i, 64) == (signed(j, 64) >> 1), 1.0)

    planes = range(1, 9)
    value = [e5[gx * 4 + i, pl.ds(pl.multiple_of(4 * gy, 4), 24)] for i in planes]
    value = select_dot(jnp.concatenate(value, axis=0), widen)
    for n, i in enumerate(planes):
        spread_rows(tmp.at[0], [i], 8, 12, value[24 * n + 5 : 24 * n + 17])

    def add_four(i):
        wide = tmp[0, i, 8:32]
        y4[2 * i, 8:32] = x4[2 * i, 8:32] + wide
        y4[2 * i + 1, 8:32] = x4[2 * i + 1, 8:32] + wide

    loop(1, 9, add_four, 4)
    finish_one(b4, wx4, wy4, wz4, inv4, y4, f4, r4, e4, 0, R4, ((3, 17), (4, 16)))

    widen3 = square(lambda i, j: signed(i, 64) == (signed(j, 96) >> 1), 1.0)

    planes = range(4, 16)
    value = jnp.concatenate([e4[i, 8:32] for i in planes], axis=0)
    spread_rows(tmp.at[0], planes, 12, 24, select_dot(value, widen3))

    def add_three(i):
        wide = tmp[0, i, 8:56]
        y3[2 * i + 1, 8:56] = x3[2 * i + 1, 8:56] + wide
        y3[2 * i + 2, 8:56] = x3[2 * i + 2, 8:56] + wide

    loop(4, 16, add_three, 3)
    finish_one(b3, wx3, wy3, wz3, inv3, y3, f3, r3, e3, 0, R3, ((11, 31), (12, 30)))

    wide = square(lambda i, j: i == (j >> 1), 1.0)
    planes = range(1, 19)
    value = jnp.concatenate([e3[i + 11, 22:46] for i in planes], axis=0)
    spread_rows(tmp.at[0], planes, 8, 24, select_dot(value, wide))
    here = slice(8, 48)
    group = lanes_of(24) >> 4
    for t in range(2):
        wide = square(lambda i, j: signed(i, 96) == ((j & 7) + 128 * t - 4) >> 1, 1.0)
        parts = select_dot(value, wide)
        for c in range(3):
            total = jnp.zeros((24, 128), F32)
            for n, i in enumerate(planes):
                if i // 8 == c:
                    total = jnp.where(group == i % 8, parts[24 * n : 24 * n + 24], total)
            spread_rows(tmp.at[1], [3 * t + c], 8, 24, total)
            ty[t, c, here] = tx[t, c, here] + tmp[1, 3 * t + c, here]
    flux = flux_strips(ty, twx, twy, twz, face_x)
    for t in range(2):
        for c in range(3):
            tf[t, c, here] = tinv[t, c, here] * (tb[t, c, here] - flux[t][c]) * inv_center
    through = [
        twz[t, c, here] * (tf[t, c, here] - pltpu.roll(tf[t, c, here], 127, 1))
        for t in range(2)
        for c in range(3)
    ]
    for c in range(3):
        face_f[c, here] = merge_faces(through[c], through[3 + c])

    def add_two(i):
        part = tmp[0, i, here]
        y2[2 * i, here] = xs[2 * i, here] + part
        y2[2 * i + 1, here] = xs[2 * i + 1, here] + part

    loop(1, 19, add_two, 3)

    def start(p):
        rest = eb[p, here] - flux_two(y2, wx, wy, wz, face_x, p, 8, R2)
        r2[p, here] = rest
        f2[p, here] = inv[p, here] * rest * inv_center

    loop(3, 37, start, 7)
    core = slice(12, 44)

    def end(i):
        p = i + 4
        rest = r2[p, core] - flux_two(f2, wx, wy, wz, face_f, p, 12, 32)
        first = f2[p, core]
        step = keep_coef * first + push_coef * inv[p, core] * rest
        ob[i] = y2[p, core] + first + step

    def leave(n):
        part = pl.ds(pl.multiple_of(8 * n, 8), 8)
        return pltpu.make_async_copy(ob.at[part], out.at[part], sems.at[n])

    @pl.loop(0, 4)
    def _(n):
        for j in range(8):
            end(8 * n + j)
        leave(n).start()

    for n in range(4):
        leave(n).wait()


def vmem(array):
    return pltpu.with_memory_space_constraint(array, pltpu.VMEM)


def call(kernel, args, outs, scratch=(), final=False):
    size = sum(4 * math.prod(shape) for shape in scratch) + sum(4 * math.prod(shape) for shape in outs)
    out_type = jax.ShapeDtypeStruct if final else pltpu.VMEM
    held = args[1:]
    return pl.pallas_call(
        kernel,
        out_shape=[out_type(shape, F32) for shape in outs],
        in_specs=[pl.BlockSpec(memory_space=pltpu.SMEM)]
        + [pl.BlockSpec(memory_space=pltpu.VMEM)] * len(held),
        out_specs=[pl.BlockSpec(memory_space=pl.ANY if final else pltpu.VMEM)] * len(outs),
        scratch_shapes=[pltpu.VMEM(shape, F32) for shape in scratch]
        + [pltpu.SemaphoreType.DMA((4,))] * final,
        compiler_params=pltpu.CompilerParams(vmem_limit_bytes=size + (4 << 20)),
    )(args[0], *held)


def load(kernel, b, k, shape, count):
    return pl.pallas_call(
        kernel,
        out_shape=[pltpu.VMEM(shape, F32)] * 2,
        in_specs=[pl.BlockSpec(memory_space=pl.ANY)] * 2,
        out_specs=[pl.BlockSpec(memory_space=pltpu.VMEM)] * 2,
        scratch_shapes=[pltpu.SemaphoreType.DMA((count,))],
    )(b, k)


def swap(low, high, axis):
    count = lax.axis_size(axis)
    ring = range(count)
    before = lax.ppermute(high, axis, [(i, (i + 1) % count) for i in ring])
    after = lax.ppermute(low, axis, [(i, (i - 1) % count) for i in ring])
    return vmem(before), vmem(after)


def shards(b, k):
    pos = jnp.stack([lax.axis_index(axis) for axis in AXES]).astype(jnp.int32)
    low, high = load(edge_kernel, b, k, (7, 32, 128), 4)
    xlo, xhi = swap(low, high, "gx")
    b, k = load(load_kernel, b, k, (32, 32, 128), 8)
    low, high = call(rows_kernel, (pos, b, k, xlo, xhi), [(N2, 8, 128)] * 2)
    ylo, yhi = swap(low, high, "gy")
    ext2, strip, face = (N2, T2, 128), (2, 3, T2, 128), (3, T2, 128)
    low, high, eb, ek = call(
        lanes_kernel, (pos, b, k, xlo, xhi, ylo, yhi), [(3, R2, 128)] * 2 + [ext2] * 2
    )
    zlo, zhi = swap(low, high, "gz")
    wx, wy, wz, sums = call(weights_kernel, (pos, ek), [ext2] * 4, [ext2])
    bk3, low, high, inv, first, second, *rest = call(
        down_kernel,
        (pos, eb, ek, wx, wy, wz, sums, low, high, zlo, zhi),
        [(16, 16, 128)] + [(13, 16, 128)] * 2 + [ext2] * 3 + [strip] * 6,
        [ext2] + [strip] * 3 + [face] * 3 + [(2, 16, 32, 128)],
    )
    (xs,) = call(add_kernel, (pos, first, second), [ext2])
    state2 = [eb, wx, wy, wz, inv, xs, *rest]
    xlo, xhi = swap(low, high, "gx")
    own, low, high = call(
        planes_kernel, (pos, bk3, xlo, xhi), [(N3, 16, 128)] + [(N3 + 24, 8, 128)] * 2
    )
    ylo, yhi = swap(low, high, "gy")
    low, high = call(slots_kernel, (pos, own, ylo, yhi), [(11, 48, 128)] * 2)
    zlo, zhi = swap(low, high, "gz")
    three, four = (N3, T3, 128), (N4, T4, 128)
    payload, *state = call(
        middle_kernel,
        (pos, own, ylo, yhi, zlo, zhi),
        [(32, 8, 128)] + [three] * 7 + [four] * 7,
        [three] * 3 + [four] * 3 + [(2, N4, T3, 128)],
    )
    (x3,) = call(add_kernel, (pos, *state[5:7]), [three])
    (x4,) = call(add_kernel, (pos, *state[12:14]), [four])
    state = [*state[:5], x3, *state[7:12], x4]
    recv = lax.all_to_all(payload, AXES[:2], 0, 0, tiled=True).reshape(256, 128)
    ring = range(DEV[2])
    recv = [recv] + [
        lax.ppermute(recv, "gz", [(i, (i - d) % DEV[2]) for i in ring]) for d in (1, -1)
    ]
    recv = [vmem(part) for part in recv]
    scratch = []
    for nx, ny, _ in WHOLE:
        scratch += [(nx + 2, ny + 16, 128)] * 12
    scratch += [(22, 56, 128), (10, 32, 128), (1024, 128)]
    scratch += [four] * 4 + [three] * 4 + [ext2] * 3 + [strip] * 2 + [face] * 2 + [(32, 32, 128)]
    scratch += [(2, 20, T3, 128)]
    (out,) = call(up_kernel, (pos, *recv, *state, *state2), [(32, 32, 128)], scratch, True)
    return out


def solution(mesh):
    spec = P(*AXES)
    return jax.shard_map(shards, mesh=mesh, in_specs=(spec, spec), out_specs=spec, check_vma=False)
```

```python
import math

import jax
import jax.numpy as jnp
from jax import lax
from jax.experimental import pallas as pl
from jax.experimental.pallas import tpu as pltpu
from jax.sharding import PartitionSpec as P

F32 = jnp.float32
AXES = ("gx", "gy", "gz")
DEV = (4, 8, 8)

center_eig = 1.25
half_width = 0.75
rho_first = half_width / center_eig
rho_second = 1.0 / (2.0 * center_eig / half_width - rho_first)
keep_coef = rho_second * rho_first
push_coef = 2.0 * rho_second / half_width
inv_center = 1.0 / center_eig

N2, R2, T2 = 40, 40, 56
N3, R3, T3 = 42, 48, 64
N4, R4, T4 = 20, 24, 40


def rcp(value):
    guess = pl.reciprocal(value, approx=True)
    return guess * (2.0 - value * guess)


def row_pairs(ref, planes, start, count):
    even = [ref[i, pl.ds(start, count, stride=2)] for i in planes]
    odd = [ref[i, pl.ds(start + 1, count, stride=2)] for i in planes]
    return jnp.concatenate(even, axis=0) + jnp.concatenate(odd, axis=0)


def spread_rows(ref, planes, start, count, value):
    for n, i in enumerate(planes):
        part = value[n * count : (n + 1) * count]
        ref[i, pl.ds(start, count, stride=2)] = part
        ref[i, pl.ds(start + 1, count, stride=2)] = part


def lanes_of(rows):
    return lax.broadcasted_iota(jnp.int32, (rows, 128), 1)


def rows_of(rows):
    return lax.broadcasted_iota(jnp.int32, (rows, 128), 0)


def rolled(value, shift):
    shift = shift % 128
    return value if shift == 0 else pltpu.roll(value, shift, 1)


def select_dot(value, matrix):
    high = value.astype(jnp.bfloat16)
    rest = value - high.astype(F32)
    middle = rest.astype(jnp.bfloat16)
    low = (rest - middle.astype(F32)).astype(jnp.bfloat16)
    parts = jnp.concatenate([high, middle, low], axis=1)
    return jnp.dot(parts, jnp.concatenate([matrix] * 3, axis=0), preferred_element_type=F32)


def square(condition, value):
    source = lax.broadcasted_iota(jnp.int32, (128, 128), 0)
    target = lax.broadcasted_iota(jnp.int32, (128, 128), 1)
    return jnp.where(condition(source, target), value, 0.0).astype(jnp.bfloat16)


def loop(low, high, body, unroll=1):
    blocks = (high - low) // unroll
    if blocks > 1:

        @pl.loop(0, blocks)
        def _(block):
            for j in range(unroll):
                body(low + block * unroll + j)

        low += blocks * unroll
    for index in range(low, high):
        body(index)


def copy_all(pairs, sems):
    copies = [
        pltpu.make_async_copy(source, target, sems.at[n]) for n, (source, target) in enumerate(pairs)
    ]
    for copy in copies:
        copy.start()
    for copy in copies:
        copy.wait()


def edge_kernel(b, k, low, high, sems):
    copy_all(
        (
            (b.at[pl.ds(0, 3)], low.at[pl.ds(0, 3)]),
            (k.at[pl.ds(0, 4)], low.at[pl.ds(3, 4)]),
            (b.at[pl.ds(29, 3)], high.at[pl.ds(0, 3)]),
            (k.at[pl.ds(28, 4)], high.at[pl.ds(3, 4)]),
        ),
        sems,
    )


def load_kernel(b, k, bv, kv, sems):
    parts = [pl.ds(8 * n, 8) for n in range(4)]
    copy_all([(x.at[part], y.at[part]) for part in parts for x, y in ((b, bv), (k, kv))], sems)


def outer_planes(pos, k, xlo, xhi, put):
    gx = pos[0]
    for j in range(4):
        kl = jnp.where(gx == 0, k[0], xlo[6]) if j == 3 else xlo[3 + j]
        kh = jnp.where(gx == DEV[0] - 1, k[31], xhi[3]) if j == 0 else xhi[3 + j]
        put(j, xlo[max(j - 1, 0)], kl)
        put(36 + j, xhi[min(j, 2)], kh)


def rows_kernel(pos, b, k, xlo, xhi, low, high):
    def put(plane, bv, kv):
        low[plane, 0:4] = bv[0:4]
        low[plane, 4:8] = kv[0:4]
        high[plane, 0:4] = bv[28:32]
        high[plane, 4:8] = kv[28:32]

    outer_planes(pos, k, xlo, xhi, put)
    loop(0, 32, lambda i: put(i + 4, b[i], k[i]), 4)


def assemble_two(pos, b, k, xlo, xhi, ylo, yhi, eb, ek):
    gy = pos[1]

    def put(plane, bv, kv):
        eb[plane, 12:44] = bv
        ek[plane, 12:44] = kv

    outer_planes(pos, k, xlo, xhi, put)
    loop(0, 32, lambda i: put(i + 4, b[i], k[i]), 4)
    row = rows_of(4)

    def edges(i):
        eb[i, 8:12] = ylo[i, 0:4]
        eb[i, 44:48] = yhi[i, 0:4]
        ek[i, 8:12] = jnp.where((row == 3) & (gy == 0), ek[i, 12:13], ylo[i, 4:8])
        ek[i, 44:48] = jnp.where((row == 0) & (gy == DEV[1] - 1), ek[i, 43:44], yhi[i, 4:8])

    loop(0, N2, edges, 4)


def lanes_kernel(pos, b, k, xlo, xhi, ylo, yhi, low, high, eb, ek):
    assemble_two(pos, b, k, xlo, xhi, ylo, yhi, eb, ek)
    group = lanes_of(R2) >> 2

    def column(col, slots):
        lo = jnp.zeros((R2, 128), F32)
        hi = jnp.zeros((R2, 128), F32)
        for s in range(slots):
            bv = eb[col * 16 + s, 8:48]
            kv = ek[col * 16 + s, 8:48]
            first, second = group == 2 * s, group == 2 * s + 1
            lo = jnp.where(first, rolled(bv, 8 * s), lo)
            lo = jnp.where(second, rolled(kv, 8 * s + 4), lo)
            hi = jnp.where(first, rolled(bv, 8 * s + 4), hi)
            hi = jnp.where(second, rolled(kv, 8 * s + 8), hi)
        low[col] = lo
        high[col] = hi

    loop(0, 2, lambda col: column(col, 16))
    column(2, 8)


def next_plane(parts):
    edge = lanes_of(parts[0].shape[0]) >= 120
    moved = [pltpu.roll(part, 120, 1) for part in parts]
    return [jnp.where(edge, moved[(c + 1) % 3], moved[c]) for c in range(3)]


def last_plane(parts):
    edge = lanes_of(parts[0].shape[0]) < 8
    moved = [pltpu.roll(part, 8, 1) for part in parts]
    return [jnp.where(edge, moved[c - 1], moved[c]) for c in range(3)]


def merge_faces(low, high):
    return jnp.where((lanes_of(low.shape[0]) & 7) == 3, high, pltpu.roll(low, 1, 1))


def flux_strips(v_ref, wx, wy, wz, faces):
    here, above, below = slice(8, 48), slice(9, 49), slice(7, 47)
    result, through = [], []
    for t in range(2):
        v = [v_ref[t, c, here] for c in range(3)]
        ahead = next_plane(v)
        fx = [wx[t, c, here] * (v[c] - ahead[c]) for c in range(3)]
        gx = last_plane(fx)
        total = []
        for c in range(3):
            fy = wy[t, c, here] * (v[c] - v_ref[t, c, above])
            gy = wy[t, c, below] * (v_ref[t, c, below] - v[c])
            fz = wz[t, c, here] * (v[c] - pltpu.roll(v[c], 127, 1))
            through.append(fz)
            total.append((fx[c] - gx[c]) + (fy - gy) + (fz - pltpu.roll(fz, 1, 1)))
        result.append(total)
    for c in range(3):
        faces[c, here] = merge_faces(through[c], through[3 + c])
    return result


def face_lanes(faces, p, here):
    return pltpu.roll(faces[p // 16, here], 124 - 8 * (p % 16), 1)


def flux_two(v_ref, wx, wy, wz, wm, faces, p, start, rows):
    here = slice(start, start + rows)
    above = slice(start + 1, start + rows + 1)
    below = slice(start - 1, start + rows - 1)
    lane = lanes_of(rows)
    v = v_ref[p, here]
    through = face_lanes(faces, p, here)
    fx = wx[p, here] * (v - v_ref[p + 1, here])
    gx = wx[p - 1, here] * (v_ref[p - 1, here] - v)
    fy = wy[p, here] * (v - v_ref[p, above])
    gy = wy[p, below] * (v_ref[p, below] - v)
    fz = jnp.where(lane == 127, through, wz[p, here] * (v - pltpu.roll(v, 127, 1)))
    gz = jnp.where(lane == 0, through, wm[p, here] * (pltpu.roll(v, 1, 1) - v))
    return (fx - gx) + (fy - gy) + (fz - gz)


def weights_kernel(pos, ek, wx, wy, wz, wm, sums, q):
    here = slice(8, 48)

    def invert(p):
        q[p, here] = 0.5 * rcp(ek[p, here])

    loop(0, N2, invert, 8)
    wx[0, here] = rcp(q[0, here] + q[1, here])

    def body(p):
        v = q[p, here]
        face_x = rcp(v + q[p + 1, here])
        face_y = rcp(v + q[p, 9:49])
        wx[p, here] = face_x
        wy[p, here] = face_y
        face_z = rcp(v + pltpu.roll(v, 127, 1))
        wz[p, here] = face_z
        wm[p, here] = pltpu.roll(face_z, 1, 1)
        sums[p, here] = rcp(v + q[p - 1, here]) + face_x + face_y + rcp(v + q[p, 7:47])

    loop(1, N2 - 1, body, 8)


def add_kernel(pos, first, second, out):
    planes, rows = out.shape[0], out.shape[1] - 16
    here = slice(8, 8 + rows)

    def add(p):
        out[p, here] = first[p, here] + second[p, here]

    loop(0, planes, add, 8)


def down_kernel(
    pos, eb, ek, wx, wy, wz, wm, sums, low, high, zlo, zhi,
    bk3, low3, high3, inv, f, s, tb, twx, twy, twz, tinv, tx,
    r1, tq, tf, ts, face_w, face_f, face_s, tmp,
):
    gx, gy, gz = pos[0], pos[1], pos[2]
    lane = lanes_of(R2)
    row = rows_of(R2) - 4
    here, above, below = slice(8, 48), slice(9, 49), slice(7, 47)
    inside_y = ((row >= 0) | (gy > 0)) & ((row < 32) | (gy < DEV[1] - 1))
    cell = lane & 7

    def inside_x(p):
        return ((p >= 4) | (gx > 0)) & ((p < 36) | (gx < DEV[0] - 1))

    for t, (first, second) in enumerate(((zlo, low), (high, zhi))):
        for c in range(3):
            one, two = first[c], second[c]
            tb[t, c, here] = jnp.where(cell < 4, one, pltpu.roll(two, 4, 1))
            k = jnp.where(cell < 4, pltpu.roll(one, 124, 1), two)
            if c == 2:
                k = jnp.where(lane < 64, k, 1.0)
            tq[t, c, here] = 0.5 * rcp(k)
    through = []
    for t in range(2):
        v = [tq[t, c, here] for c in range(3)]
        face_x = [rcp(a + b) for a, b in zip(v, next_plane(v))]
        below_x = last_plane(face_x)
        inside_z = ((cell >= 4) | (gz > 0)) if t == 0 else ((cell < 4) | (gz < DEV[2] - 1))
        for c in range(3):
            face_y = rcp(v[c] + tq[t, c, above])
            below_y = rcp(v[c] + tq[t, c, below])
            ahead = pltpu.roll(v[c], 127, 1)
            if t == 0:
                face_z = rcp(jnp.where((cell == 3) & (gz == 0), ahead, v[c]) + ahead)
            else:
                face_z = rcp(v[c] + jnp.where((cell == 3) & (gz == DEV[2] - 1), v[c], ahead))
            through.append(face_z)
            twx[t, c, here] = face_x[c]
            twy[t, c, here] = face_y
            twz[t, c, here] = face_z
            total = below_x[c] + face_x[c] + face_y + below_y + face_z + pltpu.roll(face_z, 1, 1)
            inside = inside_y & inside_z & inside_x(16 * c + (lane >> 3))
            value = jnp.where(inside, rcp(total), 0.0)
            tinv[t, c, here] = value
            tf[t, c, here] = value * tb[t, c, here] * inv_center
    for c in range(3):
        face_w[c, here] = merge_faces(through[c], through[3 + c])
    flux = flux_strips(tf, twx, twy, twz, face_f)
    for t in range(2):
        for c in range(3):
            rest = tb[t, c, here] - flux[t][c]
            step = keep_coef * tf[t, c, here] + push_coef * tinv[t, c, here] * rest
            ts[t, c, here] = step
            tx[t, c, here] = tf[t, c, here] + step
    through = [
        twz[t, c, here] * (ts[t, c, here] - pltpu.roll(ts[t, c, here], 127, 1))
        for t in range(2)
        for c in range(3)
    ]
    for c in range(3):
        face_s[c, here] = merge_faces(through[c], through[3 + c])

    mask = jnp.where(inside_y, 1.0, 0.0)

    def weigh(p):
        through = face_lanes(face_w, p, here)
        face_z = jnp.where(lane == 127, through, wz[p, here])
        below_z = jnp.where(lane == 0, through, wm[p, here])
        scale = jnp.where(inside_x(p), 1.0, 0.0)
        value = jnp.where(mask * scale > 0.5, rcp(sums[p, here] + face_z + below_z), 0.0)
        inv[p, here] = value
        f[p, here] = value * eb[p, here] * inv_center

    loop(1, N2 - 1, weigh, 13)

    def smooth(p):
        rest = eb[p, here] - flux_two(f, wx, wy, wz, wm, face_f, p, 8, R2)
        step = keep_coef * f[p, here] + push_coef * inv[p, here] * rest
        r1[p, here] = rest
        s[p, here] = step

    loop(2, N2 - 2, smooth, 6)

    to_b = square(lambda i, j: (i >> 1) == j, 0.125)
    to_k = square(lambda i, j: (i >> 1) + 64 == j, 0.125)

    def coarsen(i):
        p = 2 * i + 4
        total = r1[p, 12:44] + r1[p + 1, 12:44]
        total = total - flux_two(s, wx, wy, wz, wm, face_s, p, 12, 32)
        tmp[0, i, 0:32] = total - flux_two(s, wx, wy, wz, wm, face_s, p + 1, 12, 32)
        tmp[1, i, 0:32] = ek[p, 12:44] + ek[p + 1, 12:44]

    loop(0, 16, coarsen, 4)
    pairs = [row_pairs(tmp.at[j], range(16), 0, 16) for j in range(2)]
    both = select_dot(pairs[0], to_b) + select_dot(pairs[1], to_k)
    for i in range(16):
        part = both[16 * i : 16 * i + 16]
        bk3[i] = part
        if i < 13:
            low3[i] = part
        if i >= 3:
            high3[i - 3] = part


def planes_kernel(pos, bk, xlo, xhi, out, low, high):
    gx = pos[0]
    right = lanes_of(16) >= 64

    def put(p, value):
        out[p] = value
        low[p] = value[0:8]
        high[p] = value[8:16]
        if 9 <= p < 33:
            low[p + 33] = value[8:16]
            high[p + 33] = value[0:8]

    for j in range(13):
        lo, hi = xlo[j], xhi[j]
        if j == 12:
            lo = jnp.where(right & (gx == 0), bk[0], lo)
        if j == 0:
            hi = jnp.where(right & (gx == DEV[0] - 1), bk[15], hi)
        put(j, lo)
        put(29 + j, hi)
    for j in range(16):
        put(13 + j, bk[j])


def three_rows(pos, own, ylo, yhi, p):
    gy = pos[1]
    right = lanes_of(16) >= 64
    row = rows_of(16)
    far = jnp.where((p >= 9) & (p < 33), p + 33, p)
    lo = jnp.concatenate([ylo[far], ylo[p]], axis=0)
    hi = jnp.concatenate([yhi[p], yhi[far]], axis=0)
    lo = jnp.where(right & (row == 15) & (gy == 0), own[p, 0:1], lo)
    hi = jnp.where(right & (row == 0) & (gy == DEV[1] - 1), own[p, 15:16], hi)
    return lo, own[p], hi


def slots_kernel(pos, own, ylo, yhi, low, high):
    quarter = (lanes_of(16) & 63) >> 4

    def column(col):
        total_lo = [None] * 3
        total_hi = [None] * 3
        for slot in range(4):
            p = jnp.minimum(col * 4 + slot, N3 - 1)
            mine = quarter == slot
            for g, e in enumerate(three_rows(pos, own, ylo, yhi, p)):
                lo, hi = rolled(e, 16 * slot), rolled(e, 16 * slot - 48)
                total_lo[g] = lo if slot == 0 else jnp.where(mine, lo, total_lo[g])
                total_hi[g] = hi if slot == 0 else jnp.where(mine, hi, total_hi[g])
        for g in range(3):
            low[col, 16 * g : 16 * g + 16] = total_lo[g]
            high[col, 16 * g : 16 * g + 16] = total_hi[g]

    loop(0, 11, column, 4)


def flux_one(v_ref, wx, wy, wz, wm, p, rows):
    here, above, below = slice(8, 8 + rows), slice(9, 9 + rows), slice(7, 7 + rows)
    v = v_ref[p, here]
    fx = wx[p, here] * (v - v_ref[p + 1, here])
    gx = wx[p - 1, here] * (v_ref[p - 1, here] - v)
    fy = wy[p, here] * (v - v_ref[p, above])
    gy = wy[p, below] * (v_ref[p, below] - v)
    fz = wz[p, here] * (v - pltpu.roll(v, 127, 1))
    gz = wm[p, here] * (pltpu.roll(v, 1, 1) - v)
    return (fx - gx) + (fy - gy) + (fz - gz)


UNROLL = {48: 10, 24: 9, 32: 8, 16: 8, 8: 4}


def weigh_one(q, b, wx, wy, wz, wm, inv, f, rows, low, high, first, last, inside):
    here = slice(8, 8 + rows)
    wx[low - 1, here] = rcp(q[low - 1, here] + q[low, here])

    def body(p):
        v = q[p, here]
        up = pltpu.roll(v, 127, 1)
        face_x = rcp(v + q[p + 1, here])
        face_y = rcp(v + q[p, 9 : 9 + rows])
        below_x = rcp(v + q[p - 1, here])
        below_y = rcp(v + q[p, 7 : 7 + rows])
        face_z = rcp(jnp.where(first, up, v) + jnp.where(last, v, up))
        lower_z = pltpu.roll(face_z, 1, 1)
        wx[p, here] = face_x
        wy[p, here] = face_y
        wz[p, here] = face_z
        wm[p, here] = lower_z
        total = below_x + face_x + face_y + below_y + face_z + lower_z
        value = jnp.where(inside(p), rcp(total), 0.0)
        inv[p, here] = value
        f[p, here] = value * b[p, here] * inv_center

    loop(low, high, body, UNROLL[rows])


def smooth_one(b, wx, wy, wz, wm, inv, f, r1, s, xs, rows, low, high):
    here = slice(8, 8 + rows)

    def body(p):
        rest = b[p, here] - flux_one(f, wx, wy, wz, wm, p, rows)
        step = keep_coef * f[p, here] + push_coef * inv[p, here] * rest
        r1[p, here] = rest
        s[p, here] = step
        if xs is not None:
            xs[p, here] = f[p, here] + step

    loop(low, high, body, UNROLL[rows])


def finish_one(b, wx, wy, wz, wm, inv, xs, f, r0, out, shift, rows, ranges):
    here = slice(8, 8 + rows)

    def start(p):
        rest = b[p, here] - flux_one(xs, wx, wy, wz, wm, p, rows)
        r0[p, here] = rest
        f[p, here] = inv[p, here] * rest * inv_center

    loop(*ranges[0], start, UNROLL[rows])

    def end(p):
        rest = r0[p, here] - flux_one(f, wx, wy, wz, wm, p, rows)
        step = keep_coef * f[p, here] + push_coef * inv[p, here] * rest
        out[p + shift, here] = xs[p, here] + f[p, here] + step

    loop(*ranges[1], end, UNROLL[rows])


def signed(lane, limit):
    return jnp.where(lane < limit, lane, lane - 128)


def middle_kernel(
    pos, own, ylo, yhi, zlo, zhi,
    payload, b3, wx3, wy3, wz3, wm3, inv3, f3, s3, b4, wx4, wy4, wz4, wm4, inv4, f4, s4,
    k3, q3, r3, k4, q4, r4, tmp,
):
    gx, gy, gz = pos[0], pos[1], pos[2]
    lane = lanes_of(16)

    def unpack(p, lo, hi, slot):
        for g, e in enumerate(three_rows(pos, own, ylo, yhi, p)):
            rows = slice(8 + 16 * g, 24 + 16 * g)
            part = slice(16 * g, 16 * g + 16)
            up, dn = rolled(hi[part], 64 - 16 * slot), rolled(lo[part], 112 - 16 * slot)
            bv = jnp.where((lane >= 64) & (lane < 80), up, e)
            b3[p, rows] = jnp.where(lane >= 112, dn, bv)
            kv = jnp.where(lane < 16, up, jnp.where((lane >= 48) & (lane < 64), dn, e))
            kv = pltpu.roll(kv, 64, 1)
            kv = jnp.where((lane >= 80) & (lane < 112), 1.0, kv)
            k3[p, rows] = kv
            q3[p, rows] = 2.0 * rcp(kv)

    def column(col, slots):
        lo, hi = zlo[col], zhi[col]
        for slot in range(slots):
            unpack(col * 4 + slot, lo, hi, slot)

    loop(0, 10, lambda col: column(col, 4), 2)
    column(10, 2)

    def region(rows, y_first, x_first, nx, ny, nz):
        y = rows_of(rows) + y_first
        z = signed(lanes_of(rows), 96)
        inside_y = ((y >= 0) | (gy > 0)) & ((y < ny) | (gy < DEV[1] - 1))
        inside_z = ((z >= 0) | (gz > 0)) & ((z < nz) | (gz < DEV[2] - 1))
        inside_yz = jnp.where(inside_y & inside_z, 1.0, 0.0)

        def inside(p):
            x = p + x_first
            inside_x = ((x >= 0) | (gx > 0)) & ((x < nx) | (gx < DEV[0] - 1))
            return inside_yz * jnp.where(inside_x, 1.0, 0.0) > 0.5

        return inside

    def edges(rows, cells):
        lane = lanes_of(rows)
        return (lane == 127) & (gz == 0), (lane == cells - 1) & (gz == DEV[2] - 1)

    inside = region(R3, -16, -13, 16, 16, 64)
    weigh_one(q3, b3, wx3, wy3, wz3, wm3, inv3, f3, R3, 1, N3 - 1, *edges(R3, 64), inside)
    smooth_one(b3, wx3, wy3, wz3, wm3, inv3, f3, r3, s3, None, R3, 2, N3 - 2)

    def pick(i, j):
        target = signed(j, 64)
        return ((signed(i, 96) >> 1) == target) & (target >= -7) & (target < 39)

    narrow = square(pick, 0.125)
    valid = (lanes_of(R4) < 39) | (lanes_of(R4) >= 121)
    row = rows_of(R4)

    def coarse_k(i):
        p = 2 * i + 1
        tmp[0, i, 8:56] = k3[p, 8:56] + k3[p + 1, 8:56]

    def coarse_b(i):
        p = 2 * i + 1
        total = r3[p, 8:56] + r3[p + 1, 8:56] - flux_one(s3, wx3, wy3, wz3, wm3, p, R3)
        tmp[1, i, 8:56] = total - flux_one(s3, wx3, wy3, wz3, wm3, p + 1, R3)

    loop(0, N4, coarse_k, 5)
    loop(1, N4 - 1, coarse_b, 3)
    value = select_dot(row_pairs(tmp.at[0], range(N4), 12, R4), narrow)
    for i in range(N4):
        part = jnp.where(valid, value[R4 * i : R4 * i + R4], 1.0)
        part = jnp.where((row == 5) & (gy == 0), pltpu.roll(part, R4 - 1, 0), part)
        part = jnp.where((row == 14) & (gy == DEV[1] - 1), pltpu.roll(part, 1, 0), part)
        k4[i, 8:32] = part
    value = select_dot(row_pairs(tmp.at[1], range(1, N4 - 1), 12, R4), narrow)
    for i in range(1, N4 - 1):
        b4[i, 8:32] = value[R4 * (i - 1) : R4 * i]
    k4[5, 8:32] = jnp.where(gx == 0, k4[6, 8:32], k4[5, 8:32])
    k4[14, 8:32] = jnp.where(gx == DEV[0] - 1, k4[13, 8:32], k4[14, 8:32])

    def invert(i):
        q4[i, 8:32] = 8.0 * rcp(k4[i, 8:32])

    loop(0, N4, invert, 5)
    inside = region(R4, -6, -6, 8, 8, 32)
    weigh_one(q4, b4, wx4, wy4, wz4, wm4, inv4, f4, R4, 1, N4 - 1, *edges(R4, 32), inside)
    smooth_one(b4, wx4, wy4, wz4, wm4, inv4, f4, r4, s4, None, R4, 2, N4 - 2)

    cell = lanes_of(4) & 15
    spread = square(lambda i, j: (signed(i, 64) >> 1) == (j & 15), 0.125)
    spread_halo = square(
        lambda i, j: ((signed(i, 64) >> 1) == ((j & 15) ^ 16) - ((j & 8) << 2))
        & (((j & 15) < 4) | ((j & 15) >= 12)),
        0.125,
    )
    between = (cell >= 4) & (cell < 12)
    slot = lanes_of(4) >> 4
    quad = rows_of(4)
    parts = [[[None, None], [None, None]] for _ in range(2)]
    for i in range(4):
        p = 2 * i + 6
        total = r4[p, 8:32] + r4[p + 1, 8:32] - flux_one(s4, wx4, wy4, wz4, wm4, p, R4)
        tmp[0, i, 8:32] = total - flux_one(s4, wx4, wy4, wz4, wm4, p + 1, R4)
        tmp[1, i, 8:32] = k4[p, 8:32] + k4[p + 1, 8:32]
    for i in range(4):
        mine = slot == (i % 2) * 4 + quad
        for a in range(2):
            pair = row_pairs(tmp.at[a], [i], 14, 4)
            for h, matrix in enumerate((spread, spread_halo)):
                value = select_dot(pair, matrix)
                if h == 1:
                    value = jnp.where(between, 1.0, value)
                value = jnp.sum(jnp.where(mine, value, 0.0), axis=0, keepdims=True)
                old = parts[h][a][i // 2]
                parts[h][a][i // 2] = value if old is None else old + value
    value = jnp.concatenate([row for h in parts for a in h for row in a], axis=0)
    for d in range(32):
        payload[d] = value


def exchange_blocks(value):
    row = rows_of(8)
    group = lanes_of(8) >> 4
    for bit in (1, 2):
        upper = pltpu.roll(pltpu.roll(value, 8 - bit, 0), 16 * bit, 1)
        lower = pltpu.roll(pltpu.roll(value, bit, 0), 128 - 16 * bit, 1)
        moved = jnp.where((row & bit) == 0, upper, lower)
        value = jnp.where((row & bit) == (group & bit), value, moved)
    moved = pltpu.roll(pltpu.roll(value, 4, 0), 64, 1)
    return jnp.where((row & 4) == (group & 4), value, moved)


WHOLE = ((16, 32, 128), (8, 16, 64), (4, 8, 32))


def up_kernel(
    pos, own, up, down, b3, wx3, wy3, wz3, wm3, inv3, x3, b4, wx4, wy4, wz4, wm4, inv4, x4,
    eb, wx, wy, wz, wm, inv, xs, tb, twx, twy, twz, tinv, tx,
    out, *scratch,
):
    gx, gy, gz = pos[0], pos[1], pos[2]
    levels = [scratch[13 * i : 13 * i + 13] for i in range(3)]
    e5, e6, raw, f4, r4, e4, y4, f3, r3, e3, y3, f2, r2, y2, tf, ty, face_x, face_f, ob, tmp, sems = scratch[39:]

    for level, (nx, ny, nz) in enumerate(WHOLE):
        b, k, q, wx_, wy_, wz_, wm_, inv_, f, r, s, x, r0 = levels[level]
        for ref in (f, s, x):
            ref[0] = jnp.zeros(ref.shape[1:], F32)
            ref[nx + 1] = jnp.zeros(ref.shape[1:], F32)

            def clear(p, ref=ref, ny=ny):
                ref[p, 0:8] = jnp.zeros((8, 128), F32)
                ref[p, 8 + ny : 16 + ny] = jnp.zeros((8, 128), F32)

            loop(1, nx + 1, clear)
    for p in (0, 1, 2, 19, 20, 21):
        e5[p] = jnp.zeros(e5.shape[1:], F32)

    def clear(p):
        e5[p, 0:8] = jnp.zeros((8, 128), F32)
        e5[p, 40:48] = jnp.zeros((8, 128), F32)

    loop(3, 19, clear)

    b5, k5 = levels[0][0], levels[0][1]

    for n in (3, 4, 5):
        raw[pl.ds(n, 128, stride=8)] = jnp.ones((128, 128), F32)
    for n, part, first in ((0, own, 0), (1, up, 0), (2, up, 4), (6, down, 4), (7, down, 0)):
        for kind in range(4):
            raw[pl.ds(8 * kind + n, 32, stride=32)] = part[pl.ds(first + kind, 32, stride=8)]

    def unpack(d):
        dx, dy = d // 8, d % 8
        rows = pl.ds(8 + 4 * dy, 4)
        for kind in range(4):
            value = exchange_blocks(raw[pl.ds(pl.multiple_of(d * 32 + kind * 8, 8), 8)])
            target = (b5, k5)[kind // 2]
            p = 1 + 4 * dx + 2 * (kind % 2)
            target[p, rows] = value[0:4]
            target[p + 1, rows] = value[4:8]

    loop(0, 32, unpack, 8)

    def ends(level):
        nx, ny, nz = WHOLE[level]
        k, q = levels[level][1], levels[level][2]
        factor = 0.5 * 4.0 ** (level + 3)

        def invert(p):
            value = factor * rcp(k[p, 8 : 8 + ny])
            q[p, 8 : 8 + ny] = value
            q[p, 7:8] = value[0:1]
            q[p, 8 + ny : 9 + ny] = value[ny - 1 : ny]

        loop(1, nx + 1, invert, 4)
        q[0] = q[1]
        q[nx + 1] = q[nx]

    def down(level):
        nx, ny, nz = WHOLE[level]
        b, k, q, wx_, wy_, wz_, wm_, inv_, f, r, s, x, r0 = levels[level]
        ends(level)

        def below(p):
            wy_[p, 7:8] = rcp(q[p, 7:8] + q[p, 8:9])

        loop(1, nx + 1, below, 4)
        z = signed(lanes_of(ny), 72) + gz * (nz // DEV[2])
        weigh_one(
            q, b, wx_, wy_, wz_, wm_, inv_, f, ny, 1, nx + 1, z == -1, z == nz - 1,
            lambda p: (z >= 0) & (z < nz),
        )
        smooth_one(b, wx_, wy_, wz_, wm_, inv_, f, r, s, x, ny, 1, nx + 1)
        if level == 2:
            return
        nb, nk = levels[level + 1][0], levels[level + 1][1]
        low, high = ((-9, 17), (-4, 8))[level]

        def kept(lane):
            return (signed(lane, 64) >= low) & (signed(lane, 64) < high)

        narrow = square(lambda i, j: ((signed(i, 72) >> 1) == signed(j, 64)) & kept(j), 0.125)
        valid = kept(lanes_of(ny // 2))

        def coarsen(i):
            p = 2 * i - 1
            here = slice(8, 8 + ny)
            total = r[p, here] + r[p + 1, here] - flux_one(s, wx_, wy_, wz_, wm_, p, ny)
            tmp[0, i, here] = total - flux_one(s, wx_, wy_, wz_, wm_, p + 1, ny)
            tmp[1, i, here] = k[p, here] + k[p + 1, here]

        count = ny // 2
        planes = range(1, nx // 2 + 1)
        loop(1, nx // 2 + 1, coarsen, 64 // ny)
        for a, target in enumerate((nb, nk)):
            value = select_dot(row_pairs(tmp.at[a], planes, 8, count), narrow)
            for n, i in enumerate(planes):
                part = value[count * n : count * n + count]
                target[i, 8 : 8 + count] = jnp.where(valid, part, 1.0) if a == 1 else part

    for level in range(3):
        down(level)

    def rise(level, coarse, target, shift):
        nx, ny, nz = WHOLE[level]
        b, k, q, wx_, wy_, wz_, wm_, inv_, f, r, s, x, r0 = levels[level]
        widen = square(lambda i, j: signed(i, 64) == (signed(j, 64) >> 1), 1.0)
        count = ny // 2

        planes = range(1, nx // 2 + 1)
        value = jnp.concatenate([coarse[i, 8 : 8 + count] for i in planes], axis=0)
        spread_rows(tmp.at[0], planes, 8, count, select_dot(value, widen))

        def add(i):
            wide = tmp[0, i, 8 : 8 + ny]
            x[2 * i - 1, 8 : 8 + ny] += wide
            x[2 * i, 8 : 8 + ny] += wide

        loop(1, nx // 2 + 1, add, 64 // ny)
        span = (1, nx + 1)
        finish_one(b, wx_, wy_, wz_, wm_, inv_, x, f, r0, target, shift, ny, (span, span))

    rise(1, levels[2][11], e6, 0)
    rise(0, e6, e5, 2)

    widen = square(lambda i, j: signed(i, 64) == (signed(j, 64) >> 1), 1.0)

    planes = range(1, 9)
    value = [e5[gx * 4 + i, pl.ds(pl.multiple_of(4 * gy, 4), 24)] for i in planes]
    value = select_dot(jnp.concatenate(value, axis=0), widen)
    for n, i in enumerate(planes):
        spread_rows(tmp.at[0], [i], 8, 12, value[24 * n + 5 : 24 * n + 17])

    def add_four(i):
        wide = tmp[0, i, 8:32]
        y4[2 * i, 8:32] = x4[2 * i, 8:32] + wide
        y4[2 * i + 1, 8:32] = x4[2 * i + 1, 8:32] + wide

    loop(1, 9, add_four, 4)
    finish_one(b4, wx4, wy4, wz4, wm4, inv4, y4, f4, r4, e4, 0, R4, ((3, 17), (4, 16)))

    widen3 = square(lambda i, j: signed(i, 64) == (signed(j, 96) >> 1), 1.0)

    planes = range(4, 16)
    value = jnp.concatenate([e4[i, 8:32] for i in planes], axis=0)
    spread_rows(tmp.at[0], planes, 12, 24, select_dot(value, widen3))

    def add_three(i):
        wide = tmp[0, i, 8:56]
        y3[2 * i + 1, 8:56] = x3[2 * i + 1, 8:56] + wide
        y3[2 * i + 2, 8:56] = x3[2 * i + 2, 8:56] + wide

    loop(4, 16, add_three, 3)
    finish_one(b3, wx3, wy3, wz3, wm3, inv3, y3, f3, r3, e3, 0, R3, ((11, 31), (12, 30)))

    wide = square(lambda i, j: i == (j >> 1), 1.0)
    planes = range(1, 19)
    value = jnp.concatenate([e3[i + 11, 22:46] for i in planes], axis=0)
    spread_rows(tmp.at[0], planes, 8, 24, select_dot(value, wide))
    here = slice(8, 48)
    group = lanes_of(24) >> 4
    for t in range(2):
        wide = square(lambda i, j: signed(i, 96) == ((j & 7) + 128 * t - 4) >> 1, 1.0)
        parts = select_dot(value, wide)
        for c in range(3):
            total = jnp.zeros((24, 128), F32)
            for n, i in enumerate(planes):
                if i // 8 == c:
                    total = jnp.where(group == i % 8, parts[24 * n : 24 * n + 24], total)
            spread_rows(tmp.at[1], [3 * t + c], 8, 24, total)
            ty[t, c, here] = tx[t, c, here] + tmp[1, 3 * t + c, here]
    flux = flux_strips(ty, twx, twy, twz, face_x)
    for t in range(2):
        for c in range(3):
            tf[t, c, here] = tinv[t, c, here] * (tb[t, c, here] - flux[t][c]) * inv_center
    through = [
        twz[t, c, here] * (tf[t, c, here] - pltpu.roll(tf[t, c, here], 127, 1))
        for t in range(2)
        for c in range(3)
    ]
    for c in range(3):
        face_f[c, here] = merge_faces(through[c], through[3 + c])

    def add_two(i):
        part = tmp[0, i, here]
        y2[2 * i, here] = xs[2 * i, here] + part
        y2[2 * i + 1, here] = xs[2 * i + 1, here] + part

    loop(1, 19, add_two, 3)

    def start(p):
        rest = eb[p, here] - flux_two(y2, wx, wy, wz, wm, face_x, p, 8, R2)
        r2[p, here] = rest
        f2[p, here] = inv[p, here] * rest * inv_center

    loop(3, 37, start, 7)
    core = slice(12, 44)

    def end(i):
        p = i + 4
        rest = r2[p, core] - flux_two(f2, wx, wy, wz, wm, face_f, p, 12, 32)
        first = f2[p, core]
        step = keep_coef * first + push_coef * inv[p, core] * rest
        ob[i] = y2[p, core] + first + step

    def leave(n):
        part = pl.ds(pl.multiple_of(8 * n, 8), 8)
        return pltpu.make_async_copy(ob.at[part], out.at[part], sems.at[n])

    @pl.loop(0, 4)
    def _(n):
        for j in range(8):
            end(8 * n + j)
        leave(n).start()

    for n in range(4):
        leave(n).wait()


def vmem(array):
    return pltpu.with_memory_space_constraint(array, pltpu.VMEM)


def call(kernel, args, outs, scratch=(), final=False):
    size = sum(4 * math.prod(shape) for shape in scratch) + sum(4 * math.prod(shape) for shape in outs)
    out_type = jax.ShapeDtypeStruct if final else pltpu.VMEM
    held = args[1:]
    return pl.pallas_call(
        kernel,
        out_shape=[out_type(shape, F32) for shape in outs],
        in_specs=[pl.BlockSpec(memory_space=pltpu.SMEM)]
        + [pl.BlockSpec(memory_space=pltpu.VMEM)] * len(held),
        out_specs=[pl.BlockSpec(memory_space=pl.ANY if final else pltpu.VMEM)] * len(outs),
        scratch_shapes=[pltpu.VMEM(shape, F32) for shape in scratch]
        + [pltpu.SemaphoreType.DMA((4,))] * final,
        compiler_params=pltpu.CompilerParams(vmem_limit_bytes=size + (4 << 20)),
    )(args[0], *held)


def load(kernel, b, k, shape, count):
    return pl.pallas_call(
        kernel,
        out_shape=[pltpu.VMEM(shape, F32)] * 2,
        in_specs=[pl.BlockSpec(memory_space=pl.ANY)] * 2,
        out_specs=[pl.BlockSpec(memory_space=pltpu.VMEM)] * 2,
        scratch_shapes=[pltpu.SemaphoreType.DMA((count,))],
    )(b, k)


def swap(low, high, axis):
    count = lax.axis_size(axis)
    ring = range(count)
    before = lax.ppermute(high, axis, [(i, (i + 1) % count) for i in ring])
    after = lax.ppermute(low, axis, [(i, (i - 1) % count) for i in ring])
    return vmem(before), vmem(after)


def shards(b, k):
    pos = jnp.stack([lax.axis_index(axis) for axis in AXES]).astype(jnp.int32)
    low, high = load(edge_kernel, b, k, (7, 32, 128), 4)
    xlo, xhi = swap(low, high, "gx")
    b, k = load(load_kernel, b, k, (32, 32, 128), 8)
    low, high = call(rows_kernel, (pos, b, k, xlo, xhi), [(N2, 8, 128)] * 2)
    ylo, yhi = swap(low, high, "gy")
    ext2, strip, face = (N2, T2, 128), (2, 3, T2, 128), (3, T2, 128)
    low, high, eb, ek = call(
        lanes_kernel, (pos, b, k, xlo, xhi, ylo, yhi), [(3, R2, 128)] * 2 + [ext2] * 2
    )
    zlo, zhi = swap(low, high, "gz")
    wx, wy, wz, wm, sums = call(weights_kernel, (pos, ek), [ext2] * 5, [ext2])
    bk3, low, high, inv, first, second, *rest = call(
        down_kernel,
        (pos, eb, ek, wx, wy, wz, wm, sums, low, high, zlo, zhi),
        [(16, 16, 128)] + [(13, 16, 128)] * 2 + [ext2] * 3 + [strip] * 6,
        [ext2] + [strip] * 3 + [face] * 3 + [(2, 16, 32, 128)],
    )
    (xs,) = call(add_kernel, (pos, first, second), [ext2])
    state2 = [eb, wx, wy, wz, wm, inv, xs, *rest]
    xlo, xhi = swap(low, high, "gx")
    own, low, high = call(
        planes_kernel, (pos, bk3, xlo, xhi), [(N3, 16, 128)] + [(N3 + 24, 8, 128)] * 2
    )
    ylo, yhi = swap(low, high, "gy")
    low, high = call(slots_kernel, (pos, own, ylo, yhi), [(11, 48, 128)] * 2)
    zlo, zhi = swap(low, high, "gz")
    three, four = (N3, T3, 128), (N4, T4, 128)
    payload, *state = call(
        middle_kernel,
        (pos, own, ylo, yhi, zlo, zhi),
        [(32, 8, 128)] + [three] * 8 + [four] * 8,
        [three] * 3 + [four] * 3 + [(2, N4, T3, 128)],
    )
    (x3,) = call(add_kernel, (pos, *state[6:8]), [three])
    (x4,) = call(add_kernel, (pos, *state[14:16]), [four])
    state = [*state[:6], x3, *state[8:14], x4]
    recv = lax.all_to_all(payload, AXES[:2], 0, 0, tiled=True).reshape(256, 128)
    ring = range(DEV[2])
    recv = [recv] + [
        lax.ppermute(recv, "gz", [(i, (i - d) % DEV[2]) for i in ring]) for d in (1, -1)
    ]
    recv = [vmem(part) for part in recv]
    scratch = []
    for nx, ny, _ in WHOLE:
        scratch += [(nx + 2, ny + 16, 128)] * 13
    scratch += [(22, 56, 128), (10, 32, 128), (1024, 128)]
    scratch += [four] * 4 + [three] * 4 + [ext2] * 3 + [strip] * 2 + [face] * 2 + [(32, 32, 128)]
    scratch += [(2, 20, T3, 128)]
    (out,) = call(up_kernel, (pos, *recv, *state, *state2), [(32, 32, 128)], scratch, True)
    return out


def solution(mesh):
    spec = P(*AXES)
    return jax.shard_map(shards, mesh=mesh, in_specs=(spec, spec), out_specs=spec, check_vma=False)
```

```python
import math

import jax
import jax.numpy as jnp
from jax import lax
from jax.experimental import pallas as pl
from jax.experimental.pallas import tpu as pltpu
from jax.sharding import PartitionSpec as P

F32 = jnp.float32
AXES = ("gx", "gy", "gz")
DEV = (4, 8, 8)

center_eig = 1.25
half_width = 0.75
rho_first = half_width / center_eig
rho_second = 1.0 / (2.0 * center_eig / half_width - rho_first)
keep_coef = rho_second * rho_first
push_coef = 2.0 * rho_second / half_width
inv_center = 1.0 / center_eig

N2, R2, T2 = 40, 40, 56
N3, R3, T3 = 42, 48, 64
N4, R4, T4 = 20, 24, 40


def rcp(value):
    guess = pl.reciprocal(value, approx=True)
    return guess * (2.0 - value * guess)


def row_pairs(ref, planes, start, count):
    even = [ref[i, pl.ds(start, count, stride=2)] for i in planes]
    odd = [ref[i, pl.ds(start + 1, count, stride=2)] for i in planes]
    return jnp.concatenate(even, axis=0) + jnp.concatenate(odd, axis=0)


def spread_rows(ref, planes, start, count, value):
    for n, i in enumerate(planes):
        part = value[n * count : (n + 1) * count]
        ref[i, pl.ds(start, count, stride=2)] = part
        ref[i, pl.ds(start + 1, count, stride=2)] = part


def lanes_of(rows):
    return lax.broadcasted_iota(jnp.int32, (rows, 128), 1)


def rows_of(rows):
    return lax.broadcasted_iota(jnp.int32, (rows, 128), 0)


def rolled(value, shift):
    shift = shift % 128
    return value if shift == 0 else pltpu.roll(value, shift, 1)


def select_dot(value, matrix):
    high = value.astype(jnp.bfloat16)
    rest = value - high.astype(F32)
    middle = rest.astype(jnp.bfloat16)
    low = (rest - middle.astype(F32)).astype(jnp.bfloat16)
    parts = jnp.concatenate([high, middle, low], axis=1)
    return jnp.dot(parts, jnp.concatenate([matrix] * 3, axis=0), preferred_element_type=F32)


def square(condition, value):
    source = lax.broadcasted_iota(jnp.int32, (128, 128), 0)
    target = lax.broadcasted_iota(jnp.int32, (128, 128), 1)
    return jnp.where(condition(source, target), value, 0.0).astype(jnp.bfloat16)


def loop(low, high, body, unroll=1):
    blocks = (high - low) // unroll
    if blocks > 1:

        @pl.loop(0, blocks)
        def _(block):
            for j in range(unroll):
                body(low + block * unroll + j)

        low += blocks * unroll
    for index in range(low, high):
        body(index)


def copy_all(pairs, sems):
    copies = [
        pltpu.make_async_copy(source, target, sems.at[n]) for n, (source, target) in enumerate(pairs)
    ]
    for copy in copies:
        copy.start()
    for copy in copies:
        copy.wait()


def edge_kernel(b, k, low, high, sems):
    copy_all(
        (
            (b.at[pl.ds(0, 3)], low.at[pl.ds(0, 3)]),
            (k.at[pl.ds(0, 4)], low.at[pl.ds(3, 4)]),
            (b.at[pl.ds(29, 3)], high.at[pl.ds(0, 3)]),
            (k.at[pl.ds(28, 4)], high.at[pl.ds(3, 4)]),
        ),
        sems,
    )


def load_kernel(b, k, bv, kv, sems):
    parts = [pl.ds(8 * n, 8) for n in range(4)]
    copy_all([(x.at[part], y.at[part]) for part in parts for x, y in ((b, bv), (k, kv))], sems)


def outer_planes(pos, k, xlo, xhi, put):
    gx = pos[0]
    for j in range(4):
        kl = jnp.where(gx == 0, k[0], xlo[6]) if j == 3 else xlo[3 + j]
        kh = jnp.where(gx == DEV[0] - 1, k[31], xhi[3]) if j == 0 else xhi[3 + j]
        put(j, xlo[max(j - 1, 0)], kl)
        put(36 + j, xhi[min(j, 2)], kh)


def rows_kernel(pos, b, k, xlo, xhi, low, high):
    def put(plane, bv, kv):
        low[plane, 0:4] = bv[0:4]
        low[plane, 4:8] = kv[0:4]
        high[plane, 0:4] = bv[28:32]
        high[plane, 4:8] = kv[28:32]

    outer_planes(pos, k, xlo, xhi, put)
    loop(0, 32, lambda i: put(i + 4, b[i], k[i]), 4)


def assemble_two(pos, b, k, xlo, xhi, ylo, yhi, eb, ek):
    gy = pos[1]

    def put(plane, bv, kv):
        eb[plane, 12:44] = bv
        ek[plane, 12:44] = kv

    outer_planes(pos, k, xlo, xhi, put)
    loop(0, 32, lambda i: put(i + 4, b[i], k[i]), 4)
    row = rows_of(4)

    def edges(i):
        eb[i, 8:12] = ylo[i, 0:4]
        eb[i, 44:48] = yhi[i, 0:4]
        ek[i, 8:12] = jnp.where((row == 3) & (gy == 0), ek[i, 12:13], ylo[i, 4:8])
        ek[i, 44:48] = jnp.where((row == 0) & (gy == DEV[1] - 1), ek[i, 43:44], yhi[i, 4:8])

    loop(0, N2, edges, 4)


def lanes_kernel(pos, b, k, xlo, xhi, ylo, yhi, low, high, eb, ek):
    assemble_two(pos, b, k, xlo, xhi, ylo, yhi, eb, ek)
    group = lanes_of(R2) >> 2

    def column(col, slots):
        lo = jnp.zeros((R2, 128), F32)
        hi = jnp.zeros((R2, 128), F32)
        for s in range(slots):
            bv = eb[col * 16 + s, 8:48]
            kv = ek[col * 16 + s, 8:48]
            first, second = group == 2 * s, group == 2 * s + 1
            lo = jnp.where(first, rolled(bv, 8 * s), lo)
            lo = jnp.where(second, rolled(kv, 8 * s + 4), lo)
            hi = jnp.where(first, rolled(bv, 8 * s + 4), hi)
            hi = jnp.where(second, rolled(kv, 8 * s + 8), hi)
        low[col] = lo
        high[col] = hi

    loop(0, 2, lambda col: column(col, 16))
    column(2, 8)


def next_plane(parts):
    edge = lanes_of(parts[0].shape[0]) >= 120
    moved = [pltpu.roll(part, 120, 1) for part in parts]
    return [jnp.where(edge, moved[(c + 1) % 3], moved[c]) for c in range(3)]


def last_plane(parts):
    edge = lanes_of(parts[0].shape[0]) < 8
    moved = [pltpu.roll(part, 8, 1) for part in parts]
    return [jnp.where(edge, moved[c - 1], moved[c]) for c in range(3)]


def merge_faces(low, high):
    return jnp.where((lanes_of(low.shape[0]) & 7) == 3, high, pltpu.roll(low, 1, 1))


def flux_strips(v_ref, wx, wy, wz, faces):
    here, above, below = slice(8, 48), slice(9, 49), slice(7, 47)
    result, through = [], []
    for t in range(2):
        v = [v_ref[t, c, here] for c in range(3)]
        ahead, behind = next_plane(v), last_plane(v)
        lower = last_plane([wx[t, c, here] for c in range(3)])
        total = []
        for c in range(3):
            fx = wx[t, c, here] * (v[c] - ahead[c])
            gx = lower[c] * (behind[c] - v[c])
            fy = wy[t, c, here] * (v[c] - v_ref[t, c, above])
            gy = wy[t, c, below] * (v_ref[t, c, below] - v[c])
            fz = wz[t, c, here] * (v[c] - pltpu.roll(v[c], 127, 1))
            gz = pltpu.roll(wz[t, c, here], 1, 1) * (pltpu.roll(v[c], 1, 1) - v[c])
            through.append(fz)
            total.append((fx - gx) + (fy - gy) + (fz - gz))
        result.append(total)
    for c in range(3):
        faces[c, here] = merge_faces(through[c], through[3 + c])
    return result


def face_lanes(faces, p, here):
    return pltpu.roll(faces[p // 16, here], 124 - 8 * (p % 16), 1)


def flux_two(v_ref, wx, wy, wz, wm, faces, p, start, rows):
    here = slice(start, start + rows)
    above = slice(start + 1, start + rows + 1)
    below = slice(start - 1, start + rows - 1)
    lane = lanes_of(rows)
    v = v_ref[p, here]
    through = face_lanes(faces, p, here)
    fx = wx[p, here] * (v - v_ref[p + 1, here])
    gx = wx[p - 1, here] * (v_ref[p - 1, here] - v)
    fy = wy[p, here] * (v - v_ref[p, above])
    gy = wy[p, below] * (v_ref[p, below] - v)
    fz = jnp.where(lane == 127, through, wz[p, here] * (v - pltpu.roll(v, 127, 1)))
    gz = jnp.where(lane == 0, through, wm[p, here] * (pltpu.roll(v, 1, 1) - v))
    return (fx - gx) + (fy - gy) + (fz - gz)


def weights_kernel(pos, ek, wx, wy, wz, wm, sums, q):
    here = slice(8, 48)

    def invert(p):
        q[p, here] = 0.5 * rcp(ek[p, here])

    loop(0, N2, invert, 8)
    wx[0, here] = rcp(q[0, here] + q[1, here])

    def body(p):
        v = q[p, here]
        face_x = rcp(v + q[p + 1, here])
        face_y = rcp(v + q[p, 9:49])
        wx[p, here] = face_x
        wy[p, here] = face_y
        face_z = rcp(v + pltpu.roll(v, 127, 1))
        wz[p, here] = face_z
        wm[p, here] = pltpu.roll(face_z, 1, 1)
        sums[p, here] = rcp(v + q[p - 1, here]) + face_x + face_y + rcp(v + q[p, 7:47])

    loop(1, N2 - 1, body, 8)


def add_kernel(pos, first, second, out):
    planes, rows = out.shape[0], out.shape[1] - 16
    here = slice(8, 8 + rows)

    def add(p):
        out[p, here] = first[p, here] + second[p, here]

    loop(0, planes, add, 8)


def down_kernel(
    pos, eb, ek, wx, wy, wz, wm, sums, low, high, zlo, zhi,
    bk3, low3, high3, inv, f, s, tb, twx, twy, twz, tinv, tx,
    r1, tq, tf, ts, face_w, face_f, face_s, tmp,
):
    gx, gy, gz = pos[0], pos[1], pos[2]
    lane = lanes_of(R2)
    row = rows_of(R2) - 4
    here, above, below = slice(8, 48), slice(9, 49), slice(7, 47)
    inside_y = ((row >= 0) | (gy > 0)) & ((row < 32) | (gy < DEV[1] - 1))
    cell = lane & 7

    def inside_x(p):
        return ((p >= 4) | (gx > 0)) & ((p < 36) | (gx < DEV[0] - 1))

    for t, (first, second) in enumerate(((zlo, low), (high, zhi))):
        for c in range(3):
            one, two = first[c], second[c]
            tb[t, c, here] = jnp.where(cell < 4, one, pltpu.roll(two, 4, 1))
            k = jnp.where(cell < 4, pltpu.roll(one, 124, 1), two)
            if c == 2:
                k = jnp.where(lane < 64, k, 1.0)
            tq[t, c, here] = 0.5 * rcp(k)
    through = []
    for t in range(2):
        v = [tq[t, c, here] for c in range(3)]
        face_x = [rcp(a + b) for a, b in zip(v, next_plane(v))]
        below_x = last_plane(face_x)
        inside_z = ((cell >= 4) | (gz > 0)) if t == 0 else ((cell < 4) | (gz < DEV[2] - 1))
        for c in range(3):
            face_y = rcp(v[c] + tq[t, c, above])
            below_y = rcp(v[c] + tq[t, c, below])
            ahead = pltpu.roll(v[c], 127, 1)
            if t == 0:
                face_z = rcp(jnp.where((cell == 3) & (gz == 0), ahead, v[c]) + ahead)
            else:
                face_z = rcp(v[c] + jnp.where((cell == 3) & (gz == DEV[2] - 1), v[c], ahead))
            through.append(face_z)
            twx[t, c, here] = face_x[c]
            twy[t, c, here] = face_y
            twz[t, c, here] = face_z
            total = below_x[c] + face_x[c] + face_y + below_y + face_z + pltpu.roll(face_z, 1, 1)
            inside = inside_y & inside_z & inside_x(16 * c + (lane >> 3))
            value = jnp.where(inside, rcp(total), 0.0)
            tinv[t, c, here] = value
            tf[t, c, here] = value * tb[t, c, here] * inv_center
    for c in range(3):
        face_w[c, here] = merge_faces(through[c], through[3 + c])
    flux = flux_strips(tf, twx, twy, twz, face_f)
    for t in range(2):
        for c in range(3):
            rest = tb[t, c, here] - flux[t][c]
            step = keep_coef * tf[t, c, here] + push_coef * tinv[t, c, here] * rest
            ts[t, c, here] = step
            tx[t, c, here] = tf[t, c, here] + step
    through = [
        twz[t, c, here] * (ts[t, c, here] - pltpu.roll(ts[t, c, here], 127, 1))
        for t in range(2)
        for c in range(3)
    ]
    for c in range(3):
        face_s[c, here] = merge_faces(through[c], through[3 + c])

    mask = jnp.where(inside_y, 1.0, 0.0)

    def weigh(p):
        through = face_lanes(face_w, p, here)
        face_z = jnp.where(lane == 127, through, wz[p, here])
        below_z = jnp.where(lane == 0, through, wm[p, here])
        scale = jnp.where(inside_x(p), 1.0, 0.0)
        value = jnp.where(mask * scale > 0.5, rcp(sums[p, here] + face_z + below_z), 0.0)
        inv[p, here] = value
        f[p, here] = value * eb[p, here] * inv_center

    loop(1, N2 - 1, weigh, 13)

    def smooth(p):
        rest = eb[p, here] - flux_two(f, wx, wy, wz, wm, face_f, p, 8, R2)
        step = keep_coef * f[p, here] + push_coef * inv[p, here] * rest
        r1[p, here] = rest
        s[p, here] = step

    loop(2, N2 - 2, smooth, 6)

    to_b = square(lambda i, j: (i >> 1) == j, 0.125)
    to_k = square(lambda i, j: (i >> 1) + 64 == j, 0.125)

    def coarsen(i):
        p = 2 * i + 4
        total = r1[p, 12:44] + r1[p + 1, 12:44]
        total = total - flux_two(s, wx, wy, wz, wm, face_s, p, 12, 32)
        tmp[0, i, 0:32] = total - flux_two(s, wx, wy, wz, wm, face_s, p + 1, 12, 32)
        tmp[1, i, 0:32] = ek[p, 12:44] + ek[p + 1, 12:44]

    loop(0, 16, coarsen, 4)
    pairs = [row_pairs(tmp.at[j], range(16), 0, 16) for j in range(2)]
    both = select_dot(pairs[0], to_b) + select_dot(pairs[1], to_k)
    for i in range(16):
        part = both[16 * i : 16 * i + 16]
        bk3[i] = part
        if i < 13:
            low3[i] = part
        if i >= 3:
            high3[i - 3] = part


def planes_kernel(pos, bk, xlo, xhi, out, low, high):
    gx = pos[0]
    right = lanes_of(16) >= 64

    def put(p, value):
        out[p] = value
        low[p] = value[0:8]
        high[p] = value[8:16]
        if 7 <= p < 35:
            low[p + 35] = value[8:16]
            high[p + 35] = value[0:8]

    for j in range(13):
        lo, hi = xlo[j], xhi[j]
        if j == 12:
            lo = jnp.where(right & (gx == 0), bk[0], lo)
        if j == 0:
            hi = jnp.where(right & (gx == DEV[0] - 1), bk[15], hi)
        put(j, lo)
        put(29 + j, hi)
    for j in range(16):
        put(13 + j, bk[j])


def three_rows(pos, own, ylo, yhi, p):
    gy = pos[1]
    right = lanes_of(16) >= 64
    row = rows_of(16)
    far = jnp.where((p >= 7) & (p < 35), p + 35, p)
    lo = jnp.concatenate([ylo[far], ylo[p]], axis=0)
    hi = jnp.concatenate([yhi[p], yhi[far]], axis=0)
    lo = jnp.where(right & (row == 15) & (gy == 0), own[p, 0:1], lo)
    hi = jnp.where(right & (row == 0) & (gy == DEV[1] - 1), own[p, 15:16], hi)
    return lo, own[p], hi


def slots_kernel(pos, own, ylo, yhi, low, high):
    quarter = (lanes_of(16) & 63) >> 4

    def column(col):
        total_lo = [None] * 3
        total_hi = [None] * 3
        for slot in range(4):
            p = jnp.minimum(col * 4 + slot, N3 - 1)
            mine = quarter == slot
            for g, e in enumerate(three_rows(pos, own, ylo, yhi, p)):
                lo, hi = rolled(e, 16 * slot), rolled(e, 16 * slot - 48)
                total_lo[g] = lo if slot == 0 else jnp.where(mine, lo, total_lo[g])
                total_hi[g] = hi if slot == 0 else jnp.where(mine, hi, total_hi[g])
        for g in range(3):
            low[col, 16 * g : 16 * g + 16] = total_lo[g]
            high[col, 16 * g : 16 * g + 16] = total_hi[g]

    loop(0, 11, column, 4)


def flux_one(v_ref, wx, wy, wz, wm, p, rows):
    here, above, below = slice(8, 8 + rows), slice(9, 9 + rows), slice(7, 7 + rows)
    v = v_ref[p, here]
    fx = wx[p, here] * (v - v_ref[p + 1, here])
    gx = wx[p - 1, here] * (v_ref[p - 1, here] - v)
    fy = wy[p, here] * (v - v_ref[p, above])
    gy = wy[p, below] * (v_ref[p, below] - v)
    fz = wz[p, here] * (v - pltpu.roll(v, 127, 1))
    gz = wm[p, here] * (pltpu.roll(v, 1, 1) - v)
    return (fx - gx) + (fy - gy) + (fz - gz)


UNROLL = {48: 10, 24: 9, 32: 8, 16: 8, 8: 4}


def weigh_one(q, b, wx, wy, wz, wm, inv, f, rows, low, high, first, last, inside):
    here = slice(8, 8 + rows)
    wx[low - 1, here] = rcp(q[low - 1, here] + q[low, here])

    def body(p):
        v = q[p, here]
        up = pltpu.roll(v, 127, 1)
        face_x = rcp(v + q[p + 1, here])
        face_y = rcp(v + q[p, 9 : 9 + rows])
        below_x = rcp(v + q[p - 1, here])
        below_y = rcp(v + q[p, 7 : 7 + rows])
        face_z = rcp(jnp.where(first, up, v) + jnp.where(last, v, up))
        lower_z = pltpu.roll(face_z, 1, 1)
        wx[p, here] = face_x
        wy[p, here] = face_y
        wz[p, here] = face_z
        wm[p, here] = lower_z
        total = below_x + face_x + face_y + below_y + face_z + lower_z
        value = jnp.where(inside(p), rcp(total), 0.0)
        inv[p, here] = value
        f[p, here] = value * b[p, here] * inv_center

    loop(low, high, body, UNROLL[rows])


def smooth_one(b, wx, wy, wz, wm, inv, f, r1, s, xs, rows, low, high):
    here = slice(8, 8 + rows)

    def body(p):
        rest = b[p, here] - flux_one(f, wx, wy, wz, wm, p, rows)
        step = keep_coef * f[p, here] + push_coef * inv[p, here] * rest
        r1[p, here] = rest
        s[p, here] = step
        if xs is not None:
            xs[p, here] = f[p, here] + step

    loop(low, high, body, UNROLL[rows])


def finish_one(b, wx, wy, wz, wm, inv, xs, f, r0, out, shift, rows, ranges):
    here = slice(8, 8 + rows)

    def start(p):
        rest = b[p, here] - flux_one(xs, wx, wy, wz, wm, p, rows)
        r0[p, here] = rest
        f[p, here] = inv[p, here] * rest * inv_center

    loop(*ranges[0], start, UNROLL[rows])

    def end(p):
        rest = r0[p, here] - flux_one(f, wx, wy, wz, wm, p, rows)
        step = keep_coef * f[p, here] + push_coef * inv[p, here] * rest
        out[p + shift, here] = xs[p, here] + f[p, here] + step

    loop(*ranges[1], end, UNROLL[rows])


def signed(lane, limit):
    return jnp.where(lane < limit, lane, lane - 128)


def middle_kernel(
    pos, own, ylo, yhi, zlo, zhi,
    payload, b3, wx3, wy3, wz3, wm3, inv3, f3, s3, b4, wx4, wy4, wz4, wm4, inv4, f4, s4,
    k3, q3, r3, k4, q4, r4, tmp,
):
    gx, gy, gz = pos[0], pos[1], pos[2]
    lane = lanes_of(16)

    def unpack(p, lo, hi, slot):
        for g, e in enumerate(three_rows(pos, own, ylo, yhi, p)):
            rows = slice(8 + 16 * g, 24 + 16 * g)
            part = slice(16 * g, 16 * g + 16)
            up, dn = rolled(hi[part], 64 - 16 * slot), rolled(lo[part], 112 - 16 * slot)
            bv = jnp.where((lane >= 64) & (lane < 80), up, e)
            b3[p, rows] = jnp.where(lane >= 112, dn, bv)
            kv = jnp.where(lane < 16, up, jnp.where((lane >= 48) & (lane < 64), dn, e))
            kv = pltpu.roll(kv, 64, 1)
            kv = jnp.where((lane >= 80) & (lane < 112), 1.0, kv)
            k3[p, rows] = kv
            q3[p, rows] = 2.0 * rcp(kv)

    def column(col, slots):
        lo, hi = zlo[col], zhi[col]
        for slot in range(slots):
            unpack(col * 4 + slot, lo, hi, slot)

    loop(0, 10, lambda col: column(col, 4), 2)
    column(10, 2)

    def region(rows, y_first, x_first, nx, ny, nz):
        y = rows_of(rows) + y_first
        z = signed(lanes_of(rows), 96)
        inside_y = ((y >= 0) | (gy > 0)) & ((y < ny) | (gy < DEV[1] - 1))
        inside_z = ((z >= 0) | (gz > 0)) & ((z < nz) | (gz < DEV[2] - 1))
        inside_yz = jnp.where(inside_y & inside_z, 1.0, 0.0)

        def inside(p):
            x = p + x_first
            inside_x = ((x >= 0) | (gx > 0)) & ((x < nx) | (gx < DEV[0] - 1))
            return inside_yz * jnp.where(inside_x, 1.0, 0.0) > 0.5

        return inside

    def edges(rows, cells):
        lane = lanes_of(rows)
        return (lane == 127) & (gz == 0), (lane == cells - 1) & (gz == DEV[2] - 1)

    inside = region(R3, -16, -13, 16, 16, 64)
    weigh_one(q3, b3, wx3, wy3, wz3, wm3, inv3, f3, R3, 1, N3 - 1, *edges(R3, 64), inside)
    smooth_one(b3, wx3, wy3, wz3, wm3, inv3, f3, r3, s3, None, R3, 2, N3 - 2)

    def pick(i, j):
        target = signed(j, 64)
        return ((signed(i, 96) >> 1) == target) & (target >= -7) & (target < 39)

    narrow = square(pick, 0.125)
    valid = (lanes_of(R4) < 39) | (lanes_of(R4) >= 121)
    row = rows_of(R4)

    def coarse_k(i):
        p = 2 * i + 1
        tmp[0, i, 8:56] = k3[p, 8:56] + k3[p + 1, 8:56]

    def coarse_b(i):
        p = 2 * i + 1
        total = r3[p, 8:56] + r3[p + 1, 8:56] - flux_one(s3, wx3, wy3, wz3, wm3, p, R3)
        tmp[1, i, 8:56] = total - flux_one(s3, wx3, wy3, wz3, wm3, p + 1, R3)

    loop(0, N4, coarse_k, 5)
    loop(1, N4 - 1, coarse_b, 3)
    value = select_dot(row_pairs(tmp.at[0], range(N4), 12, R4), narrow)
    for i in range(N4):
        part = jnp.where(valid, value[R4 * i : R4 * i + R4], 1.0)
        part = jnp.where((row == 5) & (gy == 0), pltpu.roll(part, R4 - 1, 0), part)
        part = jnp.where((row == 14) & (gy == DEV[1] - 1), pltpu.roll(part, 1, 0), part)
        k4[i, 8:32] = part
    value = select_dot(row_pairs(tmp.at[1], range(1, N4 - 1), 12, R4), narrow)
    for i in range(1, N4 - 1):
        b4[i, 8:32] = value[R4 * (i - 1) : R4 * i]
    k4[5, 8:32] = jnp.where(gx == 0, k4[6, 8:32], k4[5, 8:32])
    k4[14, 8:32] = jnp.where(gx == DEV[0] - 1, k4[13, 8:32], k4[14, 8:32])

    def invert(i):
        q4[i, 8:32] = 8.0 * rcp(k4[i, 8:32])

    loop(0, N4, invert, 5)
    inside = region(R4, -6, -6, 8, 8, 32)
    weigh_one(q4, b4, wx4, wy4, wz4, wm4, inv4, f4, R4, 1, N4 - 1, *edges(R4, 32), inside)
    smooth_one(b4, wx4, wy4, wz4, wm4, inv4, f4, r4, s4, None, R4, 2, N4 - 2)

    cell = lanes_of(4) & 15
    spread = square(lambda i, j: (signed(i, 64) >> 1) == (j & 15), 0.125)
    spread_halo = square(
        lambda i, j: ((signed(i, 64) >> 1) == ((j & 15) ^ 16) - ((j & 8) << 2))
        & (((j & 15) < 4) | ((j & 15) >= 12)),
        0.125,
    )
    between = (cell >= 4) & (cell < 12)
    slot = lanes_of(4) >> 4
    quad = rows_of(4)
    parts = [[[None, None], [None, None]] for _ in range(2)]
    for i in range(4):
        p = 2 * i + 6
        total = r4[p, 8:32] + r4[p + 1, 8:32] - flux_one(s4, wx4, wy4, wz4, wm4, p, R4)
        tmp[0, i, 8:32] = total - flux_one(s4, wx4, wy4, wz4, wm4, p + 1, R4)
        tmp[1, i, 8:32] = k4[p, 8:32] + k4[p + 1, 8:32]
    for i in range(4):
        mine = slot == (i % 2) * 4 + quad
        for a in range(2):
            pair = row_pairs(tmp.at[a], [i], 14, 4)
            for h, matrix in enumerate((spread, spread_halo)):
                value = select_dot(pair, matrix)
                if h == 1:
                    value = jnp.where(between, 1.0, value)
                value = jnp.sum(jnp.where(mine, value, 0.0), axis=0, keepdims=True)
                old = parts[h][a][i // 2]
                parts[h][a][i // 2] = value if old is None else old + value
    value = jnp.concatenate([row for h in parts for a in h for row in a], axis=0)
    for d in range(32):
        payload[d] = value


def exchange_blocks(value):
    row = rows_of(8)
    group = lanes_of(8) >> 4
    for bit in (1, 2):
        upper = pltpu.roll(pltpu.roll(value, 8 - bit, 0), 16 * bit, 1)
        lower = pltpu.roll(pltpu.roll(value, bit, 0), 128 - 16 * bit, 1)
        moved = jnp.where((row & bit) == 0, upper, lower)
        value = jnp.where((row & bit) == (group & bit), value, moved)
    moved = pltpu.roll(pltpu.roll(value, 4, 0), 64, 1)
    return jnp.where((row & 4) == (group & 4), value, moved)


WHOLE = ((16, 32, 128), (8, 16, 64), (4, 8, 32))


def up_kernel(
    pos, own, up, down, b3, wx3, wy3, wz3, wm3, inv3, x3, b4, wx4, wy4, wz4, wm4, inv4, x4,
    eb, wx, wy, wz, wm, inv, xs, tb, twx, twy, twz, tinv, tx,
    out, *scratch,
):
    gx, gy, gz = pos[0], pos[1], pos[2]
    levels = [scratch[13 * i : 13 * i + 13] for i in range(3)]
    e5, e6, raw, f4, r4, e4, y4, f3, r3, e3, y3, f2, r2, y2, tf, ty, face_x, face_f, ob, tmp, sems = scratch[39:]

    for level, (nx, ny, nz) in enumerate(WHOLE):
        b, k, q, wx_, wy_, wz_, wm_, inv_, f, r, s, x, r0 = levels[level]
        for ref in (f, s, x):
            ref[0] = jnp.zeros(ref.shape[1:], F32)
            ref[nx + 1] = jnp.zeros(ref.shape[1:], F32)

            def clear(p, ref=ref, ny=ny):
                ref[p, 0:8] = jnp.zeros((8, 128), F32)
                ref[p, 8 + ny : 16 + ny] = jnp.zeros((8, 128), F32)

            loop(1, nx + 1, clear)
    for p in (0, 1, 2, 19, 20, 21):
        e5[p] = jnp.zeros(e5.shape[1:], F32)

    def clear(p):
        e5[p, 0:8] = jnp.zeros((8, 128), F32)
        e5[p, 40:48] = jnp.zeros((8, 128), F32)

    loop(3, 19, clear)

    b5, k5 = levels[0][0], levels[0][1]

    for n in (3, 4, 5):
        raw[pl.ds(n, 128, stride=8)] = jnp.ones((128, 128), F32)
    for n, part, first in ((0, own, 0), (1, up, 0), (2, up, 4), (6, down, 4), (7, down, 0)):
        for kind in range(4):
            raw[pl.ds(8 * kind + n, 32, stride=32)] = part[pl.ds(first + kind, 32, stride=8)]

    def unpack(d):
        dx, dy = d // 8, d % 8
        rows = pl.ds(8 + 4 * dy, 4)
        for kind in range(4):
            value = exchange_blocks(raw[pl.ds(pl.multiple_of(d * 32 + kind * 8, 8), 8)])
            target = (b5, k5)[kind // 2]
            p = 1 + 4 * dx + 2 * (kind % 2)
            target[p, rows] = value[0:4]
            target[p + 1, rows] = value[4:8]

    loop(0, 32, unpack, 8)

    def ends(level):
        nx, ny, nz = WHOLE[level]
        k, q = levels[level][1], levels[level][2]
        factor = 0.5 * 4.0 ** (level + 3)

        def invert(p):
            value = factor * rcp(k[p, 8 : 8 + ny])
            q[p, 8 : 8 + ny] = value
            q[p, 7:8] = value[0:1]
            q[p, 8 + ny : 9 + ny] = value[ny - 1 : ny]

        loop(1, nx + 1, invert, 4)
        q[0] = q[1]
        q[nx + 1] = q[nx]

    def down(level):
        nx, ny, nz = WHOLE[level]
        b, k, q, wx_, wy_, wz_, wm_, inv_, f, r, s, x, r0 = levels[level]
        ends(level)

        def below(p):
            wy_[p, 7:8] = rcp(q[p, 7:8] + q[p, 8:9])

        loop(1, nx + 1, below, 4)
        z = signed(lanes_of(ny), 72) + gz * (nz // DEV[2])
        weigh_one(
            q, b, wx_, wy_, wz_, wm_, inv_, f, ny, 1, nx + 1, z == -1, z == nz - 1,
            lambda p: (z >= 0) & (z < nz),
        )
        smooth_one(b, wx_, wy_, wz_, wm_, inv_, f, r, s, x, ny, 1, nx + 1)
        if level == 2:
            return
        nb, nk = levels[level + 1][0], levels[level + 1][1]
        low, high = ((-9, 17), (-4, 8))[level]

        def kept(lane):
            return (signed(lane, 64) >= low) & (signed(lane, 64) < high)

        narrow = square(lambda i, j: ((signed(i, 72) >> 1) == signed(j, 64)) & kept(j), 0.125)
        valid = kept(lanes_of(ny // 2))

        def coarsen(i):
            p = 2 * i - 1
            here = slice(8, 8 + ny)
            total = r[p, here] + r[p + 1, here] - flux_one(s, wx_, wy_, wz_, wm_, p, ny)
            tmp[0, i, here] = total - flux_one(s, wx_, wy_, wz_, wm_, p + 1, ny)
            tmp[1, i, here] = k[p, here] + k[p + 1, here]

        count = ny // 2
        planes = range(1, nx // 2 + 1)
        loop(1, nx // 2 + 1, coarsen, 64 // ny)
        for a, target in enumerate((nb, nk)):
            value = select_dot(row_pairs(tmp.at[a], planes, 8, count), narrow)
            for n, i in enumerate(planes):
                part = value[count * n : count * n + count]
                target[i, 8 : 8 + count] = jnp.where(valid, part, 1.0) if a == 1 else part

    for level in range(3):
        down(level)

    def rise(level, coarse, target, shift):
        nx, ny, nz = WHOLE[level]
        b, k, q, wx_, wy_, wz_, wm_, inv_, f, r, s, x, r0 = levels[level]
        widen = square(lambda i, j: signed(i, 64) == (signed(j, 64) >> 1), 1.0)
        count = ny // 2

        planes = range(1, nx // 2 + 1)
        value = jnp.concatenate([coarse[i, 8 : 8 + count] for i in planes], axis=0)
        spread_rows(tmp.at[0], planes, 8, count, select_dot(value, widen))

        def add(i):
            wide = tmp[0, i, 8 : 8 + ny]
            x[2 * i - 1, 8 : 8 + ny] += wide
            x[2 * i, 8 : 8 + ny] += wide

        loop(1, nx // 2 + 1, add, 64 // ny)
        span = (1, nx + 1)
        finish_one(b, wx_, wy_, wz_, wm_, inv_, x, f, r0, target, shift, ny, (span, span))

    rise(1, levels[2][11], e6, 0)
    rise(0, e6, e5, 2)

    widen = square(lambda i, j: signed(i, 64) == (signed(j, 64) >> 1), 1.0)

    planes = range(1, 9)
    value = [e5[gx * 4 + i, pl.ds(pl.multiple_of(4 * gy, 4), 24)] for i in planes]
    value = select_dot(jnp.concatenate(value, axis=0), widen)
    for n, i in enumerate(planes):
        spread_rows(tmp.at[0], [i], 8, 12, value[24 * n + 5 : 24 * n + 17])

    def add_four(i):
        wide = tmp[0, i, 8:32]
        y4[2 * i, 8:32] = x4[2 * i, 8:32] + wide
        y4[2 * i + 1, 8:32] = x4[2 * i + 1, 8:32] + wide

    loop(1, 9, add_four, 4)
    finish_one(b4, wx4, wy4, wz4, wm4, inv4, y4, f4, r4, e4, 0, R4, ((3, 17), (4, 16)))

    widen3 = square(lambda i, j: signed(i, 64) == (signed(j, 96) >> 1), 1.0)

    planes = range(4, 16)
    value = jnp.concatenate([e4[i, 8:32] for i in planes], axis=0)
    spread_rows(tmp.at[0], planes, 12, 24, select_dot(value, widen3))

    def add_three(i):
        wide = tmp[0, i, 8:56]
        y3[2 * i + 1, 8:56] = x3[2 * i + 1, 8:56] + wide
        y3[2 * i + 2, 8:56] = x3[2 * i + 2, 8:56] + wide

    loop(4, 16, add_three, 3)
    finish_one(b3, wx3, wy3, wz3, wm3, inv3, y3, f3, r3, e3, 0, R3, ((11, 31), (12, 30)))

    wide = square(lambda i, j: i == (j >> 1), 1.0)
    planes = range(1, 19)
    value = jnp.concatenate([e3[i + 11, 22:46] for i in planes], axis=0)
    spread_rows(tmp.at[0], planes, 8, 24, select_dot(value, wide))
    here = slice(8, 48)
    group = lanes_of(24) >> 4
    for t in range(2):
        wide = square(lambda i, j: signed(i, 96) == ((j & 7) + 128 * t - 4) >> 1, 1.0)
        parts = select_dot(value, wide)
        for c in range(3):
            total = jnp.zeros((24, 128), F32)
            for n, i in enumerate(planes):
                if i // 8 == c:
                    total = jnp.where(group == i % 8, parts[24 * n : 24 * n + 24], total)
            spread_rows(tmp.at[1], [3 * t + c], 8, 24, total)
            ty[t, c, here] = tx[t, c, here] + tmp[1, 3 * t + c, here]
    flux = flux_strips(ty, twx, twy, twz, face_x)
    for t in range(2):
        for c in range(3):
            tf[t, c, here] = tinv[t, c, here] * (tb[t, c, here] - flux[t][c]) * inv_center
    through = [
        twz[t, c, here] * (tf[t, c, here] - pltpu.roll(tf[t, c, here], 127, 1))
        for t in range(2)
        for c in range(3)
    ]
    for c in range(3):
        face_f[c, here] = merge_faces(through[c], through[3 + c])

    def add_two(i):
        part = tmp[0, i, here]
        y2[2 * i, here] = xs[2 * i, here] + part
        y2[2 * i + 1, here] = xs[2 * i + 1, here] + part

    loop(1, 19, add_two, 3)

    def start(p):
        rest = eb[p, here] - flux_two(y2, wx, wy, wz, wm, face_x, p, 8, R2)
        r2[p, here] = rest
        f2[p, here] = inv[p, here] * rest * inv_center

    loop(3, 37, start, 7)
    core = slice(12, 44)

    def end(i):
        p = i + 4
        rest = r2[p, core] - flux_two(f2, wx, wy, wz, wm, face_f, p, 12, 32)
        first = f2[p, core]
        step = keep_coef * first + push_coef * inv[p, core] * rest
        ob[i] = y2[p, core] + first + step

    def leave(n):
        part = pl.ds(pl.multiple_of(8 * n, 8), 8)
        return pltpu.make_async_copy(ob.at[part], out.at[part], sems.at[n])

    @pl.loop(0, 4)
    def _(n):
        for j in range(8):
            end(8 * n + j)
        leave(n).start()

    for n in range(4):
        leave(n).wait()


def vmem(array):
    return pltpu.with_memory_space_constraint(array, pltpu.VMEM)


def call(kernel, args, outs, scratch=(), final=False):
    size = sum(4 * math.prod(shape) for shape in scratch) + sum(4 * math.prod(shape) for shape in outs)
    out_type = jax.ShapeDtypeStruct if final else pltpu.VMEM
    held = args[1:]
    return pl.pallas_call(
        kernel,
        out_shape=[out_type(shape, F32) for shape in outs],
        in_specs=[pl.BlockSpec(memory_space=pltpu.SMEM)]
        + [pl.BlockSpec(memory_space=pltpu.VMEM)] * len(held),
        out_specs=[pl.BlockSpec(memory_space=pl.ANY if final else pltpu.VMEM)] * len(outs),
        scratch_shapes=[pltpu.VMEM(shape, F32) for shape in scratch]
        + [pltpu.SemaphoreType.DMA((4,))] * final,
        compiler_params=pltpu.CompilerParams(vmem_limit_bytes=size + (4 << 20)),
    )(args[0], *held)


def load(kernel, b, k, shape, count):
    return pl.pallas_call(
        kernel,
        out_shape=[pltpu.VMEM(shape, F32)] * 2,
        in_specs=[pl.BlockSpec(memory_space=pl.ANY)] * 2,
        out_specs=[pl.BlockSpec(memory_space=pltpu.VMEM)] * 2,
        scratch_shapes=[pltpu.SemaphoreType.DMA((count,))],
    )(b, k)


def swap(low, high, axis):
    count = lax.axis_size(axis)
    ring = range(count)
    before = lax.ppermute(high, axis, [(i, (i + 1) % count) for i in ring])
    after = lax.ppermute(low, axis, [(i, (i - 1) % count) for i in ring])
    return vmem(before), vmem(after)


def shards(b, k):
    pos = jnp.stack([lax.axis_index(axis) for axis in AXES]).astype(jnp.int32)
    low, high = load(edge_kernel, b, k, (7, 32, 128), 4)
    xlo, xhi = swap(low, high, "gx")
    b, k = load(load_kernel, b, k, (32, 32, 128), 8)
    low, high = call(rows_kernel, (pos, b, k, xlo, xhi), [(N2, 8, 128)] * 2)
    ylo, yhi = swap(low, high, "gy")
    ext2, strip, face = (N2, T2, 128), (2, 3, T2, 128), (3, T2, 128)
    low, high, eb, ek = call(
        lanes_kernel, (pos, b, k, xlo, xhi, ylo, yhi), [(3, R2, 128)] * 2 + [ext2] * 2
    )
    zlo, zhi = swap(low, high, "gz")
    wx, wy, wz, wm, sums = call(weights_kernel, (pos, ek), [ext2] * 5, [ext2])
    bk3, low, high, inv, first, second, *rest = call(
        down_kernel,
        (pos, eb, ek, wx, wy, wz, wm, sums, low, high, zlo, zhi),
        [(16, 16, 128)] + [(13, 16, 128)] * 2 + [ext2] * 3 + [strip] * 6,
        [ext2] + [strip] * 3 + [face] * 3 + [(2, 16, 32, 128)],
    )
    (xs,) = call(add_kernel, (pos, first, second), [ext2])
    state2 = [eb, wx, wy, wz, wm, inv, xs, *rest]
    xlo, xhi = swap(low, high, "gx")
    own, low, high = call(
        planes_kernel, (pos, bk3, xlo, xhi), [(N3, 16, 128)] + [(N3 + 28, 8, 128)] * 2
    )
    ylo, yhi = swap(low, high, "gy")
    low, high = call(slots_kernel, (pos, own, ylo, yhi), [(11, 48, 128)] * 2)
    zlo, zhi = swap(low, high, "gz")
    three, four = (N3, T3, 128), (N4, T4, 128)
    payload, *state = call(
        middle_kernel,
        (pos, own, ylo, yhi, zlo, zhi),
        [(32, 8, 128)] + [three] * 8 + [four] * 8,
        [three] * 3 + [four] * 3 + [(2, N4, T3, 128)],
    )
    (x3,) = call(add_kernel, (pos, *state[6:8]), [three])
    (x4,) = call(add_kernel, (pos, *state[14:16]), [four])
    state = [*state[:6], x3, *state[8:14], x4]
    recv = lax.all_to_all(payload, AXES[:2], 0, 0, tiled=True).reshape(256, 128)
    ring = range(DEV[2])
    recv = [recv] + [
        lax.ppermute(recv, "gz", [(i, (i - d) % DEV[2]) for i in ring]) for d in (1, -1)
    ]
    recv = [vmem(part) for part in recv]
    scratch = []
    for nx, ny, _ in WHOLE:
        scratch += [(nx + 2, ny + 16, 128)] * 13
    scratch += [(22, 56, 128), (10, 32, 128), (1024, 128)]
    scratch += [four] * 4 + [three] * 4 + [ext2] * 3 + [strip] * 2 + [face] * 2 + [(32, 32, 128)]
    scratch += [(2, 20, T3, 128)]
    (out,) = call(up_kernel, (pos, *recv, *state, *state2), [(32, 32, 128)], scratch, True)
    return out


def solution(mesh):
    spec = P(*AXES)
    return jax.shard_map(shards, mesh=mesh, in_specs=(spec, spec), out_specs=spec, check_vma=False)
```
